32 devices in a mesh: band: 4 (over y, x), slab: 8 (over z, core).
Axes of the slice: x: 2, y: 2, z: 4, core: 2. Of those that a mesh axis runs over, the one named last changes fastest.
Arguments:
- band_fields: float32 [16, 6, 6, 128, 1024], P(None, None, None, ('band', 'slab')), may hold values from -12 to 12
Outputs:
- pair_transfer: float32 [16, 16, 1024], P('band', None, 'slab')
The draws below stay inside these ranges and needn't reach their ends.
All inputs are finite; a program needn't handle non-finite values.
Results may differ from the reference program's by a relative error of at most 0.0042.
Values may be sent and summed in bfloat16 or wider, within the bound.
No kernel may reach another device: no remote copies, remote signals or barrier semaphores. Data moves between devices by JAX's collectives and lax.ppermute only.
A program may use at most 256 MiB of HBM per device.

```python
import jax
import jax.numpy as jnp
from jax import lax

NBANDS = 16
XW = 4
NY = 128
XIN = 6
NZ = 1024


def block_scale(key, dims, cuts, least, largest):
    gain, own = 1.0, jax.random.fold_in(key, 6)
    for position, blocks in cuts:
        draws = jnp.exp(jax.random.uniform(jax.random.fold_in(own, position), (blocks,), jnp.float32, least / len(cuts), largest / len(cuts)))
        gain = gain * jnp.repeat(draws, dims[position] // blocks).reshape([-1 if axis == position else 1 for axis in range(len(dims))])
    return gain


def gaussian(own_key, shape, width, most, pieces=(), held_as=jnp.bfloat16):
    array = width * jax.random.normal(own_key, shape, jnp.float32)
    if pieces:
        array = array * block_scale(own_key, shape, pieces, -0.22, 0.18)
    return jnp.clip(array, -most, most).astype(held_as)


def setup_inputs(seed: int = 0) -> dict:
    key_list = jax.random.split(jax.random.key(seed), 2)
    return {
        "band_fields": gaussian(key_list[0], (NBANDS, 6, XIN, NY, NZ), 2.0, 12.0, ((3, 32),), jnp.float32),
    }


hall_length = 0.5


def derivs(field):
    inner = field[:, 1:-1]
    ddx = (field[:, 2:] - field[:, :-2]) * 0.5
    ddy = (jnp.roll(inner, -1, 2) - jnp.roll(inner, 1, 2)) * 0.5
    ddz = (jnp.roll(inner, -1, 3) - jnp.roll(inner, 1, 3)) * 0.5
    return inner, ddx, ddy, ddz


def curl_of(ddx, ddy, ddz):
    return jnp.stack([ddy[5] - ddz[4], ddz[3] - ddx[5], ddx[4] - ddy[3]])


def advect(vector, ddx, ddy, ddz, first):
    return vector[0] * ddx[first:first + 3] + vector[1] * ddy[first:first + 3] + vector[2] * ddz[first:first + 3]


def drive_of(inner, ddx, ddy, ddz, velocity, magnetic, current):
    part_a = -advect(velocity, ddx, ddy, ddz, 0) + advect(magnetic, ddx, ddy, ddz, 3)
    part_c = -advect(velocity, ddx, ddy, ddz, 3) + advect(magnetic, ddx, ddy, ddz, 0)
    bfield = inner[3:6]
    cross = jnp.stack([current[1] * bfield[2] - current[2] * bfield[1], current[2] * bfield[0] - current[0] * bfield[2], current[0] * bfield[1] - current[1] * bfield[0]])
    return jnp.concatenate([part_a, part_c, -hall_length * cross], 0)


def reference(band_fields):
    def sums_of(field):
        inner, ddx, ddy, ddz = derivs(field)
        return jnp.concatenate([inner, curl_of(ddx, ddy, ddz)], 0)

    responses = lax.map(sums_of, band_fields)
    full = jnp.sum(responses, 0)
    velocity, magnetic, current = full[0:3], full[3:6], full[6:9]

    def drives_of(field):
        inner, ddx, ddy, ddz = derivs(field)
        return drive_of(inner, ddx, ddy, ddz, velocity, magnetic, current).astype(jnp.bfloat16)

    drives = lax.map(drives_of, band_fields)
    resp = responses.astype(jnp.bfloat16).astype(jnp.float32)
    total = jnp.einsum("qcxyz,kcxyz->qkz", resp, drives.astype(jnp.float32))
    return total * (1.0 / (XW * NY))
```

```python
import jax
import jax.numpy as jnp
from jax import lax
from jax.experimental import pallas as pl
from jax.experimental.pallas import tpu as pltpu
from jax.sharding import PartitionSpec as P

AXES = ("band", "slab")
LANES = 128
GROUP = 16
F32 = jnp.float32
BF16 = jnp.bfloat16
VMEM = pl.BlockSpec(memory_space=pltpu.VMEM)
SMEM = pl.BlockSpec(memory_space=pltpu.SMEM)
ANY = pl.BlockSpec(memory_space=pl.ANY)
PARAMS = pltpu.CompilerParams(vmem_limit_bytes=56 * 2**20)


class Sizes:
    def __init__(self, shape):
        self.bands, self.comps, self.planes, self.rows, cells = shape
        self.inner = self.planes - 2
        self.tiles = cells // LANES
        self.chunks = 4 if self.bands % 4 == 0 else 1
        self.per_chunk = self.bands // self.chunks


def row(ref, s, q, c, x, y):
    if s.rows == 1:
        return ref[q, c, x]
    return ref[q, c, x, pl.ds(y, s.tiles, stride=s.rows), :]


def z_difference(value):
    tiles = value.shape[0]
    lane = lax.broadcasted_iota(jnp.int32, value.shape, 1)
    left = pltpu.roll(value, LANES - 1, 1)
    right = pltpu.roll(value, 1, 1)
    after = jnp.where(lane == LANES - 1, pltpu.roll(left, tiles - 1, 0), left)
    before = jnp.where(lane == 0, pltpu.roll(right, 1, 0), right)
    return after - before


def start_copies(s, x_hbm, buf, sems):
    copies = []
    for i in range(s.chunks):
        part = pl.ds(i * s.per_chunk, s.per_chunk)
        copy = pltpu.make_async_copy(x_hbm.at[part], buf.at[part], sems.at[i])
        copy.start()
        copies.append(copy)
    return copies


def edge_kernel(s, x_hbm, up_ref, down_ref, buf, sems):
    copies = start_copies(s, x_hbm, buf, sems)
    last = s.rows - 1
    n = s.inner
    zero = jnp.zeros((s.tiles, LANES), F32)

    def band(q, sums):
        at_last, below, first = sums
        for c in range(s.comps):
            for p in range(n // 2):
                pair = [row(buf, s, q, c, 1 + 2 * p + k, last) for k in range(2)]
                up_ref[(q * s.comps + c) * (n // 2) + p] = jnp.concatenate(pair, 0).astype(BF16)
        at_last = [a + row(buf, s, q, 3 + i // s.planes, i % s.planes, last) for i, a in enumerate(at_last)]
        first = [a + row(buf, s, q, 3 + 2 * (i // n), 1 + i % n, 0) for i, a in enumerate(first)]
        if s.rows > 1:
            below = [a + row(buf, s, q, 3 + 2 * (i // n), 1 + i % n, last - 1) for i, a in enumerate(below)]
        return at_last, below, first

    sums = ([zero] * (3 * s.planes), [zero] * (2 * n), [zero] * (2 * n))
    for i, copy in enumerate(copies):
        copy.wait()
        sums = lax.fori_loop(i * s.per_chunk, (i + 1) * s.per_chunk, band, sums)
    at_last, below, first = sums
    for i, value in enumerate(first):
        down_ref[i] = value
    current = [[], [], []]
    for x in range(n):
        bx, by, bz = ([at_last[c * s.planes + x + k] for k in range(3)] for c in range(3))
        current[0].append((-below[n + x] - z_difference(by[1])) * 0.5)
        current[1].append((z_difference(bx[1]) - (bz[2] - bz[0])) * 0.5)
        current[2].append(((by[2] - by[0]) + below[x]) * 0.5)
    base = s.bands * s.comps * (n // 2)
    for c in range(3):
        for p in range(n // 2):
            up_ref[base + c * (n // 2) + p] = jnp.concatenate(current[c][2 * p : 2 * p + 2], 0).astype(BF16)


def transposed_store(s, source, target, slot, zt):
    depth = source.shape[0] // s.tiles
    block = source[pl.ds(zt, depth, stride=s.tiles), :].astype(BF16).T
    target[zt, :, slot] = block.reshape(LANES // GROUP, GROUP, depth)


def diagonal_products(s, rt, dt, zt, g):
    wide = s.bands * GROUP
    left = rt[zt, g].reshape(wide, rt.shape[-1])
    right = dt[zt, g].reshape(wide, dt.shape[-1])
    full = lax.dot_general(left, right, (((1,), (1,)), ((), ())), preferred_element_type=F32)
    full = full.reshape(s.bands, GROUP, wide)
    cell = lax.broadcasted_iota(jnp.int32, full.shape, 1)
    lane = lax.broadcasted_iota(jnp.int32, full.shape, 2)
    return jnp.sum(jnp.where(cell == lane % GROUP, full, 0.0), 1)


def zero_tail(s, ref, used):
    tail = ref.shape[0] - used * s.tiles
    if tail:
        ref[pl.ds(used * s.tiles, tail), :] = jnp.zeros((tail, LANES), F32)


def slot_of(s, place, q, n_band):
    share = s.bands // n_band
    return (q // share ^ place[0]) * share + q % share


def cross(a, b):
    return [a[1] * b[2] - a[2] * b[1], a[2] * b[0] - a[0] * b[2], a[0] * b[1] - a[1] * b[0]]


def local_depth(s):
    return (s.rows - 1) * s.inner * 6 + max(s.rows - 2, 0) * s.inner * 3


def local_kernel(s, n_band, place, x_hbm, g_ref, drive_ref, field_ref, last_ref, coef_ref, buf, sums, coefs, sr, sd, rt, dt, sems):
    copies = start_copies(s, x_hbm, buf, sems)
    n = s.inner
    for i, copy in enumerate(copies):
        copy.wait()

        def add(j, carry):
            c, x = (j // s.planes, j % s.planes)
            for y in range(s.rows):
                total = row(buf, s, i * s.per_chunk, c, x, y)
                for q in range(1, s.per_chunk):
                    total = total + row(buf, s, i * s.per_chunk + q, c, x, y)
                if i:
                    total = total + sums[c, x, y]
                sums[c, x, y] = total
            return carry

        lax.fori_loop(0, s.comps * s.planes, add, 0)
    for x in range(n):
        for y in range(s.rows):
            v = [sums[c, x + 1, y] for c in range(3)]
            b = [sums[c, x + 1, y] for c in range(3, 6)]

            def dy(c):
                high = sums[c, x + 1, y + 1] if y + 1 < s.rows else 0.0
                low = sums[c, x + 1, y - 1] if y else 0.0
                return high - low

            def dx(c):
                return sums[c, x + 2, y] - sums[c, x, y]

            j = [dy(5) - z_difference(b[1]), z_difference(b[0]) - dx(5), dx(4) - dy(3)]
            j = [value * 0.5 for value in j]
            for d in range(3):
                coefs[x, y, d] = (v[d] - b[d]) * -0.25
                coefs[x, y, 3 + d] = (v[d] + b[d]) * -0.25
                coefs[x, y, 6 + d] = j[d]
            if y == 0:
                coef_ref[x, 0] = coefs[x, 0, 1]
                coef_ref[x, 1] = coefs[x, 0, 4]
                for d in range(3):
                    coef_ref[x, 2 + d] = j[d]
                coef_ref[x, 5] = b[0]
                coef_ref[x, 6] = b[2]
            if y == s.rows - 1:
                for d in range(3):
                    coef_ref[x, 7 + d] = j[d]
    used = local_depth(s)
    zero_tail(s, sr, used)
    zero_tail(s, sd, used)

    def band(q, carry):
        entry = 0
        for x in range(n):
            for y in range(s.rows):
                f = [row(buf, s, q, c, x + 1, y) for c in range(6)]
                deltas = [[], [], []]
                for c in range(6):
                    deltas[0].append(row(buf, s, q, c, x + 2, y) - row(buf, s, q, c, x, y))
                    high = row(buf, s, q, c, x + 1, y + 1) if y + 1 < s.rows else None
                    low = row(buf, s, q, c, x + 1, y - 1) if y else None
                    if high is None:
                        delta = jnp.zeros_like(f[0]) if low is None else -low
                    else:
                        delta = high if low is None else high - low
                    deltas[1].append(delta)
                    deltas[2].append(z_difference(f[c]))
                da, dc = ([], [])
                for c in range(3):
                    plus = minus = None
                    for d in range(3):
                        p = coefs[x, y, d] * (deltas[d][c] + deltas[d][c + 3])
                        m = coefs[x, y, 3 + d] * (deltas[d][c] - deltas[d][c + 3])
                        plus = p if plus is None else plus + p
                        minus = m if minus is None else minus + m
                    da.append(plus + minus)
                    dc.append(plus - minus)
                dx, dy, dz = deltas
                j = [(dy[5] - dz[4]) * 0.5, (dz[3] - dx[5]) * 0.5, (dx[4] - dy[3]) * 0.5]
                drives = da + dc
                if y == 0:
                    for c in range(6):
                        drive_ref[q, x, c] = drives[c]
                        field_ref[q, x, c] = f[c]
                    for c in range(3):
                        drive_ref[q, x, 6 + c] = j[c]
                if y == s.rows - 1 and s.rows > 1:
                    for c in range(3):
                        last_ref[q, x, c] = j[c]
                        last_ref[q, x, 3 + c] = f[3 + c]
                left, right = ([], [])
                if y:
                    left, right = (list(f), list(drives))
                if 0 < y < s.rows - 1:
                    turn = cross([coefs[x, y, 6 + d] * -0.5 for d in range(3)], f[3:6])
                    left, right = (left + j, right + turn)
                for a, b in zip(left, right):
                    sr[pl.ds(entry * s.tiles, s.tiles), :] = a
                    sd[pl.ds(entry * s.tiles, s.tiles), :] = b
                    entry += 1
        if used:
            slot = slot_of(s, place, q, n_band)
            for zt in range(s.tiles):
                transposed_store(s, sr, rt, slot, zt)
                transposed_store(s, sd, dt, q, zt)
        return carry

    lax.fori_loop(0, s.bands, band, 0)

    def tile(zt, carry):
        for g in range(LANES // GROUP):
            g_ref[zt, g] = diagonal_products(s, rt, dt, zt, g)
        return carry

    if used:
        lax.fori_loop(0, s.tiles, tile, 0)
    else:
        g_ref[...] = jnp.zeros_like(g_ref)


def halo_row(s, up_ref, index, x):
    pair = up_ref[index * (s.inner // 2) + x // 2].astype(F32)
    return pair[(x % 2) * s.tiles : (x % 2 + 1) * s.tiles]


def boundary_kernel(s, n_band, scale, place, g_ref, drive_ref, field_ref, last_ref, coef_ref, up_ref, down_ref, keep_ref, send_ref, tots, consts, sr, sd, rt, dt):
    n = s.inner
    zero = jnp.zeros((s.tiles, LANES), F32)
    kinds = (1, 4, 3, 5)

    def add(q, totals):
        return [t + halo_row(s, up_ref, q * s.comps + kinds[i // n], i % n) for i, t in enumerate(totals)]

    totals = lax.fori_loop(0, s.bands, add, [zero] * (4 * n))
    for x in range(n):
        vy, my, bx, bz = (totals[k * n + x] for k in range(4))
        ahead_x, ahead_z = (down_ref[x], down_ref[n + x])
        tots[x, 0] = coef_ref[x, 0]
        tots[x, 1] = coef_ref[x, 1]
        tots[x, 2] = (vy - my) * -0.25
        tots[x, 3] = (vy + my) * -0.25
        j = [coef_ref[x, 2] - bz * 0.5, coef_ref[x, 3], coef_ref[x, 4] + bx * 0.5]
        if s.rows == 1:
            j = [j[0] + ahead_z * 0.5, j[1], j[2] - ahead_x * 0.5]
        behind = [halo_row(s, up_ref, s.bands * s.comps + c, x) for c in range(3)]
        behind = [behind[0] + coef_ref[x, 6] * 0.5, behind[1], behind[2] - coef_ref[x, 5] * 0.5]
        at_last = [coef_ref[x, 7] + ahead_z * 0.5, coef_ref[x, 8], coef_ref[x, 9] - ahead_x * 0.5]
        for c in range(3):
            tots[x, 4 + c] = j[c] * -0.5
            tots[x, 7 + c] = behind[c] * -0.5
            tots[x, 10 + c] = at_last[c] * -0.5
    used = n * (15 + (3 if s.rows > 1 else 0))
    zero_tail(s, sr, used)
    zero_tail(s, sd, used)

    def band(q, carry):
        entry = 0
        for x in range(n):
            f = [field_ref[q, x, c] for c in range(6)]
            h = [halo_row(s, up_ref, q * s.comps + c, x) for c in range(6)]
            left, right = ([], [])
            local, other = ([], [])
            for c in range(3):
                p = tots[x, 0] * (h[c] + h[c + 3])
                m = tots[x, 1] * (h[c] - h[c + 3])
                local.append((p, m))
                p = tots[x, 2] * (f[c] + f[c + 3])
                m = tots[x, 3] * (f[c] - f[c + 3])
                other.append((p, m))
            da = [drive_ref[q, x, c] - (p + m) for c, (p, m) in enumerate(local)]
            dc = [drive_ref[q, x, 3 + c] - (p - m) for c, (p, m) in enumerate(local)]
            behind = cross([tots[x, 7 + c] for c in range(3)], h[3:6])
            dc[0] = dc[0] - behind[2] * 0.5
            dc[2] = dc[2] + behind[0] * 0.5
            j = [drive_ref[q, x, 6] - h[5] * 0.5, drive_ref[q, x, 7], drive_ref[q, x, 8] + h[3] * 0.5]
            left += f + j
            right += da + dc + cross([tots[x, 4 + c] for c in range(3)], f[3:6])
            left += h
            right += [p + m for p, m in other] + [p - m for p, m in other]
            if s.rows > 1:
                left += [last_ref[q, x, c] for c in range(3)]
                right += cross([tots[x, 10 + c] for c in range(3)], [last_ref[q, x, 3 + c] for c in range(3)])
            for a, b in zip(left, right):
                sr[pl.ds(entry * s.tiles, s.tiles), :] = a
                sd[pl.ds(entry * s.tiles, s.tiles), :] = b
                entry += 1
        slot = slot_of(s, place, q, n_band)
        for zt in range(s.tiles):
            transposed_store(s, sr, rt, slot, zt)
            transposed_store(s, sd, dt, q, zt)
        return carry

    lax.fori_loop(0, s.bands, band, 0)
    share = s.bands // n_band

    def tile(r, carry):
        for core in range(2):
            zt = (r * 2 + core) ^ place[1]
            parts = [(diagonal_products(s, rt, dt, zt, g) + g_ref[zt, g]) * scale for g in range(LANES // GROUP)]
            for b in range(n_band):
                block = jnp.concatenate([p[b * share : (b + 1) * share] for p in parts], 0)
                if core == 0:
                    keep_ref[r, b] = block
                else:
                    send_ref[r, b] = block.astype(BF16)
        return carry

    lax.fori_loop(0, s.tiles // 2, tile, 0)


def exchange(value, distance, size):
    return lax.ppermute(value, AXES, [(i, i ^ distance) for i in range(size)])


def body(band_fields):
    s = Sizes(band_fields.shape)
    n_band, n_slab = (lax.axis_size("band"), lax.axis_size("slab"))
    devices = n_band * n_slab
    n, tiles, rows = (s.inner, s.tiles, s.rows)
    x = band_fields.reshape(s.bands, s.comps, s.planes, rows, tiles, LANES)
    x = x.transpose(0, 1, 2, 4, 3, 5).reshape(s.bands, s.comps, s.planes, tiles * rows, LANES)
    place = jnp.stack([lax.axis_index("band"), lax.axis_index("slab")]).astype(jnp.int32)

    def vector(*lead):
        return jax.ShapeDtypeStruct(lead + (tiles, LANES), F32)

    buffer = pltpu.VMEM(x.shape, F32)
    sems = pltpu.SemaphoreType.DMA((s.chunks,))
    depth = -(-(max(local_depth(s), 1)) // LANES) * LANES
    groups = LANES // GROUP
    wide = s.bands * GROUP
    rows_up = (s.bands * s.comps + 3) * (n // 2)

    up, down = pl.pallas_call(
        lambda *refs: edge_kernel(s, *refs),
        out_shape=(jax.ShapeDtypeStruct((rows_up, 2 * tiles, LANES), BF16), vector(2 * n)),
        in_specs=[ANY],
        out_specs=(VMEM, VMEM),
        scratch_shapes=[buffer, sems],
        compiler_params=PARAMS,
    )(x)
    step = [(i, (i + 1) % devices) for i in range(devices)]
    from_below = lax.ppermute(up, AXES, step)
    from_above = lax.ppermute(down, AXES, [(j, i) for i, j in step])

    def operands(used):
        return [
            pltpu.VMEM((used * tiles, LANES), F32),
            pltpu.VMEM((used * tiles, LANES), F32),
            pltpu.VMEM((tiles, groups, s.bands, GROUP, used), BF16),
            pltpu.VMEM((tiles, groups, s.bands, GROUP, used), BF16),
        ]

    local = pl.pallas_call(
        lambda *refs: local_kernel(s, n_band, *refs),
        out_shape=(
            jax.ShapeDtypeStruct((tiles, groups, s.bands, wide), F32),
            vector(s.bands, n, 9),
            vector(s.bands, n, 6),
            vector(s.bands, n, 6),
            vector(n, 10),
        ),
        in_specs=[SMEM, ANY],
        out_specs=(VMEM,) * 5,
        scratch_shapes=[buffer, pltpu.VMEM((s.comps, s.planes, rows, tiles, LANES), F32), pltpu.VMEM((n, rows, 9, tiles, LANES), F32)]
        + operands(depth)
        + [sems],
        compiler_params=PARAMS,
        cost_estimate=pl.CostEstimate(flops=2 * 10**9, bytes_accessed=2 * 10**7, transcendentals=0),
    )(place, x)
    if rows == 1:
        two = lax.ppermute(down, AXES, [(i, (i + 2) % devices) for i in range(devices)])
        two = two.reshape(2, n // 2, 2 * tiles, LANES) * 0.5
        base = s.bands * s.comps * (n // 2)
        behind = from_below[base:].astype(F32).reshape(3, n // 2, 2 * tiles, LANES)
        behind = jnp.stack([behind[0] - two[1], behind[1], behind[2] + two[0]])
        behind = behind.reshape(3 * (n // 2), 2 * tiles, LANES).astype(BF16)
        from_below = jnp.concatenate([from_below[:base], behind], 0)

    share = s.bands // n_band
    shape = (tiles // 2, n_band, groups * share, wide)
    scale = 1.0 / (n * rows * devices)
    keep, send = pl.pallas_call(
        lambda *refs: boundary_kernel(s, n_band, scale, *refs),
        out_shape=(jax.ShapeDtypeStruct(shape, F32), jax.ShapeDtypeStruct(shape, BF16)),
        in_specs=[SMEM] + [VMEM] * 7,
        out_specs=(VMEM, VMEM),
        scratch_shapes=[pltpu.VMEM((n, 13, tiles, LANES), F32), pltpu.SMEM((1,), jnp.int32)] + operands(LANES),
        compiler_params=PARAMS,
    )(place, *local, from_below, from_above)

    value = keep + exchange(send, 1, devices).astype(F32)
    parts = [exchange(value[:, d].astype(BF16), d * n_slab, devices) for d in range(1, n_band)]
    value = sum([p.astype(F32) for p in parts], value[:, 0])
    parts = [exchange(value[e].astype(BF16), 2 * e, devices) for e in range(1, tiles // 2)]
    value = sum([p.astype(F32) for p in parts], value[0])
    value = value.reshape(groups, share, s.bands, GROUP).transpose(1, 2, 0, 3)
    return value.reshape(share, s.bands, groups * GROUP)


def solution(mesh):
    return jax.shard_map(
        body,
        mesh=mesh,
        in_specs=(P(None, None, None, AXES, None),),
        out_specs=P("band", None, "slab"),
        check_vma=False,
    )
```

```python
import jax
import jax.numpy as jnp
from jax import lax
from jax.experimental import pallas as pl
from jax.experimental.pallas import tpu as pltpu
from jax.sharding import PartitionSpec as P

AXES = ("band", "slab")
LANES = 128
GROUP = 16
F32 = jnp.float32
BF16 = jnp.bfloat16
VMEM = pl.BlockSpec(memory_space=pltpu.VMEM)
SMEM = pl.BlockSpec(memory_space=pltpu.SMEM)
ANY = pl.BlockSpec(memory_space=pl.ANY)
PARAMS = pltpu.CompilerParams(vmem_limit_bytes=32 * 2**20)


class Sizes:
    def __init__(self, shape):
        self.bands, self.comps, self.planes, self.rows, cells = shape
        self.inner = self.planes - 2
        self.tiles = cells // LANES


def row(ref, s, q, c, x, y):
    if s.rows == 1:
        return ref[q, c, x]
    return ref[q, c, x, pl.ds(y, s.tiles, stride=s.rows), :]


def z_difference(value):
    tiles = value.shape[0]
    lane = lax.broadcasted_iota(jnp.int32, value.shape, 1)
    left = pltpu.roll(value, LANES - 1, 1)
    right = pltpu.roll(value, 1, 1)
    after = jnp.where(lane == LANES - 1, pltpu.roll(left, tiles - 1, 0), left)
    before = jnp.where(lane == 0, pltpu.roll(right, 1, 0), right)
    return after - before


def edge_kernel(s, x_ref, up_ref, down_ref, coefs, sums):
    last = s.rows - 1
    n = s.inner

    def band(q, carry):
        for c in range(s.comps):
            for p in range(n // 2):
                pair = [row(x_ref, s, q, c, 1 + 2 * p + k, last) for k in range(2)]
                up_ref[(q * s.comps + c) * (n // 2) + p] = jnp.concatenate(pair, 0).astype(BF16)
        return carry

    lax.fori_loop(0, s.bands, band, 0)

    def add(j, carry):
        c, x = (j // s.planes, j % s.planes)
        for y in range(s.rows):
            total = row(x_ref, s, 0, c, x, y)
            for q in range(1, s.bands):
                total = total + row(x_ref, s, q, c, x, y)
            sums[c, x, y] = total
        return carry

    lax.fori_loop(0, s.comps * s.planes, add, 0)
    currents = [[], [], []]
    for x in range(n):
        down_ref[x] = sums[3, x + 1, 0]
        down_ref[n + x] = sums[5, x + 1, 0]
        for y in range(s.rows):
            v = [sums[c, x + 1, y] for c in range(3)]
            b = [sums[c, x + 1, y] for c in range(3, 6)]

            def dy(c):
                high = sums[c, x + 1, y + 1] if y + 1 < s.rows else 0.0
                low = sums[c, x + 1, y - 1] if y else 0.0
                return high - low

            def dx(c):
                return sums[c, x + 2, y] - sums[c, x, y]

            j = [dy(5) - z_difference(b[1]), z_difference(b[0]) - dx(5), dx(4) - dy(3)]
            j = [value * 0.5 for value in j]
            for d in range(3):
                coefs[x, y, d] = (v[d] - b[d]) * -0.25
                coefs[x, y, 3 + d] = (v[d] + b[d]) * -0.25
                coefs[x, y, 6 + d] = j[d]
                if y == last:
                    currents[d].append(j[d])
    base = s.bands * s.comps * (n // 2)
    for c in range(3):
        for p in range(n // 2):
            up_ref[base + c * (n // 2) + p] = jnp.concatenate(currents[c][2 * p : 2 * p + 2], 0).astype(BF16)


def transposed(s, source, zt):
    depth = source.shape[0] // s.tiles
    return source[pl.ds(zt, depth, stride=s.tiles), :].T.astype(BF16)


def put(s, target, zt, slot, block):
    target[zt, :, slot] = block.reshape(LANES // GROUP, GROUP, block.shape[-1])


def diagonal_products(s, rt, dt, zt, g):
    wide = s.bands * GROUP
    left = rt[zt, g].reshape(wide, rt.shape[-1])
    right = dt[zt, g].reshape(wide, dt.shape[-1])
    full = lax.dot_general(left, right, (((1,), (1,)), ((), ())), preferred_element_type=F32)
    full = full.reshape(s.bands, GROUP, wide)
    cell = lax.broadcasted_iota(jnp.int32, full.shape, 1)
    lane = lax.broadcasted_iota(jnp.int32, full.shape, 2)
    return jnp.sum(jnp.where(cell == lane % GROUP, full, 0.0), 1)


def slot_of(s, place, q, n_band):
    share = s.bands // n_band
    return (q // share ^ place[0]) * share + q % share


def cross(a, b):
    return [a[1] * b[2] - a[2] * b[1], a[2] * b[0] - a[0] * b[2], a[0] * b[1] - a[1] * b[0]]


def local_depth(s):
    return (s.rows - 1) * s.inner * 9 if s.rows > 1 else 0


def set_row(s, ref, entry, value):
    ref[pl.ds(entry * s.tiles, s.tiles), :] = value


def local_band(s, q, x_ref, coefs, above_ref, drive_ref, field_ref, sr, sd, between):
    n, last = (s.inner, s.rows - 1)
    entry = 0
    for y in range(s.rows):
        behind, here = ([row(x_ref, s, q, c, x, y) for c in range(6)] for x in range(2))
        for x in range(n):
            ahead = [row(x_ref, s, q, c, x + 2, y) for c in range(6)]
            f = here
            dx = [p - m for p, m in zip(ahead, behind)]
            dy, dz = ([], [])
            for c in range(6):
                high = row(x_ref, s, q, c, x + 1, y + 1) if y < last else None
                low = row(x_ref, s, q, c, x + 1, y - 1) if y else None
                if high is None:
                    dy.append(jnp.zeros_like(f[0]) if low is None else -low)
                else:
                    dy.append(high if low is None else high - low)
                dz.append(z_difference(f[c]))
            deltas = (dx, dy, dz)
            da, dc = ([], [])
            for c in range(3):
                plus = minus = None
                for d in range(3):
                    p = coefs[x, y, d] * (deltas[d][c] + deltas[d][c + 3])
                    m = coefs[x, y, 3 + d] * (deltas[d][c] - deltas[d][c + 3])
                    plus = p if plus is None else plus + p
                    minus = m if minus is None else minus + m
                da.append(plus + minus)
                dc.append(plus - minus)
            j = [(dy[5] - dz[4]) * 0.5, (dz[3] - dx[5]) * 0.5, (dx[4] - dy[3]) * 0.5]
            drives = da + dc
            if y == 0:
                for c in range(6):
                    drive_ref[q, x, c] = drives[c]
                    field_ref[q, x, c] = f[c]
                for c in range(3):
                    drive_ref[q, x, 6 + c] = j[c]
            else:
                turn = [coefs[x, y, 6 + d] * -0.5 for d in range(3)]
                if y == last:
                    turn = [turn[0] - above_ref[n + x] * 0.25, turn[1], turn[2] + above_ref[x] * 0.25]
                for a, b in zip(f + j, drives + cross(turn, f[3:6])):
                    set_row(s, sr, entry, a)
                    set_row(s, sd, entry, b)
                    entry += 1
            behind, here = (here, ahead)
        between(y)


def local_kernel(s, n_band, place, x_hbm, coefs, above_ref, g_ref, drive_ref, field_ref, x_ref, rt, dt, *rest):
    pads, sems = (rest[:-1], rest[-1])
    for q in range(s.bands):
        pltpu.make_async_copy(x_hbm.at[q], x_ref.at[q], sems.at[q]).start()
    used = local_depth(s)
    for ref in pads:
        tail = ref.shape[0] - used * s.tiles
        ref[pl.ds(used * s.tiles, tail), :] = jnp.zeros((tail, LANES), F32)

    def turn(sr, sd, q, tiles):
        for zt in tiles:
            put(s, rt, zt, slot_of(s, place, q, n_band), transposed(s, sr, zt))
            put(s, dt, zt, q, transposed(s, sd, zt))

    def pair(p, carry):
        for k in range(2):
            q = 2 * p + k
            pltpu.make_async_copy(x_hbm.at[q], x_ref.at[q], sems.at[q]).wait()
            other = pads[2 - 2 * k : 4 - 2 * k]
            before = lax.rem(q + s.bands - 1, s.bands)

            def between(y):
                if used:
                    turn(*other, before, range(y * s.tiles // s.rows, (y + 1) * s.tiles // s.rows))

            local_band(s, q, x_ref, coefs, above_ref, drive_ref, field_ref, *pads[2 * k : 2 * k + 2], between)
        return carry

    lax.fori_loop(0, s.bands // 2, pair, 0)

    def tile(zt, carry):
        for g in range(LANES // GROUP):
            g_ref[zt, g] = diagonal_products(s, rt, dt, zt, g)
        return carry

    if used:
        turn(*pads[2:4], s.bands - 1, range(s.tiles))
        lax.fori_loop(0, s.tiles, tile, 0)
    else:
        g_ref[...] = jnp.zeros_like(g_ref)


def halo_pair(s, up_ref, index):
    rows = []
    for p in range(s.inner // 2):
        both = up_ref[index * (s.inner // 2) + p].astype(F32)
        rows += [both[: s.tiles], both[s.tiles :]]
    return rows


def boundary_kernel(s, n_band, scale, place, g_ref, drive_ref, field_ref, coefs, down_ref, up_ref, above_ref, keep_ref, send_ref, tots, rt, dt, *pads):
    n = s.inner
    half = LANES // 2
    zero = jnp.zeros((s.tiles, LANES), F32)
    kinds = (1, 4, 3, 5)

    def add(q, totals):
        rows = sum([halo_pair(s, up_ref, q * s.comps + c) for c in kinds], [])
        return [t + r for t, r in zip(totals, rows)]

    totals = lax.fori_loop(0, s.bands, add, [zero] * (4 * n))
    behinds = [halo_pair(s, up_ref, s.bands * s.comps + c) for c in range(3)]
    for x in range(n):
        vy, my, bx, bz = (totals[k * n + x] for k in range(4))
        tots[x, 0] = coefs[x, 0, 1]
        tots[x, 1] = coefs[x, 0, 4]
        tots[x, 2] = (vy - my) * -0.25
        tots[x, 3] = (vy + my) * -0.25
        j = [coefs[x, 0, 6] - bz * 0.5, coefs[x, 0, 7], coefs[x, 0, 8] + bx * 0.5]
        if s.rows == 1:
            j = [j[0] + above_ref[n + x] * 0.5, j[1], j[2] - above_ref[x] * 0.5]
        behind = [behinds[0][x] + down_ref[n + x] * 0.5, behinds[1][x], behinds[2][x] - down_ref[x] * 0.5]
        for c in range(3):
            tots[x, 4 + c] = j[c] * -0.5
            tots[x, 7 + c] = behind[c] * -0.5
    used = n * 15
    for ref in pads:
        for start in (0, half):
            tail = (half - used) * s.tiles
            ref[pl.ds((start + used) * s.tiles, tail), :] = jnp.zeros((tail, LANES), F32)

    def turn(pad, q, tiles):
        lane = lax.broadcasted_iota(jnp.int32, (LANES, LANES), 1)
        for zt in tiles:
            block = transposed(s, pad, zt)
            put(s, rt, zt, slot_of(s, place, q, n_band), block)
            put(s, dt, zt, q, jnp.where(lane < half, pltpu.roll(block, half, 1), jnp.zeros_like(block)))

    def band(q, pad, between):
        entry = 0
        h_all = [halo_pair(s, up_ref, q * s.comps + c) for c in range(6)]
        for x in range(n):
            f = [field_ref[q, x, c] for c in range(6)]
            h = [h_all[c][x] for c in range(6)]
            da, dc, ea, ec = ([], [], [], [])
            for c in range(3):
                p = tots[x, 0] * (h[c] + h[c + 3])
                m = tots[x, 1] * (h[c] - h[c + 3])
                da.append(drive_ref[q, x, c] - (p + m))
                dc.append(drive_ref[q, x, 3 + c] - (p - m))
                p = tots[x, 2] * (f[c] + f[c + 3])
                m = tots[x, 3] * (f[c] - f[c + 3])
                ea.append(p + m)
                ec.append(p - m)
            behind = cross([tots[x, 7 + c] for c in range(3)], h[3:6])
            dc[0] = dc[0] - behind[2] * 0.5
            dc[2] = dc[2] + behind[0] * 0.5
            j = [drive_ref[q, x, 6] - h[5] * 0.5, drive_ref[q, x, 7], drive_ref[q, x, 8] + h[3] * 0.5]
            left = f + j + h
            right = da + dc + cross([tots[x, 4 + c] for c in range(3)], f[3:6]) + ea + ec
            for a, b in zip(left, right):
                set_row(s, pad, entry, a)
                set_row(s, pad, half + entry, b)
                entry += 1
            between(x)

    def pair(p, carry):
        for k in range(2):
            q = 2 * p + k
            before = lax.rem(q + s.bands - 1, s.bands)
            band(q, pads[k], lambda x: turn(pads[1 - k], before, range(x * s.tiles // n, (x + 1) * s.tiles // n)))
        return carry

    lax.fori_loop(0, s.bands // 2, pair, 0)
    turn(pads[1], s.bands - 1, range(s.tiles))
    share = s.bands // n_band

    def tile(r, carry):
        for core in range(2):
            zt = (r * 2 + core) ^ place[1]
            parts = [(diagonal_products(s, rt, dt, zt, g) + g_ref[zt, g]) * scale for g in range(LANES // GROUP)]
            for b in range(n_band):
                block = jnp.concatenate([p[b * share : (b + 1) * share] for p in parts], 0)
                if core == 0:
                    keep_ref[r, b] = block
                else:
                    send_ref[r, b] = block.astype(BF16)
        return carry

    lax.fori_loop(0, s.tiles // 2, tile, 0)


def exchange(value, distance, size):
    return lax.ppermute(value, AXES, [(i, i ^ distance) for i in range(size)])


def body(band_fields):
    s = Sizes(band_fields.shape)
    n_band, n_slab = (lax.axis_size("band"), lax.axis_size("slab"))
    devices = n_band * n_slab
    n, tiles, rows = (s.inner, s.tiles, s.rows)
    x = band_fields.reshape(s.bands, s.comps, s.planes, rows, tiles, LANES)
    x = x.transpose(0, 1, 2, 4, 3, 5).reshape(s.bands, s.comps, s.planes, tiles * rows, LANES)
    place = jnp.stack([lax.axis_index("band"), lax.axis_index("slab")]).astype(jnp.int32)

    def vector(*lead):
        return jax.ShapeDtypeStruct(lead + (tiles, LANES), F32)

    depth = -(-(max(local_depth(s), 1)) // LANES) * LANES
    groups = LANES // GROUP
    wide = s.bands * GROUP
    share = s.bands // n_band
    rows_up = (s.bands * s.comps + 3) * (n // 2)

    up, down, coefs = pl.pallas_call(
        lambda *refs: edge_kernel(s, *refs),
        out_shape=(jax.ShapeDtypeStruct((rows_up, 2 * tiles, LANES), BF16), vector(2 * n), vector(n, rows, 9)),
        in_specs=[VMEM],
        out_specs=(VMEM,) * 3,
        scratch_shapes=[pltpu.VMEM((s.comps, s.planes, rows, tiles, LANES), F32)],
        compiler_params=PARAMS,
    )(x)
    step = [(i, (i + 1) % devices) for i in range(devices)]
    from_below = lax.ppermute(up, AXES, step)
    from_above = lax.ppermute(down, AXES, [(j, i) for i, j in step])

    def operands(used, pads):
        return [pltpu.VMEM((tiles, groups, s.bands, GROUP, used), BF16)] * 2 + [pltpu.VMEM((used * tiles, LANES), F32)] * pads

    local, drive, field = pl.pallas_call(
        lambda *refs: local_kernel(s, n_band, *refs),
        out_shape=(jax.ShapeDtypeStruct((tiles, groups, s.bands, wide), F32), vector(s.bands, n, 9), vector(s.bands, n, 6)),
        in_specs=[SMEM, ANY, VMEM, VMEM],
        out_specs=(VMEM,) * 3,
        scratch_shapes=[pltpu.VMEM(x.shape, F32)] + operands(depth, 4) + [pltpu.SemaphoreType.DMA((s.bands,))],
        compiler_params=PARAMS,
        cost_estimate=pl.CostEstimate(flops=2 * 10**9, bytes_accessed=2 * 10**7, transcendentals=0),
    )(place, x, coefs, from_above)
    if rows == 1:
        two = lax.ppermute(down, AXES, [(i, (i + 2) % devices) for i in range(devices)])
        two = two.reshape(2, n // 2, 2 * tiles, LANES) * 0.5
        base = s.bands * s.comps * (n // 2)
        behind = from_below[base:].astype(F32).reshape(3, n // 2, 2 * tiles, LANES)
        behind = jnp.stack([behind[0] - two[1], behind[1], behind[2] + two[0]])
        behind = behind.reshape(3 * (n // 2), 2 * tiles, LANES).astype(BF16)
        from_below = jnp.concatenate([from_below[:base], behind], 0)

    shape = (tiles // 2, n_band, groups * share, wide)
    scale = 1.0 / (n * rows * devices)
    keep, send = pl.pallas_call(
        lambda *refs: boundary_kernel(s, n_band, scale, *refs),
        out_shape=(jax.ShapeDtypeStruct(shape, F32), jax.ShapeDtypeStruct(shape, BF16)),
        in_specs=[SMEM] + [VMEM] * 7,
        out_specs=(VMEM, VMEM),
        scratch_shapes=[pltpu.VMEM((n, 10, tiles, LANES), F32)] + operands(LANES, 2),
        compiler_params=PARAMS,
    )(place, local, drive, field, coefs, down, from_below, from_above)

    value = keep + exchange(send, 1, devices).astype(F32)
    parts = [exchange(value[:, d].astype(BF16), d * n_slab, devices) for d in range(1, n_band)]
    value = sum([p.astype(F32) for p in parts], value[:, 0])
    parts = [exchange(value[e].astype(BF16), 2 * e, devices) for e in range(1, tiles // 2)]
    value = sum([p.astype(F32) for p in parts], value[0])
    value = value.reshape(groups, share, s.bands, GROUP).transpose(1, 2, 0, 3)
    return value.reshape(share, s.bands, groups * GROUP)


def solution(mesh):
    return jax.shard_map(
        body,
        mesh=mesh,
        in_specs=(P(None, None, None, AXES, None),),
        out_specs=P("band", None, "slab"),
        check_vma=False,
    )
```

```python
import jax
import jax.numpy as jnp
from jax import lax
from jax.experimental import pallas as pl
from jax.experimental.pallas import tpu as pltpu
from jax.sharding import PartitionSpec as P

AXES = ("band", "slab")
LANES = 128
GROUP = 16
F32 = jnp.float32
BF16 = jnp.bfloat16
VMEM = pl.BlockSpec(memory_space=pltpu.VMEM)
SMEM = pl.BlockSpec(memory_space=pltpu.SMEM)
HBM = pl.BlockSpec(memory_space=pltpu.HBM)
EDGE = pltpu.CompilerParams(vmem_limit_bytes=50 * 2**20)
LOCAL = pltpu.CompilerParams(vmem_limit_bytes=38 * 2**20)
BOUNDARY = pltpu.CompilerParams(vmem_limit_bytes=32 * 2**20)


class Sizes:
    def __init__(self, shape):
        self.bands, self.comps, self.planes, self.rows, cells = shape
        self.inner = self.planes - 2
        self.tiles = cells // LANES


def row(ref, s, q, c, x, y):
    if s.rows == 1:
        return ref[q, c, x]
    return ref[q, c, x, pl.ds(y, s.tiles, stride=s.rows), :]


def z_difference(value):
    tiles = value.shape[0]
    lane = lax.broadcasted_iota(jnp.int32, value.shape, 1)
    left = pltpu.roll(value, LANES - 1, 1)
    right = pltpu.roll(value, 1, 1)
    after = jnp.where(lane == LANES - 1, pltpu.roll(left, tiles - 1, 0), left)
    before = jnp.where(lane == 0, pltpu.roll(right, 1, 0), right)
    return after - before


def edge_kernel(s, x_hbm, up_ref, down_ref, coefs, x_ref, sums, sems):
    last = s.rows - 1
    n = s.inner
    whole, inside = (pl.ds(4, 2), pl.ds(0, 4))
    copies = []
    for q in range(s.bands):
        copies.append(pltpu.make_async_copy(x_hbm.at[q, whole], x_ref.at[q, whole], sems.at[q, 0]))
        part = (q, inside, pl.ds(1, n))
        copies.append(pltpu.make_async_copy(x_hbm.at[part], x_ref.at[part], sems.at[q, 1]))
    for copy in copies:
        copy.start()

    def band(q, carry):
        for c in range(s.comps):
            for p in range(n // 2):
                pair = [row(x_ref, s, q, c, 1 + 2 * p + k, last) for k in range(2)]
                up_ref[(q * s.comps + c) * (n // 2) + p] = jnp.concatenate(pair, 0).astype(BF16)
        return carry

    def total_of(first, count, c, x):
        for y in range(s.rows):
            total = row(x_ref, s, first, c, x, y)
            for q in range(first + 1, first + count):
                total = total + row(x_ref, s, q, c, x, y)
            if first:
                total = total + sums[c, x, y]
            sums[c, x, y] = total

    def add(first, count):
        def one(j, carry):
            c, x = (j // n, j % n + 1)
            total_of(first, count, c, x)
            return carry

        lax.fori_loop(0, s.comps * n, one, 0)
        for c in (4, 5):
            for x in (0, s.planes - 1):
                total_of(first, count, c, x)

    share = s.bands // 4
    for first in range(0, s.bands, share):
        for copy in copies[2 * first : 2 * (first + share)]:
            copy.wait()
        lax.fori_loop(first, first + share, band, 0)
        add(first, share)
    currents = [[], [], []]
    for x in range(n):
        down_ref[x] = sums[3, x + 1, 0]
        down_ref[n + x] = sums[5, x + 1, 0]
        for y in range(s.rows):
            v = [sums[c, x + 1, y] for c in range(3)]
            b = [sums[c, x + 1, y] for c in range(3, 6)]

            def dy(c):
                high = sums[c, x + 1, y + 1] if y + 1 < s.rows else 0.0
                low = sums[c, x + 1, y - 1] if y else 0.0
                return high - low

            def dx(c):
                return sums[c, x + 2, y] - sums[c, x, y]

            j = [dy(5) - z_difference(b[1]), z_difference(b[0]) - dx(5), dx(4) - dy(3)]
            j = [value * 0.5 for value in j]
            for d in range(3):
                coefs[x, y, d] = (v[d] - b[d]) * -0.25
                coefs[x, y, 3 + d] = (v[d] + b[d]) * -0.25
                coefs[x, y, 6 + d] = j[d]
                if y == last:
                    currents[d].append(j[d])
    base = s.bands * s.comps * (n // 2)
    for c in range(3):
        for p in range(n // 2):
            up_ref[base + c * (n // 2) + p] = jnp.concatenate(currents[c][2 * p : 2 * p + 2], 0).astype(BF16)


def transposed(s, source, zt):
    depth = source.shape[0] // s.tiles
    return source[pl.ds(zt, depth, stride=s.tiles), :].T.astype(BF16)


def put(s, target, zt, slot, block):
    target[zt, :, slot] = block.reshape(LANES // GROUP, GROUP, block.shape[-1])


def diagonal_products(s, left, right):
    wide = s.bands * GROUP
    full = lax.dot_general(left, right, (((1,), (1,)), ((), ())), preferred_element_type=F32)
    full = full.reshape(s.bands, GROUP, wide)
    cell = lax.broadcasted_iota(jnp.int32, full.shape, 1)
    lane = lax.broadcasted_iota(jnp.int32, full.shape, 2)
    return jnp.sum(jnp.where(cell == lane % GROUP, full, 0.0), 1)


def slot_of(s, place, q, n_band):
    share = s.bands // n_band
    return (q // share ^ place[0]) * share + q % share


def cross(a, b):
    return [a[1] * b[2] - a[2] * b[1], a[2] * b[0] - a[0] * b[2], a[0] * b[1] - a[1] * b[0]]


LAST_PAIRS = ((0, 1), (1, 0), (1, 2), (2, 1))


def local_depth(s):
    return (s.rows - 1) * s.inner * 9 + 4 * s.inner if s.rows > 1 else 0


def set_row(s, ref, entry, value):
    ref[pl.ds(entry * s.tiles, s.tiles), :] = value


def shift_matrix():
    source = lax.broadcasted_iota(jnp.int32, (2 * LANES, 2 * LANES), 0) % LANES
    target = lax.broadcasted_iota(jnp.int32, (2 * LANES, 2 * LANES), 1)
    inside = jnp.where(source == target + 1, 1.0, jnp.where(source == target - 1, -1.0, 0.0))
    carry_up = (target == 2 * LANES - 1) & (source == 0)
    carry_down = (target == LANES) & (source == LANES - 1)
    across = jnp.where(carry_up, 1.0, jnp.where(carry_down, -1.0, 0.0))
    return jnp.where(target < LANES, inside, across).astype(BF16)


def z_differences(s, values, matrix):
    rows = jnp.concatenate(values, 0)
    high = rows.astype(BF16)
    low = (rows - high.astype(F32)).astype(BF16)
    both = jnp.dot(jnp.concatenate([high, low], 1), matrix, preferred_element_type=F32)
    lane = lax.broadcasted_iota(jnp.int32, (s.tiles, LANES), 1)
    out = []
    for i in range(len(values)):
        part = both[i * s.tiles : (i + 1) * s.tiles]
        across = part[:, LANES:]
        across = jnp.where(lane < LANES // 2, pltpu.roll(across, 1, 0), pltpu.roll(across, s.tiles - 1, 0))
        out.append(part[:, :LANES] + across)
    return out


def local_band(s, q, z_ref, x_ref, coefs, drive_ref, field_ref, sr, sd, before, between):
    n, last = (s.inner, s.rows - 1)
    entry = 0
    for y in range(s.rows):
        before(y)
        behind, here = ([row(x_ref, s, q, c, x, y) for c in range(6)] for x in range(2))
        for x in range(n):
            ahead = [row(x_ref, s, q, c, x + 2, y) for c in range(6)]
            f = here
            dx = [p - m for p, m in zip(ahead, behind)]
            dy, dz = ([], [z_ref[y, x, c] for c in range(6)])
            for c in range(6):
                high = row(x_ref, s, q, c, x + 1, y + 1) if y < last else None
                low = row(x_ref, s, q, c, x + 1, y - 1) if y else None
                if high is None:
                    dy.append(jnp.zeros_like(f[0]) if low is None else -low)
                else:
                    dy.append(high if low is None else high - low)
            deltas = (dx, dy, dz)
            da, dc = ([], [])
            for c in range(3):
                plus = minus = None
                for d in range(3):
                    p = coefs[x, y, d] * (deltas[d][c] + deltas[d][c + 3])
                    m = coefs[x, y, 3 + d] * (deltas[d][c] - deltas[d][c + 3])
                    plus = p if plus is None else plus + p
                    minus = m if minus is None else minus + m
                da.append(plus + minus)
                dc.append(plus - minus)
            j = [(dy[5] - dz[4]) * 0.5, (dz[3] - dx[5]) * 0.5, (dx[4] - dy[3]) * 0.5]
            drives = da + dc
            if y == 0:
                for c in range(6):
                    drive_ref[q, x, c] = drives[c]
                    field_ref[q, x, c] = f[c]
                for c in range(3):
                    drive_ref[q, x, 6 + c] = j[c]
            else:
                turn = [coefs[x, y, 6 + d] * -0.5 for d in range(3)]
                left, right = (f + j, drives + cross(turn, f[3:6]))
                if y == last:
                    left += [j[c] for c, _ in LAST_PAIRS]
                    right += [f[3 + c] for _, c in LAST_PAIRS]
                for a, b in zip(left, right):
                    set_row(s, sr, entry, a)
                    set_row(s, sd, entry, b)
                    entry += 1
            behind, here = (here, ahead)
        between(y)


def local_kernel(s, n_band, place, x_hbm, coefs, rt, dt, drive_ref, field_ref, x_ref, sems, matrix, *rest):
    n = s.inner
    z_refs, pads = (rest[:2], rest[2:])

    def fetch(q):
        return pltpu.make_async_copy(x_hbm.at[q], x_ref.at[q], sems.at[q])

    for q in range(s.bands):
        fetch(q).start()
    matrix[...] = shift_matrix()
    used = local_depth(s)
    for ref in pads:
        tail = ref.shape[0] - used * s.tiles
        ref[pl.ds(used * s.tiles, tail), :] = jnp.zeros((tail, LANES), F32)

    def shifted(z_ref, q, y):
        values = [row(x_ref, s, q, c, x + 1, y) for x in range(n) for c in range(6)]
        for i, value in enumerate(z_differences(s, values, matrix[...])):
            z_ref[y, i // 6, i % 6] = value

    def turn(sr, sd, q, tiles):
        for zt in tiles:
            put(s, rt, zt, slot_of(s, place, q, n_band), transposed(s, sr, zt))
            put(s, dt, zt, q, transposed(s, sd, zt))

    def pair(p, carry):
        for k in range(2):
            q = 2 * p + k
            other = pads[2 - 2 * k : 4 - 2 * k]
            behind = lax.rem(q + s.bands - 1, s.bands)
            ahead = lax.rem(q + 1, s.bands)

            @pl.when(q + 1 < s.bands)
            def _():
                fetch(ahead).wait()

            def before(y):
                shifted(z_refs[1 - k], ahead, y)

            def between(y):
                if used:
                    turn(*other, behind, range(y * s.tiles // s.rows, (y + 1) * s.tiles // s.rows))

            local_band(s, q, z_refs[k], x_ref, coefs, drive_ref, field_ref, *pads[2 * k : 2 * k + 2], before, between)
        return carry

    fetch(0).wait()
    for y in range(s.rows):
        shifted(z_refs[0], 0, y)
    lax.fori_loop(0, s.bands // 2, pair, 0)
    if used:
        turn(*pads[2:4], s.bands - 1, range(s.tiles))
    else:
        rt[...] = jnp.zeros_like(rt)
        dt[...] = jnp.zeros_like(dt)


def halo_pair(s, up_ref, index):
    rows = []
    for p in range(s.inner // 2):
        both = up_ref[index * (s.inner // 2) + p].astype(F32)
        rows += [both[: s.tiles], both[s.tiles :]]
    return rows


def boundary_kernel(s, n_band, scale, place, local_rt, local_dt, drive_ref, field_ref, coefs, down_ref, up_ref, above_ref, keep_ref, send_ref, tots, factors, rt, dt, *pads):
    n = s.inner
    half = LANES // 2
    zero = jnp.zeros((s.tiles, LANES), F32)
    kinds = (1, 4, 3, 5)

    def add(q, totals):
        rows = sum([halo_pair(s, up_ref, q * s.comps + c) for c in kinds], [])
        return [t + r for t, r in zip(totals, rows)]

    totals = lax.fori_loop(0, s.bands, add, [zero] * (4 * n))
    behinds = [halo_pair(s, up_ref, s.bands * s.comps + c) for c in range(3)]
    for x in range(n):
        vy, my, bx, bz = (totals[k * n + x] for k in range(4))
        tots[x, 0] = coefs[x, 0, 1]
        tots[x, 1] = coefs[x, 0, 4]
        tots[x, 2] = (vy - my) * -0.25
        tots[x, 3] = (vy + my) * -0.25
        j = [coefs[x, 0, 6] - bz * 0.5, coefs[x, 0, 7], coefs[x, 0, 8] + bx * 0.5]
        if s.rows == 1:
            j = [j[0] + above_ref[n + x] * 0.5, j[1], j[2] - above_ref[x] * 0.5]
        behind = [behinds[0][x] + down_ref[n + x] * 0.5, behinds[1][x], behinds[2][x] - down_ref[x] * 0.5]
        for c in range(3):
            tots[x, 4 + c] = j[c] * -0.5
            tots[x, 7 + c] = behind[c] * -0.5
    if s.rows > 1:
        for k in range(2):
            for entry in range(half):
                e = k * half + entry - (s.rows - 2) * n * 9
                x, i = divmod(e, 13)
                value = jnp.ones((s.tiles, LANES), F32)
                if 0 <= x < n and i >= 9:
                    value = above_ref[(i - 9) // 2 * n + x] * (-0.25, 0.25, 0.25, -0.25)[i - 9]
                set_row(s, pads[k], entry, value)
        for zt in range(s.tiles):
            both = [pads[k][pl.ds(zt, half, stride=s.tiles), :] for k in range(2)]
            factors[zt] = jnp.concatenate(both, 0).T.astype(BF16).reshape(LANES // GROUP, GROUP, LANES)
    used = n * 15
    for ref in pads:
        tail = (half - used) * s.tiles
        ref[pl.ds(used * s.tiles, tail), :] = jnp.zeros((tail, LANES), F32)

    def turn(sr, sd, q, pairs):
        for t in pairs:
            for source, target, slot in ((sr, rt, slot_of(s, place, q, n_band)), (sd, dt, q)):
                both = [source[pl.ds(2 * t + k, half, stride=s.tiles), :] for k in range(2)]
                put(s, target, t, slot, jnp.concatenate(both, 0).T.astype(BF16))

    def band(q, sr, sd, between):
        entry = 0
        h_all = [halo_pair(s, up_ref, q * s.comps + c) for c in range(6)]
        for x in range(n):
            f = [field_ref[q, x, c] for c in range(6)]
            h = [h_all[c][x] for c in range(6)]
            da, dc, ea, ec = ([], [], [], [])
            for c in range(3):
                p = tots[x, 0] * (h[c] + h[c + 3])
                m = tots[x, 1] * (h[c] - h[c + 3])
                da.append(drive_ref[q, x, c] - (p + m))
                dc.append(drive_ref[q, x, 3 + c] - (p - m))
                p = tots[x, 2] * (f[c] + f[c + 3])
                m = tots[x, 3] * (f[c] - f[c + 3])
                ea.append(p + m)
                ec.append(p - m)
            behind = cross([tots[x, 7 + c] for c in range(3)], h[3:6])
            dc[0] = dc[0] - behind[2] * 0.5
            dc[2] = dc[2] + behind[0] * 0.5
            j = [drive_ref[q, x, 6] - h[5] * 0.5, drive_ref[q, x, 7], drive_ref[q, x, 8] + h[3] * 0.5]
            left = f + j + h
            right = da + dc + cross([tots[x, 4 + c] for c in range(3)], f[3:6]) + ea + ec
            for a, b in zip(left, right):
                set_row(s, sr, entry, a)
                set_row(s, sd, entry, b)
                entry += 1
            between(x)

    def pair(p, carry):
        for k in range(2):
            q = 2 * p + k
            before = lax.rem(q + s.bands - 1, s.bands)
            other = pads[2 - 2 * k : 4 - 2 * k]
            band(q, *pads[2 * k : 2 * k + 2], lambda x: turn(*other, before, range(x * steps // n, (x + 1) * steps // n)))
        return carry

    steps = s.tiles // 2
    lax.fori_loop(0, s.bands // 2, pair, 0)
    turn(*pads[2:4], s.bands - 1, range(steps))
    wide = s.bands * GROUP
    lane = lax.broadcasted_iota(jnp.int32, (wide, LANES), 1)
    share = s.bands // n_band

    def tile(r, carry):
        for core in range(2):
            zt = (r * 2 + core) ^ place[1]
            wanted = (lane >= half) == ((core ^ place[1]) % 2 == 1)
            parts = []
            for g in range(LANES // GROUP):
                left = rt[zt // 2, g].reshape(wide, LANES)
                left = jnp.where(wanted, left, jnp.zeros_like(left))
                right = dt[zt // 2, g].reshape(wide, LANES)
                if s.rows > 1:
                    scaled = local_rt[zt, g] * factors[zt, g][None]
                    left = jnp.concatenate([scaled.reshape(wide, -1), left], 1)
                    right = jnp.concatenate([local_dt[zt, g].reshape(wide, -1), right], 1)
                parts.append(diagonal_products(s, left, right) * scale)
            for b in range(n_band):
                block = jnp.concatenate([p[b * share : (b + 1) * share] for p in parts], 0)
                if core == 0:
                    keep_ref[r, b] = block
                else:
                    send_ref[r, b] = block.astype(BF16)
        return carry

    lax.fori_loop(0, s.tiles // 2, tile, 0)


def exchange(value, distance, size):
    return lax.ppermute(value, AXES, [(i, i ^ distance) for i in range(size)])


def body(band_fields):
    s = Sizes(band_fields.shape)
    n_band, n_slab = (lax.axis_size("band"), lax.axis_size("slab"))
    devices = n_band * n_slab
    n, tiles, rows = (s.inner, s.tiles, s.rows)
    x = band_fields.reshape(s.bands, s.comps, s.planes, rows, tiles, LANES)
    x = x.transpose(0, 1, 2, 4, 3, 5).reshape(s.bands, s.comps, s.planes, tiles * rows, LANES)
    place = jnp.stack([lax.axis_index("band"), lax.axis_index("slab")]).astype(jnp.int32)

    def vector(*lead):
        return jax.ShapeDtypeStruct(lead + (tiles, LANES), F32)

    depth = -(-(max(local_depth(s), 1)) // LANES) * LANES
    groups = LANES // GROUP
    wide = s.bands * GROUP
    share = s.bands // n_band
    rows_up = (s.bands * s.comps + 3) * (n // 2)

    up, down, coefs = pl.pallas_call(
        lambda *refs: edge_kernel(s, *refs),
        out_shape=(jax.ShapeDtypeStruct((rows_up, 2 * tiles, LANES), BF16), vector(2 * n), vector(n, rows, 9)),
        in_specs=[HBM],
        out_specs=(VMEM,) * 3,
        scratch_shapes=[pltpu.VMEM(x.shape, F32), pltpu.VMEM((s.comps, s.planes, rows, tiles, LANES), F32), pltpu.SemaphoreType.DMA((s.bands, 2))],
        compiler_params=EDGE,
    )(x)
    step = [(i, (i + 1) % devices) for i in range(devices)]
    from_below = lax.ppermute(up, AXES, step)
    from_above = lax.ppermute(down, AXES, [(j, i) for i, j in step])

    turned = jax.ShapeDtypeStruct((tiles, groups, s.bands, GROUP, depth), BF16)
    local_rt, local_dt, drive, field = pl.pallas_call(
        lambda *refs: local_kernel(s, n_band, *refs),
        out_shape=(turned, turned, vector(s.bands, n, 9), vector(s.bands, n, 6)),
        in_specs=[SMEM, HBM, VMEM],
        out_specs=(VMEM,) * 4,
        scratch_shapes=[pltpu.VMEM(x.shape, F32), pltpu.SemaphoreType.DMA((s.bands,)), pltpu.VMEM((2 * LANES, 2 * LANES), BF16)]
        + [pltpu.VMEM((rows, n, 6, tiles, LANES), F32)] * 2
        + [pltpu.VMEM((depth * tiles, LANES), F32)] * 4,
        compiler_params=LOCAL,
        cost_estimate=pl.CostEstimate(flops=2 * 10**9, bytes_accessed=2 * 10**7, transcendentals=0),
    )(place, x, coefs)
    if rows == 1:
        two = lax.ppermute(down, AXES, [(i, (i + 2) % devices) for i in range(devices)])
        two = two.reshape(2, n // 2, 2 * tiles, LANES) * 0.5
        base = s.bands * s.comps * (n // 2)
        behind = from_below[base:].astype(F32).reshape(3, n // 2, 2 * tiles, LANES)
        behind = jnp.stack([behind[0] - two[1], behind[1], behind[2] + two[0]])
        behind = behind.reshape(3 * (n // 2), 2 * tiles, LANES).astype(BF16)
        from_below = jnp.concatenate([from_below[:base], behind], 0)

    shape = (tiles // 2, n_band, groups * share, wide)
    scale = 1.0 / (n * rows * devices)
    keep, send = pl.pallas_call(
        lambda *refs: boundary_kernel(s, n_band, scale, *refs),
        out_shape=(jax.ShapeDtypeStruct(shape, F32), jax.ShapeDtypeStruct(shape, BF16)),
        in_specs=[SMEM] + [VMEM] * 8,
        out_specs=(VMEM, VMEM),
        scratch_shapes=[pltpu.VMEM((n, 10, tiles, LANES), F32), pltpu.VMEM((tiles, groups, GROUP, LANES), BF16)]
        + [pltpu.VMEM((tiles // 2, groups, s.bands, GROUP, LANES), BF16)] * 2
        + [pltpu.VMEM((LANES // 2 * tiles, LANES), F32)] * 4,
        compiler_params=BOUNDARY,
    )(place, local_rt, local_dt, drive, field, coefs, down, from_below, from_above)

    value = keep + exchange(send, 1, devices).astype(F32)
    parts = [exchange(value[:, d].astype(BF16), d * n_slab, devices) for d in range(1, n_band)]
    value = sum([p.astype(F32) for p in parts], value[:, 0])
    parts = [exchange(value[e].astype(BF16), 2 * e, devices) for e in range(1, tiles // 2)]
    value = sum([p.astype(F32) for p in parts], value[0])
    value = value.reshape(groups, share, s.bands, GROUP).transpose(1, 2, 0, 3)
    return value.reshape(share, s.bands, groups * GROUP)


def solution(mesh):
    return jax.shard_map(
        body,
        mesh=mesh,
        in_specs=(P(None, None, None, AXES, None),),
        out_specs=P("band", None, "slab"),
        check_vma=False,
    )
```

```python
import jax
import jax.numpy as jnp
from jax import lax
from jax.experimental import pallas as pl
from jax.experimental.pallas import tpu as pltpu
from jax.sharding import PartitionSpec as P

AXES = ("band", "slab")
LANES = 128
GROUP = 16
SUBLANES = 8
F32 = jnp.float32
BF16 = jnp.bfloat16
VMEM = pl.BlockSpec(memory_space=pltpu.VMEM)
SMEM = pl.BlockSpec(memory_space=pltpu.SMEM)
HBM = pl.BlockSpec(memory_space=pltpu.HBM)
EDGE = pltpu.CompilerParams(vmem_limit_bytes=50 * 2**20)
LOCAL = pltpu.CompilerParams(vmem_limit_bytes=38 * 2**20)
BOUNDARY = pltpu.CompilerParams(vmem_limit_bytes=32 * 2**20)


class Sizes:
    def __init__(self, shape):
        self.bands, self.comps, self.planes, self.rows, cells = shape
        self.inner = self.planes - 2
        self.tiles = cells // LANES
        self.pitch = self.tiles + 1


def row(ref, s, q, c, x, y):
    if s.rows == 1:
        return ref[q, c, x]
    return ref[q, c, x, pl.ds(y, s.tiles, stride=s.rows), :]


def z_difference(value):
    tiles = value.shape[0]
    lane = lax.broadcasted_iota(jnp.int32, value.shape, 1)
    left = pltpu.roll(value, LANES - 1, 1)
    right = pltpu.roll(value, 1, 1)
    after = jnp.where(lane == LANES - 1, pltpu.roll(left, tiles - 1, 0), left)
    before = jnp.where(lane == 0, pltpu.roll(right, 1, 0), right)
    return after - before


def edge_kernel(s, x_hbm, up_ref, down_ref, coefs, x_ref, sums, sems):
    last = s.rows - 1
    n = s.inner
    whole, inside = (pl.ds(4, 2), pl.ds(0, 4))
    copies = []
    for q in range(s.bands):
        copies.append(pltpu.make_async_copy(x_hbm.at[q, whole], x_ref.at[q, whole], sems.at[q, 0]))
        part = (q, inside, pl.ds(1, n))
        copies.append(pltpu.make_async_copy(x_hbm.at[part], x_ref.at[part], sems.at[q, 1]))
    for copy in copies:
        copy.start()

    def band(q, carry):
        for c in range(s.comps):
            for p in range(n // 2):
                pair = [row(x_ref, s, q, c, 1 + 2 * p + k, last) for k in range(2)]
                up_ref[(q * s.comps + c) * (n // 2) + p] = jnp.concatenate(pair, 0).astype(BF16)
        return carry

    def total_of(first, count, c, x):
        for y in range(s.rows):
            total = row(x_ref, s, first, c, x, y)
            for q in range(first + 1, first + count):
                total = total + row(x_ref, s, q, c, x, y)
            if first:
                total = total + sums[c, x, y]
            sums[c, x, y] = total

    def add(first, count):
        def one(j, carry):
            c, x = (j // n, j % n + 1)
            total_of(first, count, c, x)
            return carry

        lax.fori_loop(0, s.comps * n, one, 0)
        for c in (4, 5):
            for x in (0, s.planes - 1):
                total_of(first, count, c, x)

    share = s.bands // 4
    for first in range(0, s.bands, share):
        for copy in copies[2 * first : 2 * (first + share)]:
            copy.wait()
        lax.fori_loop(first, first + share, band, 0)
        add(first, share)
    currents = [[], [], []]
    for x in range(n):
        down_ref[x] = sums[3, x + 1, 0]
        down_ref[n + x] = sums[5, x + 1, 0]
        for y in range(s.rows):
            v = [sums[c, x + 1, y] for c in range(3)]
            b = [sums[c, x + 1, y] for c in range(3, 6)]

            def dy(c):
                high = sums[c, x + 1, y + 1] if y + 1 < s.rows else 0.0
                low = sums[c, x + 1, y - 1] if y else 0.0
                return high - low

            def dx(c):
                return sums[c, x + 2, y] - sums[c, x, y]

            j = [dy(5) - z_difference(b[1]), z_difference(b[0]) - dx(5), dx(4) - dy(3)]
            j = [value * 0.5 for value in j]
            for d in range(3):
                coefs[x, y, d] = (v[d] - b[d]) * -0.25
                coefs[x, y, 3 + d] = (v[d] + b[d]) * -0.25
                coefs[x, y, 6 + d] = j[d]
                if y == last:
                    currents[d].append(j[d])
    base = s.bands * s.comps * (n // 2)
    for c in range(3):
        for p in range(n // 2):
            up_ref[base + c * (n // 2) + p] = jnp.concatenate(currents[c][2 * p : 2 * p + 2], 0).astype(BF16)


def transposed(s, source, zt):
    depth = source.shape[0] // s.pitch
    return source[pl.ds(zt, depth, stride=s.pitch), :].astype(BF16).T


def put(s, target, zt, slot, block):
    target[zt, :, slot] = block.reshape(LANES // GROUP, GROUP, block.shape[-1])


def diagonal_products(s, left, right):
    wide = s.bands * GROUP
    full = lax.dot_general(left, right, (((1,), (1,)), ((), ())), preferred_element_type=F32)
    lane = lax.broadcasted_iota(jnp.int32, (SUBLANES, wide), 1)
    sublane = lax.broadcasted_iota(jnp.int32, (SUBLANES, wide), 0)
    upper = lane % GROUP >= SUBLANES
    skew = (sublane - lane) % SUBLANES
    blocks = []
    for first in range(0, s.bands, SUBLANES):
        mixed = None
        for k in range(SUBLANES):
            top = (first + k) * GROUP
            part = jnp.where(upper, full[top + SUBLANES : top + GROUP], full[top : top + SUBLANES])
            part = pltpu.roll(part, k, 0) if k else part
            mixed = part if mixed is None else jnp.where(skew == k, part, mixed)
        for bit in (1, 2, 4):
            mixed = jnp.where((lane & bit) != 0, pltpu.roll(mixed, SUBLANES - bit, 0), mixed)
        blocks.append(mixed)
    return jnp.concatenate(blocks, 0)


def slot_of(s, place, q, n_band):
    share = s.bands // n_band
    return (q // share ^ place[0]) * share + q % share


def cross(a, b):
    return [a[1] * b[2] - a[2] * b[1], a[2] * b[0] - a[0] * b[2], a[0] * b[1] - a[1] * b[0]]


LAST_PAIRS = ((0, 1), (1, 0), (1, 2), (2, 1))


def local_depth(s):
    return (s.rows - 1) * s.inner * 9 + 4 * s.inner if s.rows > 1 else 0


def set_row(s, ref, entry, value):
    ref[pl.ds(entry * s.pitch, s.tiles), :] = value


def shift_matrix():
    source = lax.broadcasted_iota(jnp.int32, (2 * LANES, 2 * LANES), 0) % LANES
    target = lax.broadcasted_iota(jnp.int32, (2 * LANES, 2 * LANES), 1)
    inside = jnp.where(source == target + 1, 1.0, jnp.where(source == target - 1, -1.0, 0.0))
    carry_up = (target == 2 * LANES - 1) & (source == 0)
    carry_down = (target == LANES) & (source == LANES - 1)
    across = jnp.where(carry_up, 1.0, jnp.where(carry_down, -1.0, 0.0))
    return jnp.where(target < LANES, inside, across).astype(BF16)


def z_differences(s, values, matrix):
    rows = jnp.concatenate(values, 0)
    high = rows.astype(BF16)
    low = (rows - high.astype(F32)).astype(BF16)
    both = jnp.dot(jnp.concatenate([high, low], 1), matrix, preferred_element_type=F32)
    lane = lax.broadcasted_iota(jnp.int32, (s.tiles, LANES), 1)
    out = []
    for i in range(len(values)):
        part = both[i * s.tiles : (i + 1) * s.tiles]
        across = part[:, LANES:]
        across = jnp.where(lane < LANES // 2, pltpu.roll(across, 1, 0), pltpu.roll(across, s.tiles - 1, 0))
        out.append(part[:, :LANES] + across)
    return out


def local_band(s, q, z_ref, x_ref, coefs, drive_ref, field_ref, sr, sd, before, between):
    n, last = (s.inner, s.rows - 1)
    entry = 0
    for y in range(s.rows):
        before(y)
        behind, here = ([row(x_ref, s, q, c, x, y) for c in range(6)] for x in range(2))
        for x in range(n):
            ahead = [row(x_ref, s, q, c, x + 2, y) for c in range(6)]
            f = here
            dx = [p - m for p, m in zip(ahead, behind)]
            dy, dz = ([], [z_ref[y, x, c] for c in range(6)])
            for c in range(6):
                high = row(x_ref, s, q, c, x + 1, y + 1) if y < last else None
                low = row(x_ref, s, q, c, x + 1, y - 1) if y else None
                if high is None:
                    dy.append(jnp.zeros_like(f[0]) if low is None else -low)
                else:
                    dy.append(high if low is None else high - low)
            deltas = (dx, dy, dz)
            da, dc = ([], [])
            for c in range(3):
                plus = minus = None
                for d in range(3):
                    p = coefs[x, y, d] * (deltas[d][c] + deltas[d][c + 3])
                    m = coefs[x, y, 3 + d] * (deltas[d][c] - deltas[d][c + 3])
                    plus = p if plus is None else plus + p
                    minus = m if minus is None else minus + m
                da.append(plus + minus)
                dc.append(plus - minus)
            j = [(dy[5] - dz[4]) * 0.5, (dz[3] - dx[5]) * 0.5, (dx[4] - dy[3]) * 0.5]
            drives = da + dc
            if y == 0:
                for c in range(6):
                    drive_ref[q, x, c] = drives[c]
                    field_ref[q, x, c] = f[c]
                for c in range(3):
                    drive_ref[q, x, 6 + c] = j[c]
            else:
                turn = [coefs[x, y, 6 + d] * -0.5 for d in range(3)]
                left, right = (f + j, drives + cross(turn, f[3:6]))
                if y == last:
                    left += [j[c] for c, _ in LAST_PAIRS]
                    right += [f[3 + c] for _, c in LAST_PAIRS]
                for a, b in zip(left, right):
                    set_row(s, sr, entry, a)
                    set_row(s, sd, entry, b)
                    entry += 1
            behind, here = (here, ahead)
        between(y)


def local_kernel(s, n_band, place, x_hbm, coefs, rt, dt, drive_ref, field_ref, x_ref, sems, matrix, *rest):
    n = s.inner
    z_refs, pads = (rest[:2], rest[2:])

    def fetch(q):
        return pltpu.make_async_copy(x_hbm.at[q], x_ref.at[q], sems.at[q])

    for q in range(s.bands):
        fetch(q).start()
    matrix[...] = shift_matrix()
    used = local_depth(s)
    for ref in pads:
        tail = ref.shape[0] - used * s.pitch
        ref[pl.ds(used * s.pitch, tail), :] = jnp.zeros((tail, LANES), F32)

    def shifted(z_ref, q, y):
        values = [row(x_ref, s, q, c, x + 1, y) for x in range(n) for c in range(6)]
        for i, value in enumerate(z_differences(s, values, matrix[...])):
            z_ref[y, i // 6, i % 6] = value

    def turn(sr, sd, q, tiles):
        for zt in tiles:
            put(s, rt, zt, slot_of(s, place, q, n_band), transposed(s, sr, zt))
            put(s, dt, zt, q, transposed(s, sd, zt))

    def pair(p, carry):
        for k in range(2):
            q = 2 * p + k
            other = pads[2 - 2 * k : 4 - 2 * k]
            behind = lax.rem(q + s.bands - 1, s.bands)
            ahead = lax.rem(q + 1, s.bands)

            @pl.when(q + 1 < s.bands)
            def _():
                fetch(ahead).wait()

            def before(y):
                shifted(z_refs[1 - k], ahead, y)

            def between(y):
                if used:
                    turn(*other, behind, range(y * s.tiles // s.rows, (y + 1) * s.tiles // s.rows))

            local_band(s, q, z_refs[k], x_ref, coefs, drive_ref, field_ref, *pads[2 * k : 2 * k + 2], before, between)
        return carry

    fetch(0).wait()
    for y in range(s.rows):
        shifted(z_refs[0], 0, y)
    lax.fori_loop(0, s.bands // 2, pair, 0)
    if used:
        turn(*pads[2:4], s.bands - 1, range(s.tiles))
    else:
        rt[...] = jnp.zeros_like(rt)
        dt[...] = jnp.zeros_like(dt)


def halo_pair(s, up_ref, index):
    rows = []
    for p in range(s.inner // 2):
        both = up_ref[index * (s.inner // 2) + p].astype(F32)
        rows += [both[: s.tiles], both[s.tiles :]]
    return rows


def boundary_kernel(s, n_band, scale, place, local_rt, local_dt, drive_ref, field_ref, coefs, down_ref, up_ref, above_ref, keep_ref, send_ref, tots, factors, rt, dt, *pads):
    n = s.inner
    half = LANES // 2
    zero = jnp.zeros((s.tiles, LANES), F32)
    kinds = (1, 4, 3, 5)

    def add(q, totals):
        rows = sum([halo_pair(s, up_ref, q * s.comps + c) for c in kinds], [])
        return [t + r for t, r in zip(totals, rows)]

    totals = lax.fori_loop(0, s.bands, add, [zero] * (4 * n))
    behinds = [halo_pair(s, up_ref, s.bands * s.comps + c) for c in range(3)]
    for x in range(n):
        vy, my, bx, bz = (totals[k * n + x] for k in range(4))
        tots[x, 0] = coefs[x, 0, 1]
        tots[x, 1] = coefs[x, 0, 4]
        tots[x, 2] = (vy - my) * -0.25
        tots[x, 3] = (vy + my) * -0.25
        j = [coefs[x, 0, 6] - bz * 0.5, coefs[x, 0, 7], coefs[x, 0, 8] + bx * 0.5]
        if s.rows == 1:
            j = [j[0] + above_ref[n + x] * 0.5, j[1], j[2] - above_ref[x] * 0.5]
        behind = [behinds[0][x] + down_ref[n + x] * 0.5, behinds[1][x], behinds[2][x] - down_ref[x] * 0.5]
        for c in range(3):
            tots[x, 4 + c] = j[c] * -0.5
            tots[x, 7 + c] = behind[c] * -0.5
    if s.rows > 1:
        for k in range(2):
            for entry in range(half):
                e = k * half + entry - (s.rows - 2) * n * 9
                x, i = divmod(e, 13)
                value = jnp.ones((s.tiles, LANES), F32)
                if 0 <= x < n and i >= 9:
                    value = above_ref[(i - 9) // 2 * n + x] * (-0.25, 0.25, 0.25, -0.25)[i - 9]
                set_row(s, pads[k], entry, value)
        for zt in range(s.tiles):
            both = [pads[k][pl.ds(zt, half, stride=s.pitch), :] for k in range(2)]
            factors[zt] = jnp.concatenate(both, 0).T.astype(BF16).reshape(LANES // GROUP, GROUP, LANES)
    used = n * 15
    for ref in pads:
        tail = (half - used) * s.pitch
        ref[pl.ds(used * s.pitch, tail), :] = jnp.zeros((tail, LANES), F32)

    def turn(sr, sd, q, pairs):
        for t in pairs:
            for source, target, slot in ((sr, rt, slot_of(s, place, q, n_band)), (sd, dt, q)):
                both = [source[pl.ds(2 * t + k, half, stride=s.pitch), :] for k in range(2)]
                put(s, target, t, slot, jnp.concatenate(both, 0).astype(BF16).T)

    def band(q, sr, sd, between):
        entry = 0
        h_all = [halo_pair(s, up_ref, q * s.comps + c) for c in range(6)]
        for x in range(n):
            f = [field_ref[q, x, c] for c in range(6)]
            h = [h_all[c][x] for c in range(6)]
            da, dc, ea, ec = ([], [], [], [])
            for c in range(3):
                p = tots[x, 0] * (h[c] + h[c + 3])
                m = tots[x, 1] * (h[c] - h[c + 3])
                da.append(drive_ref[q, x, c] - (p + m))
                dc.append(drive_ref[q, x, 3 + c] - (p - m))
                p = tots[x, 2] * (f[c] + f[c + 3])
                m = tots[x, 3] * (f[c] - f[c + 3])
                ea.append(p + m)
                ec.append(p - m)
            behind = cross([tots[x, 7 + c] for c in range(3)], h[3:6])
            dc[0] = dc[0] - behind[2] * 0.5
            dc[2] = dc[2] + behind[0] * 0.5
            j = [drive_ref[q, x, 6] - h[5] * 0.5, drive_ref[q, x, 7], drive_ref[q, x, 8] + h[3] * 0.5]
            left = f + j + h
            right = da + dc + cross([tots[x, 4 + c] for c in range(3)], f[3:6]) + ea + ec
            for a, b in zip(left, right):
                set_row(s, sr, entry, a)
                set_row(s, sd, entry, b)
                entry += 1
            between(x)

    def pair(p, carry):
        for k in range(2):
            q = 2 * p + k
            before = lax.rem(q + s.bands - 1, s.bands)
            other = pads[2 - 2 * k : 4 - 2 * k]
            band(q, *pads[2 * k : 2 * k + 2], lambda x: turn(*other, before, range(x * steps // n, (x + 1) * steps // n)))
        return carry

    steps = s.tiles // 2
    lax.fori_loop(0, s.bands // 2, pair, 0)
    turn(*pads[2:4], s.bands - 1, range(steps))
    wide = s.bands * GROUP
    lane = lax.broadcasted_iota(jnp.int32, (wide, LANES), 1)
    share = s.bands // n_band

    def tile(r, carry):
        for core in range(2):
            zt = (r * 2 + core) ^ place[1]
            wanted = (lane >= half) == ((core ^ place[1]) % 2 == 1)
            parts = []
            for g in range(LANES // GROUP):
                left = rt[zt // 2, g].reshape(wide, LANES)
                left = jnp.where(wanted, left, jnp.zeros_like(left))
                right = dt[zt // 2, g].reshape(wide, LANES)
                if s.rows > 1:
                    scaled = local_rt[zt, g] * factors[zt, g][None]
                    left = jnp.concatenate([scaled.reshape(wide, -1), left], 1)
                    right = jnp.concatenate([local_dt[zt, g].reshape(wide, -1), right], 1)
                parts.append(diagonal_products(s, left, right) * scale)
            for b in range(n_band):
                block = jnp.concatenate([p[b * share : (b + 1) * share] for p in parts], 0)
                if core == 0:
                    keep_ref[r, b] = block
                else:
                    send_ref[r, b] = block.astype(BF16)
        return carry

    lax.fori_loop(0, s.tiles // 2, tile, 0)


def exchange(value, distance, size):
    return lax.ppermute(value, AXES, [(i, i ^ distance) for i in range(size)])


def body(band_fields):
    s = Sizes(band_fields.shape)
    n_band, n_slab = (lax.axis_size("band"), lax.axis_size("slab"))
    devices = n_band * n_slab
    n, tiles, rows = (s.inner, s.tiles, s.rows)
    x = band_fields.reshape(s.bands, s.comps, s.planes, rows, tiles, LANES)
    x = x.transpose(0, 1, 2, 4, 3, 5).reshape(s.bands, s.comps, s.planes, tiles * rows, LANES)
    place = jnp.stack([lax.axis_index("band"), lax.axis_index("slab")]).astype(jnp.int32)

    def vector(*lead):
        return jax.ShapeDtypeStruct(lead + (tiles, LANES), F32)

    depth = -(-(max(local_depth(s), 1)) // LANES) * LANES
    groups = LANES // GROUP
    wide = s.bands * GROUP
    share = s.bands // n_band
    rows_up = (s.bands * s.comps + 3) * (n // 2)

    up, down, coefs = pl.pallas_call(
        lambda *refs: edge_kernel(s, *refs),
        out_shape=(jax.ShapeDtypeStruct((rows_up, 2 * tiles, LANES), BF16), vector(2 * n), vector(n, rows, 9)),
        in_specs=[HBM],
        out_specs=(VMEM,) * 3,
        scratch_shapes=[pltpu.VMEM(x.shape, F32), pltpu.VMEM((s.comps, s.planes, rows, tiles, LANES), F32), pltpu.SemaphoreType.DMA((s.bands, 2))],
        compiler_params=EDGE,
    )(x)
    step = [(i, (i + 1) % devices) for i in range(devices)]
    from_below = lax.ppermute(up, AXES, step)
    from_above = lax.ppermute(down, AXES, [(j, i) for i, j in step])

    turned = jax.ShapeDtypeStruct((tiles, groups, s.bands, GROUP, depth), BF16)
    local_rt, local_dt, drive, field = pl.pallas_call(
        lambda *refs: local_kernel(s, n_band, *refs),
        out_shape=(turned, turned, vector(s.bands, n, 9), vector(s.bands, n, 6)),
        in_specs=[SMEM, HBM, VMEM],
        out_specs=(VMEM,) * 4,
        scratch_shapes=[pltpu.VMEM(x.shape, F32), pltpu.SemaphoreType.DMA((s.bands,)), pltpu.VMEM((2 * LANES, 2 * LANES), BF16)]
        + [pltpu.VMEM((rows, n, 6, tiles, LANES), F32)] * 2
        + [pltpu.VMEM((depth * s.pitch, LANES), F32)] * 4,
        compiler_params=LOCAL,
        cost_estimate=pl.CostEstimate(flops=2 * 10**9, bytes_accessed=2 * 10**7, transcendentals=0),
    )(place, x, coefs)
    if rows == 1:
        two = lax.ppermute(down, AXES, [(i, (i + 2) % devices) for i in range(devices)])
        two = two.reshape(2, n // 2, 2 * tiles, LANES) * 0.5
        base = s.bands * s.comps * (n // 2)
        behind = from_below[base:].astype(F32).reshape(3, n // 2, 2 * tiles, LANES)
        behind = jnp.stack([behind[0] - two[1], behind[1], behind[2] + two[0]])
        behind = behind.reshape(3 * (n // 2), 2 * tiles, LANES).astype(BF16)
        from_below = jnp.concatenate([from_below[:base], behind], 0)

    shape = (tiles // 2, n_band, groups * share, wide)
    scale = 1.0 / (n * rows * devices)
    keep, send = pl.pallas_call(
        lambda *refs: boundary_kernel(s, n_band, scale, *refs),
        out_shape=(jax.ShapeDtypeStruct(shape, F32), jax.ShapeDtypeStruct(shape, BF16)),
        in_specs=[SMEM] + [VMEM] * 8,
        out_specs=(VMEM, VMEM),
        scratch_shapes=[pltpu.VMEM((n, 10, tiles, LANES), F32), pltpu.VMEM((tiles, groups, GROUP, LANES), BF16)]
        + [pltpu.VMEM((tiles // 2, groups, s.bands, GROUP, LANES), BF16)] * 2
        + [pltpu.VMEM((LANES // 2 * s.pitch, LANES), F32)] * 4,
        compiler_params=BOUNDARY,
    )(place, local_rt, local_dt, drive, field, coefs, down, from_below, from_above)

    value = keep + exchange(send, 1, devices).astype(F32)
    parts = [exchange(value[:, d].astype(BF16), d * n_slab, devices) for d in range(1, n_band)]
    value = sum([p.astype(F32) for p in parts], value[:, 0])
    parts = [exchange(value[e].astype(BF16), 2 * e, devices) for e in range(1, tiles // 2)]
    value = sum([p.astype(F32) for p in parts], value[0])
    value = value.reshape(groups, share, s.bands, GROUP).transpose(1, 2, 0, 3)
    return value.reshape(share, s.bands, groups * GROUP)


def solution(mesh):
    return jax.shard_map(
        body,
        mesh=mesh,
        in_specs=(P(None, None, None, AXES, None),),
        out_specs=P("band", None, "slab"),
        check_vma=False,
    )
```

```python
import jax
import jax.numpy as jnp
from jax import lax
from jax.experimental import pallas as pl
from jax.experimental.pallas import tpu as pltpu
from jax.sharding import PartitionSpec as P

AXES = ("band", "slab")
LANES = 128
GROUP = 16
SUBLANES = 8
F32 = jnp.float32
BF16 = jnp.bfloat16
VMEM = pl.BlockSpec(memory_space=pltpu.VMEM)
SMEM = pl.BlockSpec(memory_space=pltpu.SMEM)
HBM = pl.BlockSpec(memory_space=pltpu.HBM)
EDGE = pltpu.CompilerParams(vmem_limit_bytes=50 * 2**20)
LOCAL = pltpu.CompilerParams(vmem_limit_bytes=38 * 2**20)
BOUNDARY = pltpu.CompilerParams(vmem_limit_bytes=32 * 2**20)


class Sizes:
    def __init__(self, shape):
        self.bands, self.comps, self.planes, self.rows, cells = shape
        self.inner = self.planes - 2
        self.tiles = cells // LANES
        self.pitch = self.tiles + 1


def row(ref, s, q, c, x, y):
    if s.rows == 1:
        return ref[q, c, x]
    return ref[q, c, x, pl.ds(y, s.tiles, stride=s.rows), :]


def z_difference(value):
    tiles = value.shape[0]
    lane = lax.broadcasted_iota(jnp.int32, value.shape, 1)
    left = pltpu.roll(value, LANES - 1, 1)
    right = pltpu.roll(value, 1, 1)
    after = jnp.where(lane == LANES - 1, pltpu.roll(left, tiles - 1, 0), left)
    before = jnp.where(lane == 0, pltpu.roll(right, 1, 0), right)
    return after - before


def edge_kernel(s, x_hbm, up_ref, down_ref, coefs, x_ref, sums, sems):
    last = s.rows - 1
    n = s.inner
    whole, inside = (pl.ds(4, 2), pl.ds(0, 4))
    copies = []
    for q in range(s.bands):
        copies.append(pltpu.make_async_copy(x_hbm.at[q, whole], x_ref.at[q, whole], sems.at[q, 0]))
        part = (q, inside, pl.ds(1, n))
        copies.append(pltpu.make_async_copy(x_hbm.at[part], x_ref.at[part], sems.at[q, 1]))
    for copy in copies:
        copy.start()

    def band(q, carry):
        for c in range(s.comps):
            for p in range(n // 2):
                pair = [row(x_ref, s, q, c, 1 + 2 * p + k, last) for k in range(2)]
                up_ref[(q * s.comps + c) * (n // 2) + p] = jnp.concatenate(pair, 0).astype(BF16)
        return carry

    def total_of(first, count, c, x):
        for y in range(s.rows):
            total = row(x_ref, s, first, c, x, y)
            for q in range(first + 1, first + count):
                total = total + row(x_ref, s, q, c, x, y)
            if first:
                total = total + sums[c, x, y]
            sums[c, x, y] = total

    def add(first, count):
        def one(j, carry):
            c, x = (j // n, j % n + 1)
            total_of(first, count, c, x)
            return carry

        lax.fori_loop(0, s.comps * n, one, 0)
        for c in (4, 5):
            for x in (0, s.planes - 1):
                total_of(first, count, c, x)

    share = s.bands // 4
    for first in range(0, s.bands, share):
        for copy in copies[2 * first : 2 * (first + share)]:
            copy.wait()
        lax.fori_loop(first, first + share, band, 0)
        add(first, share)
    currents = [[], [], []]
    for x in range(n):
        down_ref[x] = sums[3, x + 1, 0]
        down_ref[n + x] = sums[5, x + 1, 0]
        for y in range(s.rows):
            v = [sums[c, x + 1, y] for c in range(3)]
            b = [sums[c, x + 1, y] for c in range(3, 6)]

            def dy(c):
                high = sums[c, x + 1, y + 1] if y + 1 < s.rows else 0.0
                low = sums[c, x + 1, y - 1] if y else 0.0
                return high - low

            def dx(c):
                return sums[c, x + 2, y] - sums[c, x, y]

            j = [dy(5) - z_difference(b[1]), z_difference(b[0]) - dx(5), dx(4) - dy(3)]
            j = [value * 0.5 for value in j]
            for d in range(3):
                coefs[x, y, d] = (v[d] - b[d]) * -0.25
                coefs[x, y, 3 + d] = (v[d] + b[d]) * -0.25
                coefs[x, y, 6 + d] = j[d]
                if y == last:
                    currents[d].append(j[d])
    base = s.bands * s.comps * (n // 2)
    for c in range(3):
        for p in range(n // 2):
            up_ref[base + c * (n // 2) + p] = jnp.concatenate(currents[c][2 * p : 2 * p + 2], 0).astype(BF16)


def transposed(s, source, zt):
    depth = source.shape[0] // s.pitch
    return source[pl.ds(zt, depth, stride=s.pitch), :].astype(BF16).T


def put(s, target, zt, slot, block):
    target[zt, :, slot] = block.reshape(LANES // GROUP, GROUP, block.shape[-1])


def diagonal_products(s, left, right):
    wide = s.bands * GROUP
    full = lax.dot_general(left, right, (((1,), (1,)), ((), ())), preferred_element_type=F32)
    lane = lax.broadcasted_iota(jnp.int32, (SUBLANES, wide), 1)
    sublane = lax.broadcasted_iota(jnp.int32, (SUBLANES, wide), 0)
    upper = lane % GROUP >= SUBLANES
    skew = (sublane - lane) % SUBLANES
    blocks = []
    for first in range(0, s.bands, SUBLANES):
        mixed = None
        for k in range(SUBLANES):
            top = (first + k) * GROUP
            part = jnp.where(upper, full[top + SUBLANES : top + GROUP], full[top : top + SUBLANES])
            part = pltpu.roll(part, k, 0) if k else part
            mixed = part if mixed is None else jnp.where(skew == k, part, mixed)
        for bit in (1, 2, 4):
            mixed = jnp.where((lane & bit) != 0, pltpu.roll(mixed, SUBLANES - bit, 0), mixed)
        blocks.append(mixed)
    return jnp.concatenate(blocks, 0)


def slot_of(s, place, q, n_band):
    share = s.bands // n_band
    return (q // share ^ place[0]) * share + q % share


def cross(a, b):
    return [a[1] * b[2] - a[2] * b[1], a[2] * b[0] - a[0] * b[2], a[0] * b[1] - a[1] * b[0]]


LAST_PAIRS = ((0, 1), (1, 0), (1, 2), (2, 1))


def local_depth(s):
    return (s.rows - 1) * s.inner * 9 + 4 * s.inner if s.rows > 1 else 0


def set_row(s, ref, entry, value):
    ref[pl.ds(entry * s.pitch, s.tiles), :] = value


def shift_matrix():
    source = lax.broadcasted_iota(jnp.int32, (2 * LANES, 2 * LANES), 0) % LANES
    target = lax.broadcasted_iota(jnp.int32, (2 * LANES, 2 * LANES), 1)
    inside = jnp.where(source == target + 1, 1.0, jnp.where(source == target - 1, -1.0, 0.0))
    carry_up = (target == 2 * LANES - 1) & (source == 0)
    carry_down = (target == LANES) & (source == LANES - 1)
    across = jnp.where(carry_up, 1.0, jnp.where(carry_down, -1.0, 0.0))
    return jnp.where(target < LANES, inside, across).astype(BF16)


def z_differences(s, values, matrix):
    rows = jnp.concatenate(values, 0)
    high = rows.astype(BF16)
    low = (rows - high.astype(F32)).astype(BF16)
    both = jnp.dot(jnp.concatenate([high, low], 1), matrix, preferred_element_type=F32)
    lane = lax.broadcasted_iota(jnp.int32, (s.tiles, LANES), 1)
    out = []
    for i in range(len(values)):
        part = both[i * s.tiles : (i + 1) * s.tiles]
        across = part[:, LANES:]
        across = jnp.where(lane < LANES // 2, pltpu.roll(across, 1, 0), pltpu.roll(across, s.tiles - 1, 0))
        out.append(part[:, :LANES] + across)
    return out


def local_band(s, q, z_ref, x_ref, coefs, drive_ref, field_ref, sr, sd, before, begin, between):
    n, last = (s.inner, s.rows - 1)
    entry = 0
    for y in range(s.rows):
        before(y)
        behind, here = ([row(x_ref, s, q, c, x, y) for c in range(6)] for x in range(2))
        for x in range(n):
            held = begin(y * n + x)
            ahead = [row(x_ref, s, q, c, x + 2, y) for c in range(6)]
            f = here
            dx = [p - m for p, m in zip(ahead, behind)]
            dy, dz = ([], [z_ref[y, x, c] for c in range(6)])
            for c in range(6):
                high = row(x_ref, s, q, c, x + 1, y + 1) if y < last else None
                low = row(x_ref, s, q, c, x + 1, y - 1) if y else None
                if high is None:
                    dy.append(jnp.zeros_like(f[0]) if low is None else -low)
                else:
                    dy.append(high if low is None else high - low)
            deltas = (dx, dy, dz)
            da, dc = ([], [])
            for c in range(3):
                plus = minus = None
                for d in range(3):
                    p = coefs[x, y, d] * (deltas[d][c] + deltas[d][c + 3])
                    m = coefs[x, y, 3 + d] * (deltas[d][c] - deltas[d][c + 3])
                    plus = p if plus is None else plus + p
                    minus = m if minus is None else minus + m
                da.append(plus + minus)
                dc.append(plus - minus)
            j = [(dy[5] - dz[4]) * 0.5, (dz[3] - dx[5]) * 0.5, (dx[4] - dy[3]) * 0.5]
            drives = da + dc
            if y == 0:
                for c in range(6):
                    drive_ref[q, x, c] = drives[c]
                    field_ref[q, x, c] = f[c]
                for c in range(3):
                    drive_ref[q, x, 6 + c] = j[c]
            else:
                turn = [coefs[x, y, 6 + d] * -0.5 for d in range(3)]
                left, right = (f + j, drives + cross(turn, f[3:6]))
                if y == last:
                    left += [j[c] for c, _ in LAST_PAIRS]
                    right += [f[3 + c] for _, c in LAST_PAIRS]
                for a, b in zip(left, right):
                    set_row(s, sr, entry, a)
                    set_row(s, sd, entry, b)
                    entry += 1
            behind, here = (here, ahead)
            between(y * n + x, held)


def local_kernel(s, n_band, place, x_hbm, coefs, rt, dt, drive_ref, field_ref, x_ref, sems, matrix, *rest):
    n = s.inner
    z_refs, pads = (rest[:2], rest[2:])

    def fetch(q):
        return pltpu.make_async_copy(x_hbm.at[q], x_ref.at[q], sems.at[q])

    for q in range(s.bands):
        fetch(q).start()
    matrix[...] = shift_matrix()
    used = local_depth(s)
    for ref in pads:
        tail = ref.shape[0] - used * s.pitch
        ref[pl.ds(used * s.pitch, tail), :] = jnp.zeros((tail, LANES), F32)

    def shifted(z_ref, q, y):
        values = [row(x_ref, s, q, c, x + 1, y) for x in range(n) for c in range(6)]
        for i, value in enumerate(z_differences(s, values, matrix[...])):
            z_ref[y, i // 6, i % 6] = value

    def turn(sr, sd, q, tiles):
        for zt in tiles:
            put(s, rt, zt, slot_of(s, place, q, n_band), transposed(s, sr, zt))
            put(s, dt, zt, q, transposed(s, sd, zt))

    def pair(p, carry):
        for k in range(2):
            q = 2 * p + k
            other = pads[2 - 2 * k : 4 - 2 * k]
            behind = lax.rem(q + s.bands - 1, s.bands)
            ahead = lax.rem(q + 1, s.bands)

            @pl.when(q + 1 < s.bands)
            def _():
                fetch(ahead).wait()

            def before(y):
                shifted(z_refs[1 - k], ahead, y)

            def begin(step):
                steps = s.rows * n
                items = range(step * 2 * s.tiles // steps, (step + 1) * 2 * s.tiles // steps if used else 0)
                return [(item, transposed(s, other[item % 2], item // 2)) for item in items]

            def between(step, held):
                for item, block in held:
                    if item % 2:
                        put(s, dt, item // 2, behind, block)
                    else:
                        put(s, rt, item // 2, slot_of(s, place, behind, n_band), block)

            local_band(s, q, z_refs[k], x_ref, coefs, drive_ref, field_ref, *pads[2 * k : 2 * k + 2], before, begin, between)
        return carry

    fetch(0).wait()
    for y in range(s.rows):
        shifted(z_refs[0], 0, y)
    lax.fori_loop(0, s.bands // 2, pair, 0)
    if used:
        turn(*pads[2:4], s.bands - 1, range(s.tiles))
    else:
        rt[...] = jnp.zeros_like(rt)
        dt[...] = jnp.zeros_like(dt)


def halo_pair(s, up_ref, index):
    rows = []
    for p in range(s.inner // 2):
        both = up_ref[index * (s.inner // 2) + p].astype(F32)
        rows += [both[: s.tiles], both[s.tiles :]]
    return rows


def boundary_kernel(s, n_band, scale, place, local_rt, local_dt, drive_ref, field_ref, coefs, down_ref, up_ref, above_ref, send_ref, rt, dt, factors, tots, *pads):
    n = s.inner
    half = LANES // 2
    zero = jnp.zeros((s.tiles, LANES), F32)
    kinds = (1, 4, 3, 5)

    def add(q, totals):
        rows = sum([halo_pair(s, up_ref, q * s.comps + c) for c in kinds], [])
        return [t + r for t, r in zip(totals, rows)]

    totals = lax.fori_loop(0, s.bands, add, [zero] * (4 * n))
    behinds = [halo_pair(s, up_ref, s.bands * s.comps + c) for c in range(3)]
    for x in range(n):
        vy, my, bx, bz = (totals[k * n + x] for k in range(4))
        tots[x, 0] = coefs[x, 0, 1]
        tots[x, 1] = coefs[x, 0, 4]
        tots[x, 2] = (vy - my) * -0.25
        tots[x, 3] = (vy + my) * -0.25
        j = [coefs[x, 0, 6] - bz * 0.5, coefs[x, 0, 7], coefs[x, 0, 8] + bx * 0.5]
        if s.rows == 1:
            j = [j[0] + above_ref[n + x] * 0.5, j[1], j[2] - above_ref[x] * 0.5]
        behind = [behinds[0][x] + down_ref[n + x] * 0.5, behinds[1][x], behinds[2][x] - down_ref[x] * 0.5]
        for c in range(3):
            tots[x, 4 + c] = j[c] * -0.5
            tots[x, 7 + c] = behind[c] * -0.5
    if s.rows > 1:
        for k in range(2):
            for entry in range(half):
                e = k * half + entry - (s.rows - 2) * n * 9
                x, i = divmod(e, 13)
                value = jnp.ones((s.tiles, LANES), F32)
                if 0 <= x < n and i >= 9:
                    value = above_ref[(i - 9) // 2 * n + x] * (-0.25, 0.25, 0.25, -0.25)[i - 9]
                set_row(s, pads[k], entry, value)
        for zt in range(s.tiles):
            both = [pads[k][pl.ds(zt, half, stride=s.pitch), :] for k in range(2)]
            factors[zt] = jnp.concatenate(both, 0).T.astype(BF16).reshape(LANES // GROUP, GROUP, LANES)
    used = n * 15
    for ref in pads:
        tail = (half - used) * s.pitch
        ref[pl.ds(used * s.pitch, tail), :] = jnp.zeros((tail, LANES), F32)

    def turn(sr, sd, q, pairs):
        for t in pairs:
            for source, target, slot in ((sr, rt, slot_of(s, place, q, n_band)), (sd, dt, q)):
                both = [source[pl.ds(2 * t + k, half, stride=s.pitch), :] for k in range(2)]
                put(s, target, t, slot, jnp.concatenate(both, 0).astype(BF16).T)

    def band(q, sr, sd, between):
        entry = 0
        h_all = [halo_pair(s, up_ref, q * s.comps + c) for c in range(6)]
        for x in range(n):
            f = [field_ref[q, x, c] for c in range(6)]
            h = [h_all[c][x] for c in range(6)]
            da, dc, ea, ec = ([], [], [], [])
            for c in range(3):
                p = tots[x, 0] * (h[c] + h[c + 3])
                m = tots[x, 1] * (h[c] - h[c + 3])
                da.append(drive_ref[q, x, c] - (p + m))
                dc.append(drive_ref[q, x, 3 + c] - (p - m))
                p = tots[x, 2] * (f[c] + f[c + 3])
                m = tots[x, 3] * (f[c] - f[c + 3])
                ea.append(p + m)
                ec.append(p - m)
            behind = cross([tots[x, 7 + c] for c in range(3)], h[3:6])
            dc[0] = dc[0] - behind[2] * 0.5
            dc[2] = dc[2] + behind[0] * 0.5
            j = [drive_ref[q, x, 6] - h[5] * 0.5, drive_ref[q, x, 7], drive_ref[q, x, 8] + h[3] * 0.5]
            left = f + j + h
            right = da + dc + cross([tots[x, 4 + c] for c in range(3)], f[3:6]) + ea + ec
            for a, b in zip(left, right):
                set_row(s, sr, entry, a)
                set_row(s, sd, entry, b)
                entry += 1
            between(x)

    def pair(p, carry):
        for k in range(2):
            q = 2 * p + k
            before = lax.rem(q + s.bands - 1, s.bands)
            other = pads[2 - 2 * k : 4 - 2 * k]
            band(q, *pads[2 * k : 2 * k + 2], lambda x: turn(*other, before, range(x * steps // n, (x + 1) * steps // n)))
        return carry

    steps = s.tiles // 2
    lax.fori_loop(0, s.bands // 2, pair, 0)
    turn(*pads[2:4], s.bands - 1, range(steps))
    products(s, n_band, scale, 1, place, local_rt, local_dt, rt, dt, factors, send_ref)


def products(s, n_band, scale, core, place, local_rt, local_dt, rt, dt, factors, out_ref):
    wide = s.bands * GROUP
    half = LANES // 2
    share = s.bands // n_band
    lane = lax.broadcasted_iota(jnp.int32, (wide, LANES), 1)
    wanted = (lane >= half) == ((core ^ place[1]) % 2 == 1)

    def tile(r, carry):
        zt = (r * 2 + core) ^ place[1]
        parts = []
        for g in range(LANES // GROUP):
            left = rt[zt // 2, g].reshape(wide, LANES)
            left = jnp.where(wanted, left, jnp.zeros_like(left))
            right = dt[zt // 2, g].reshape(wide, LANES)
            if s.rows > 1:
                scaled = local_rt[zt, g] * factors[zt, g][None]
                left = jnp.concatenate([scaled.reshape(wide, -1), left], 1)
                right = jnp.concatenate([local_dt[zt, g].reshape(wide, -1), right], 1)
            parts.append(diagonal_products(s, left, right) * scale)
        for b in range(n_band):
            block = jnp.concatenate([p[b * share : (b + 1) * share] for p in parts], 0)
            out_ref[r, b] = block.astype(out_ref.dtype)
        return carry

    lax.fori_loop(0, s.tiles // 2, tile, 0, unroll=4)


def farthest_first(size):
    return sorted(range(1, size), key=lambda d: (-d.bit_count(), d))


def exchange(value, distance, size):
    return lax.ppermute(value, AXES, [(i, i ^ distance) for i in range(size)])


def body(band_fields):
    s = Sizes(band_fields.shape)
    n_band, n_slab = (lax.axis_size("band"), lax.axis_size("slab"))
    devices = n_band * n_slab
    n, tiles, rows = (s.inner, s.tiles, s.rows)
    x = band_fields.reshape(s.bands, s.comps, s.planes, rows, tiles, LANES)
    x = x.transpose(0, 1, 2, 4, 3, 5).reshape(s.bands, s.comps, s.planes, tiles * rows, LANES)
    place = jnp.stack([lax.axis_index("band"), lax.axis_index("slab")]).astype(jnp.int32)

    def vector(*lead):
        return jax.ShapeDtypeStruct(lead + (tiles, LANES), F32)

    depth = -(-(max(local_depth(s), 1)) // LANES) * LANES
    groups = LANES // GROUP
    wide = s.bands * GROUP
    share = s.bands // n_band
    rows_up = (s.bands * s.comps + 3) * (n // 2)

    up, down, coefs = pl.pallas_call(
        lambda *refs: edge_kernel(s, *refs),
        out_shape=(jax.ShapeDtypeStruct((rows_up, 2 * tiles, LANES), BF16), vector(2 * n), vector(n, rows, 9)),
        in_specs=[HBM],
        out_specs=(VMEM,) * 3,
        scratch_shapes=[pltpu.VMEM(x.shape, F32), pltpu.VMEM((s.comps, s.planes, rows, tiles, LANES), F32), pltpu.SemaphoreType.DMA((s.bands, 2))],
        compiler_params=EDGE,
    )(x)
    step = [(i, (i + 1) % devices) for i in range(devices)]
    from_below = lax.ppermute(up, AXES, step)
    from_above = lax.ppermute(down, AXES, [(j, i) for i, j in step])

    turned = jax.ShapeDtypeStruct((tiles, groups, s.bands, GROUP, depth), BF16)
    local_rt, local_dt, drive, field = pl.pallas_call(
        lambda *refs: local_kernel(s, n_band, *refs),
        out_shape=(turned, turned, vector(s.bands, n, 9), vector(s.bands, n, 6)),
        in_specs=[SMEM, HBM, VMEM],
        out_specs=(VMEM,) * 4,
        scratch_shapes=[pltpu.VMEM(x.shape, F32), pltpu.SemaphoreType.DMA((s.bands,)), pltpu.VMEM((2 * LANES, 2 * LANES), BF16)]
        + [pltpu.VMEM((rows, n, 6, tiles, LANES), F32)] * 2
        + [pltpu.VMEM((depth * s.pitch, LANES), F32)] * 4,
        compiler_params=LOCAL,
        cost_estimate=pl.CostEstimate(flops=2 * 10**9, bytes_accessed=2 * 10**7, transcendentals=0),
    )(place, x, coefs)
    if rows == 1:
        two = lax.ppermute(down, AXES, [(i, (i + 2) % devices) for i in range(devices)])
        two = two.reshape(2, n // 2, 2 * tiles, LANES) * 0.5
        base = s.bands * s.comps * (n // 2)
        behind = from_below[base:].astype(F32).reshape(3, n // 2, 2 * tiles, LANES)
        behind = jnp.stack([behind[0] - two[1], behind[1], behind[2] + two[0]])
        behind = behind.reshape(3 * (n // 2), 2 * tiles, LANES).astype(BF16)
        from_below = jnp.concatenate([from_below[:base], behind], 0)

    shape = (tiles // 2, n_band, groups * share, wide)
    scale = 1.0 / (n * rows * devices)
    blocks = jax.ShapeDtypeStruct((tiles // 2, groups, s.bands, GROUP, LANES), BF16)
    send, rt, dt, factors = pl.pallas_call(
        lambda *refs: boundary_kernel(s, n_band, scale, *refs),
        out_shape=(jax.ShapeDtypeStruct(shape, BF16), blocks, blocks, jax.ShapeDtypeStruct((tiles, groups, GROUP, LANES), BF16)),
        in_specs=[SMEM] + [VMEM] * 8,
        out_specs=(VMEM,) * 4,
        scratch_shapes=[pltpu.VMEM((n, 10, tiles, LANES), F32)] + [pltpu.VMEM((LANES // 2 * s.pitch, LANES), F32)] * 4,
        compiler_params=BOUNDARY,
    )(place, local_rt, local_dt, drive, field, coefs, down, from_below, from_above)
    arrived = exchange(send, 1, devices)
    keep = pl.pallas_call(
        lambda place, *refs: products(s, n_band, scale, 0, place, *refs),
        out_shape=jax.ShapeDtypeStruct(shape, F32),
        in_specs=[SMEM] + [VMEM] * 5,
        out_specs=VMEM,
        compiler_params=BOUNDARY,
        cost_estimate=pl.CostEstimate(flops=2 * 10**9, bytes_accessed=2 * 10**7, transcendentals=0),
    )(place, local_rt, local_dt, rt, dt, factors)

    value = keep + arrived.astype(F32)
    parts = [exchange(value[:, d].astype(BF16), d * n_slab, devices) for d in farthest_first(n_band)]
    value = sum([p.astype(F32) for p in parts], value[:, 0])
    parts = [exchange(value[e].astype(BF16), 2 * e, devices) for e in range(tiles // 2 - 1, 0, -1)]
    value = sum([p.astype(F32) for p in parts], value[0])
    value = value.reshape(groups, share, s.bands, GROUP).transpose(1, 2, 0, 3)
    return value.reshape(share, s.bands, groups * GROUP)


def solution(mesh):
    return jax.shard_map(
        body,
        mesh=mesh,
        in_specs=(P(None, None, None, AXES, None),),
        out_specs=P("band", None, "slab"),
        check_vma=False,
    )
```

```python
import jax
import jax.numpy as jnp
from jax import lax
from jax.experimental import pallas as pl
from jax.experimental.pallas import tpu as pltpu
from jax.sharding import PartitionSpec as P

AXES = ("band", "slab")
LANES = 128
GROUP = 16
SUBLANES = 8
F32 = jnp.float32
BF16 = jnp.bfloat16
VMEM = pl.BlockSpec(memory_space=pltpu.VMEM)
SMEM = pl.BlockSpec(memory_space=pltpu.SMEM)
HBM = pl.BlockSpec(memory_space=pltpu.HBM)
EDGE = pltpu.CompilerParams(vmem_limit_bytes=50 * 2**20)
LOCAL = pltpu.CompilerParams(vmem_limit_bytes=38 * 2**20)
BOUNDARY = pltpu.CompilerParams(vmem_limit_bytes=32 * 2**20)


class Sizes:
    def __init__(self, shape):
        self.bands, self.comps, self.planes, self.rows, cells = shape
        self.inner = self.planes - 2
        self.tiles = cells // LANES
        self.pitch = self.tiles + 1


def row(ref, s, q, c, x, y):
    if s.rows == 1:
        return ref[q, c, x]
    return ref[q, c, x, pl.ds(y, s.tiles, stride=s.rows), :]


def z_difference(value):
    tiles = value.shape[0]
    lane = lax.broadcasted_iota(jnp.int32, value.shape, 1)
    left = pltpu.roll(value, LANES - 1, 1)
    right = pltpu.roll(value, 1, 1)
    after = jnp.where(lane == LANES - 1, pltpu.roll(left, tiles - 1, 0), left)
    before = jnp.where(lane == 0, pltpu.roll(right, 1, 0), right)
    return after - before


def edge_kernel(s, x_hbm, up_ref, down_ref, coefs, x_ref, sums, sems):
    last = s.rows - 1
    n = s.inner
    whole, inside = (pl.ds(4, 2), pl.ds(0, 4))
    copies = []
    for q in range(s.bands):
        copies.append(pltpu.make_async_copy(x_hbm.at[q, whole], x_ref.at[q, whole], sems.at[q, 0]))
        part = (q, inside, pl.ds(1, n))
        copies.append(pltpu.make_async_copy(x_hbm.at[part], x_ref.at[part], sems.at[q, 1]))
    for copy in copies:
        copy.start()

    def band(q, carry):
        for c in range(s.comps):
            for p in range(n // 2):
                pair = [row(x_ref, s, q, c, 1 + 2 * p + k, last) for k in range(2)]
                up_ref[(q * s.comps + c) * (n // 2) + p] = jnp.concatenate(pair, 0).astype(BF16)
        return carry

    def total_of(first, count, c, x):
        for y in range(s.rows):
            total = row(x_ref, s, first, c, x, y)
            for q in range(first + 1, first + count):
                total = total + row(x_ref, s, q, c, x, y)
            if first:
                total = total + sums[c, x, y]
            sums[c, x, y] = total

    def add(first, count):
        def one(j, carry):
            c, x = (j // n, j % n + 1)
            total_of(first, count, c, x)
            return carry

        lax.fori_loop(0, s.comps * n, one, 0)
        for c in (4, 5):
            for x in (0, s.planes - 1):
                total_of(first, count, c, x)

    share = s.bands // 4
    for first in range(0, s.bands, share):
        for copy in copies[2 * first : 2 * (first + share)]:
            copy.wait()
        lax.fori_loop(first, first + share, band, 0)
        add(first, share)
    currents = [[], [], []]
    for x in range(n):
        down_ref[x] = sums[3, x + 1, 0]
        down_ref[n + x] = sums[5, x + 1, 0]
        for y in range(s.rows):
            v = [sums[c, x + 1, y] for c in range(3)]
            b = [sums[c, x + 1, y] for c in range(3, 6)]

            def dy(c):
                high = sums[c, x + 1, y + 1] if y + 1 < s.rows else 0.0
                low = sums[c, x + 1, y - 1] if y else 0.0
                return high - low

            def dx(c):
                return sums[c, x + 2, y] - sums[c, x, y]

            j = [dy(5) - z_difference(b[1]), z_difference(b[0]) - dx(5), dx(4) - dy(3)]
            j = [value * 0.5 for value in j]
            for d in range(3):
                coefs[x, y, d] = (v[d] - b[d]) * -0.25
                coefs[x, y, 3 + d] = (v[d] + b[d]) * -0.25
                coefs[x, y, 6 + d] = j[d]
                if y == last:
                    currents[d].append(j[d])
    base = s.bands * s.comps * (n // 2)
    for c in range(3):
        for p in range(n // 2):
            up_ref[base + c * (n // 2) + p] = jnp.concatenate(currents[c][2 * p : 2 * p + 2], 0).astype(BF16)


def transposed(s, source, zt):
    depth = source.shape[0] // s.pitch
    return source[pl.ds(zt, depth, stride=s.pitch), :].astype(BF16).T


def put(s, target, zt, slot, block):
    target[zt, :, slot] = block.reshape(LANES // GROUP, GROUP, block.shape[-1])


def diagonal_products(s, left, right):
    wide = s.bands * GROUP
    full = lax.dot_general(left, right, (((1,), (1,)), ((), ())), preferred_element_type=F32)
    lane = lax.broadcasted_iota(jnp.int32, (SUBLANES, wide), 1)
    sublane = lax.broadcasted_iota(jnp.int32, (SUBLANES, wide), 0)
    upper = lane % GROUP >= SUBLANES
    skew = (sublane - lane) % SUBLANES
    blocks = []
    for first in range(0, s.bands, SUBLANES):
        mixed = None
        for k in range(SUBLANES):
            top = (first + k) * GROUP
            part = jnp.where(upper, full[top + SUBLANES : top + GROUP], full[top : top + SUBLANES])
            part = pltpu.roll(part, k, 0) if k else part
            mixed = part if mixed is None else jnp.where(skew == k, part, mixed)
        for bit in (1, 2, 4):
            mixed = jnp.where((lane & bit) != 0, pltpu.roll(mixed, SUBLANES - bit, 0), mixed)
        blocks.append(mixed)
    return jnp.concatenate(blocks, 0)


def slot_of(s, place, q, n_band):
    share = s.bands // n_band
    return (q // share ^ place[0]) * share + q % share


def cross(a, b):
    return [a[1] * b[2] - a[2] * b[1], a[2] * b[0] - a[0] * b[2], a[0] * b[1] - a[1] * b[0]]


LAST_PAIRS = ((0, 1), (1, 0), (1, 2), (2, 1))


def local_depth(s):
    return (s.rows - 1) * s.inner * 9 + 4 * s.inner if s.rows > 1 else 0


def set_row(s, ref, entry, value):
    ref[pl.ds(entry * s.pitch, s.tiles), :] = value


def shift_matrix():
    source = lax.broadcasted_iota(jnp.int32, (2 * LANES, 2 * LANES), 0) % LANES
    target = lax.broadcasted_iota(jnp.int32, (2 * LANES, 2 * LANES), 1)
    inside = jnp.where(source == target + 1, 1.0, jnp.where(source == target - 1, -1.0, 0.0))
    carry_up = (target == 2 * LANES - 1) & (source == 0)
    carry_down = (target == LANES) & (source == LANES - 1)
    across = jnp.where(carry_up, 1.0, jnp.where(carry_down, -1.0, 0.0))
    return jnp.where(target < LANES, inside, across).astype(BF16)


def z_differences(s, values, matrix):
    rows = jnp.concatenate(values, 0)
    high = rows.astype(BF16)
    low = (rows - high.astype(F32)).astype(BF16)
    both = jnp.dot(jnp.concatenate([high, low], 1), matrix, preferred_element_type=F32)
    lane = lax.broadcasted_iota(jnp.int32, (s.tiles, LANES), 1)
    out = []
    for i in range(len(values)):
        part = both[i * s.tiles : (i + 1) * s.tiles]
        across = part[:, LANES:]
        across = jnp.where(lane < LANES // 2, pltpu.roll(across, 1, 0), pltpu.roll(across, s.tiles - 1, 0))
        out.append(part[:, :LANES] + across)
    return out


def local_band(s, q, z_ref, x_ref, coefs, drive_ref, field_ref, sr, sd, before, begin, between):
    n, last = (s.inner, s.rows - 1)
    entry = 0
    for y in range(s.rows):
        before(y)
        behind, here = ([row(x_ref, s, q, c, x, y) for c in range(6)] for x in range(2))
        for x in range(n):
            held = begin(y * n + x)
            ahead = [row(x_ref, s, q, c, x + 2, y) for c in range(6)]
            f = here
            dx = [p - m for p, m in zip(ahead, behind)]
            dy, dz = ([], [z_ref[y, x, c] for c in range(6)])
            for c in range(6):
                high = row(x_ref, s, q, c, x + 1, y + 1) if y < last else None
                low = row(x_ref, s, q, c, x + 1, y - 1) if y else None
                if high is None:
                    dy.append(jnp.zeros_like(f[0]) if low is None else -low)
                else:
                    dy.append(high if low is None else high - low)
            deltas = (dx, dy, dz)
            da, dc = ([], [])
            for c in range(3):
                plus = minus = None
                for d in range(3):
                    p = coefs[x, y, d] * (deltas[d][c] + deltas[d][c + 3])
                    m = coefs[x, y, 3 + d] * (deltas[d][c] - deltas[d][c + 3])
                    plus = p if plus is None else plus + p
                    minus = m if minus is None else minus + m
                da.append(plus + minus)
                dc.append(plus - minus)
            j = [(dy[5] - dz[4]) * 0.5, (dz[3] - dx[5]) * 0.5, (dx[4] - dy[3]) * 0.5]
            drives = da + dc
            if y == 0:
                for c in range(6):
                    drive_ref[q, x, c] = drives[c]
                    field_ref[q, x, c] = f[c]
                for c in range(3):
                    drive_ref[q, x, 6 + c] = j[c]
            else:
                turn = [coefs[x, y, 6 + d] * -0.5 for d in range(3)]
                left, right = (f + j, drives + cross(turn, f[3:6]))
                if y == last:
                    left += [j[c] for c, _ in LAST_PAIRS]
                    right += [f[3 + c] for _, c in LAST_PAIRS]
                for a, b in zip(left, right):
                    set_row(s, sr, entry, a)
                    set_row(s, sd, entry, b)
                    entry += 1
            behind, here = (here, ahead)
            between(y * n + x, held)


def local_kernel(s, n_band, place, x_hbm, coefs, rt, dt, drive_ref, field_ref, x_ref, sems, matrix, *rest):
    n = s.inner
    z_refs, pads = (rest[:2], rest[2:])

    def fetch(q):
        return pltpu.make_async_copy(x_hbm.at[q], x_ref.at[q], sems.at[q])

    for q in range(s.bands):
        fetch(q).start()
    matrix[...] = shift_matrix()
    used = local_depth(s)
    for ref in pads:
        tail = ref.shape[0] - used * s.pitch
        ref[pl.ds(used * s.pitch, tail), :] = jnp.zeros((tail, LANES), F32)

    def shifted(z_ref, q, y):
        values = [row(x_ref, s, q, c, x + 1, y) for x in range(n) for c in range(6)]
        for i, value in enumerate(z_differences(s, values, matrix[...])):
            z_ref[y, i // 6, i % 6] = value

    def turn(sr, sd, q, tiles):
        for zt in tiles:
            put(s, rt, zt, slot_of(s, place, q, n_band), transposed(s, sr, zt))
            put(s, dt, zt, q, transposed(s, sd, zt))

    def pair(p, carry):
        for k in range(2):
            q = 2 * p + k
            other = pads[2 - 2 * k : 4 - 2 * k]
            behind = lax.rem(q + s.bands - 1, s.bands)
            ahead = lax.rem(q + 1, s.bands)

            @pl.when(q + 1 < s.bands)
            def _():
                fetch(ahead).wait()

            def before(y):
                shifted(z_refs[1 - k], ahead, y)

            def begin(step):
                steps = s.rows * n
                items = range(step * 2 * s.tiles // steps, (step + 1) * 2 * s.tiles // steps if used else 0)
                return [(item, transposed(s, other[item % 2], item // 2)) for item in items]

            def between(step, held):
                for item, block in held:
                    if item % 2:
                        put(s, dt, item // 2, behind, block)
                    else:
                        put(s, rt, item // 2, slot_of(s, place, behind, n_band), block)

            local_band(s, q, z_refs[k], x_ref, coefs, drive_ref, field_ref, *pads[2 * k : 2 * k + 2], before, begin, between)
        return carry

    fetch(0).wait()
    for y in range(s.rows):
        shifted(z_refs[0], 0, y)
    lax.fori_loop(0, s.bands // 2, pair, 0)
    if used:
        turn(*pads[2:4], s.bands - 1, range(s.tiles))
    else:
        rt[...] = jnp.zeros_like(rt)
        dt[...] = jnp.zeros_like(dt)


def factor_kernel(s, above_ref, factors, held):
    n = s.inner
    for entry in range(LANES):
        x, i = divmod(entry - (s.rows - 2) * n * 9, 13)
        value = jnp.ones((s.tiles, LANES), F32)
        if 0 <= x < n and i >= 9:
            value = above_ref[(i - 9) // 2 * n + x] * (-0.25, 0.25, 0.25, -0.25)[i - 9]
        set_row(s, held, entry, value)
    for zt in range(s.tiles):
        factors[zt] = transposed(s, held, zt).reshape(LANES // GROUP, GROUP, LANES)


def halo_pair(s, up_ref, index):
    rows = []
    for p in range(s.inner // 2):
        both = up_ref[index * (s.inner // 2) + p].astype(F32)
        rows += [both[: s.tiles], both[s.tiles :]]
    return rows


def boundary_kernel(s, n_band, scale, place, local_rt, local_dt, drive_ref, field_ref, coefs, down_ref, up_ref, above_ref, factors, send_ref, rt, dt, tots, *pads):
    n = s.inner
    half = LANES // 2
    zero = jnp.zeros((s.tiles, LANES), F32)
    kinds = (1, 4, 3, 5)

    def add(q, totals):
        rows = sum([halo_pair(s, up_ref, q * s.comps + c) for c in kinds], [])
        return [t + r for t, r in zip(totals, rows)]

    totals = lax.fori_loop(0, s.bands, add, [zero] * (4 * n))
    behinds = [halo_pair(s, up_ref, s.bands * s.comps + c) for c in range(3)]
    for x in range(n):
        vy, my, bx, bz = (totals[k * n + x] for k in range(4))
        tots[x, 0] = coefs[x, 0, 1]
        tots[x, 1] = coefs[x, 0, 4]
        tots[x, 2] = (vy - my) * -0.25
        tots[x, 3] = (vy + my) * -0.25
        j = [coefs[x, 0, 6] - bz * 0.5, coefs[x, 0, 7], coefs[x, 0, 8] + bx * 0.5]
        if s.rows == 1:
            j = [j[0] + above_ref[n + x] * 0.5, j[1], j[2] - above_ref[x] * 0.5]
        behind = [behinds[0][x] + down_ref[n + x] * 0.5, behinds[1][x], behinds[2][x] - down_ref[x] * 0.5]
        for c in range(3):
            tots[x, 4 + c] = j[c] * -0.5
            tots[x, 7 + c] = behind[c] * -0.5
    used = n * 15
    for ref in pads:
        tail = (half - used) * s.pitch
        ref[pl.ds(used * s.pitch, tail), :] = jnp.zeros((tail, LANES), F32)

    def turned(source, t):
        both = [source[pl.ds(2 * t + k, half, stride=s.pitch), :] for k in range(2)]
        return jnp.concatenate(both, 0).astype(BF16).T

    def turn(sr, sd, q, pairs):
        for t in pairs:
            put(s, rt, t, slot_of(s, place, q, n_band), turned(sr, t))
            put(s, dt, t, q, turned(sd, t))

    def band(q, sr, sd, begin, between):
        entry = 0
        h_all = [halo_pair(s, up_ref, q * s.comps + c) for c in range(6)]
        for x in range(n):
            held = begin(x)
            f = [field_ref[q, x, c] for c in range(6)]
            h = [h_all[c][x] for c in range(6)]
            da, dc, ea, ec = ([], [], [], [])
            for c in range(3):
                p = tots[x, 0] * (h[c] + h[c + 3])
                m = tots[x, 1] * (h[c] - h[c + 3])
                da.append(drive_ref[q, x, c] - (p + m))
                dc.append(drive_ref[q, x, 3 + c] - (p - m))
                p = tots[x, 2] * (f[c] + f[c + 3])
                m = tots[x, 3] * (f[c] - f[c + 3])
                ea.append(p + m)
                ec.append(p - m)
            behind = cross([tots[x, 7 + c] for c in range(3)], h[3:6])
            dc[0] = dc[0] - behind[2] * 0.5
            dc[2] = dc[2] + behind[0] * 0.5
            j = [drive_ref[q, x, 6] - h[5] * 0.5, drive_ref[q, x, 7], drive_ref[q, x, 8] + h[3] * 0.5]
            left = f + j + h
            right = da + dc + cross([tots[x, 4 + c] for c in range(3)], f[3:6]) + ea + ec
            for a, b in zip(left, right):
                set_row(s, sr, entry, a)
                set_row(s, sd, entry, b)
                entry += 1
            between(held)

    def pair(p, carry):
        for k in range(2):
            q = 2 * p + k
            before = lax.rem(q + s.bands - 1, s.bands)
            other = pads[2 - 2 * k : 4 - 2 * k]

            def begin(x):
                return [(t, turned(other[0], t), turned(other[1], t)) for t in range(x * steps // n, (x + 1) * steps // n)]

            def between(held):
                for t, left, right in held:
                    put(s, rt, t, slot_of(s, place, before, n_band), left)
                    put(s, dt, t, before, right)

            band(q, *pads[2 * k : 2 * k + 2], begin, between)
        return carry

    steps = s.tiles // 2
    lax.fori_loop(0, s.bands // 2, pair, 0)
    turn(*pads[2:4], s.bands - 1, range(steps))
    products(s, n_band, scale, 1, place, local_rt, local_dt, rt, dt, factors, send_ref)


def products(s, n_band, scale, core, place, local_rt, local_dt, rt, dt, factors, out_ref):
    wide = s.bands * GROUP
    half = LANES // 2
    share = s.bands // n_band
    lane = lax.broadcasted_iota(jnp.int32, (wide, LANES), 1)
    wanted = (lane >= half) == ((core ^ place[1]) % 2 == 1)

    def tile(r, carry):
        zt = (r * 2 + core) ^ place[1]
        parts = []
        for g in range(LANES // GROUP):
            left = rt[zt // 2, g].reshape(wide, LANES)
            left = jnp.where(wanted, left, jnp.zeros_like(left))
            right = dt[zt // 2, g].reshape(wide, LANES)
            if s.rows > 1:
                scaled = local_rt[zt, g] * factors[zt, g][None]
                left = jnp.concatenate([scaled.reshape(wide, -1), left], 1)
                right = jnp.concatenate([local_dt[zt, g].reshape(wide, -1), right], 1)
            parts.append(diagonal_products(s, left, right) * scale)
        for b in range(n_band):
            block = jnp.concatenate([p[b * share : (b + 1) * share] for p in parts], 0)
            out_ref[r, b] = block.astype(out_ref.dtype)
        return carry

    lax.fori_loop(0, s.tiles // 2, tile, 0, unroll=4)


def farthest_first(size):
    return sorted(range(1, size), key=lambda d: (-d.bit_count(), d))


def exchange(value, distance, size):
    return lax.ppermute(value, AXES, [(i, i ^ distance) for i in range(size)])


def body(band_fields):
    s = Sizes(band_fields.shape)
    n_band, n_slab = (lax.axis_size("band"), lax.axis_size("slab"))
    devices = n_band * n_slab
    n, tiles, rows = (s.inner, s.tiles, s.rows)
    x = band_fields.reshape(s.bands, s.comps, s.planes, rows, tiles, LANES)
    x = x.transpose(0, 1, 2, 4, 3, 5).reshape(s.bands, s.comps, s.planes, tiles * rows, LANES)
    place = jnp.stack([lax.axis_index("band"), lax.axis_index("slab")]).astype(jnp.int32)

    def vector(*lead):
        return jax.ShapeDtypeStruct(lead + (tiles, LANES), F32)

    depth = -(-(max(local_depth(s), 1)) // LANES) * LANES
    groups = LANES // GROUP
    wide = s.bands * GROUP
    share = s.bands // n_band
    rows_up = (s.bands * s.comps + 3) * (n // 2)

    up, down, coefs = pl.pallas_call(
        lambda *refs: edge_kernel(s, *refs),
        out_shape=(jax.ShapeDtypeStruct((rows_up, 2 * tiles, LANES), BF16), vector(2 * n), vector(n, rows, 9)),
        in_specs=[HBM],
        out_specs=(VMEM,) * 3,
        scratch_shapes=[pltpu.VMEM(x.shape, F32), pltpu.VMEM((s.comps, s.planes, rows, tiles, LANES), F32), pltpu.SemaphoreType.DMA((s.bands, 2))],
        compiler_params=EDGE,
    )(x)
    step = [(i, (i + 1) % devices) for i in range(devices)]
    from_below = lax.ppermute(up, AXES, step)
    from_above = lax.ppermute(down, AXES, [(j, i) for i, j in step])

    turned = jax.ShapeDtypeStruct((tiles, groups, s.bands, GROUP, depth), BF16)
    local_rt, local_dt, drive, field = pl.pallas_call(
        lambda *refs: local_kernel(s, n_band, *refs),
        out_shape=(turned, turned, vector(s.bands, n, 9), vector(s.bands, n, 6)),
        in_specs=[SMEM, HBM, VMEM],
        out_specs=(VMEM,) * 4,
        scratch_shapes=[pltpu.VMEM(x.shape, F32), pltpu.SemaphoreType.DMA((s.bands,)), pltpu.VMEM((2 * LANES, 2 * LANES), BF16)]
        + [pltpu.VMEM((rows, n, 6, tiles, LANES), F32)] * 2
        + [pltpu.VMEM((depth * s.pitch, LANES), F32)] * 4,
        compiler_params=LOCAL,
        cost_estimate=pl.CostEstimate(flops=2 * 10**9, bytes_accessed=2 * 10**7, transcendentals=0),
    )(place, x, coefs)
    if rows == 1:
        two = lax.ppermute(down, AXES, [(i, (i + 2) % devices) for i in range(devices)])
        two = two.reshape(2, n // 2, 2 * tiles, LANES) * 0.5
        base = s.bands * s.comps * (n // 2)
        behind = from_below[base:].astype(F32).reshape(3, n // 2, 2 * tiles, LANES)
        behind = jnp.stack([behind[0] - two[1], behind[1], behind[2] + two[0]])
        behind = behind.reshape(3 * (n // 2), 2 * tiles, LANES).astype(BF16)
        from_below = jnp.concatenate([from_below[:base], behind], 0)

    shape = (tiles // 2, n_band, groups * share, wide)
    scale = 1.0 / (n * rows * devices)
    blocks = jax.ShapeDtypeStruct((tiles // 2, groups, s.bands, GROUP, LANES), BF16)
    factors = pl.pallas_call(
        lambda *refs: factor_kernel(s, *refs),
        out_shape=jax.ShapeDtypeStruct((tiles, groups, GROUP, LANES), BF16),
        in_specs=[VMEM],
        out_specs=VMEM,
        scratch_shapes=[pltpu.VMEM((LANES * s.pitch, LANES), F32)],
        compiler_params=BOUNDARY,
    )(from_above)
    send, rt, dt = pl.pallas_call(
        lambda *refs: boundary_kernel(s, n_band, scale, *refs),
        out_shape=(jax.ShapeDtypeStruct(shape, BF16), blocks, blocks),
        in_specs=[SMEM] + [VMEM] * 9,
        out_specs=(VMEM,) * 3,
        scratch_shapes=[pltpu.VMEM((n, 10, tiles, LANES), F32)] + [pltpu.VMEM((LANES // 2 * s.pitch, LANES), F32)] * 4,
        compiler_params=BOUNDARY,
    )(place, local_rt, local_dt, drive, field, coefs, down, from_below, from_above, factors)
    arrived = exchange(send, 1, devices)
    keep = pl.pallas_call(
        lambda place, *refs: products(s, n_band, scale, 0, place, *refs),
        out_shape=jax.ShapeDtypeStruct(shape, F32),
        in_specs=[SMEM] + [VMEM] * 5,
        out_specs=VMEM,
        compiler_params=BOUNDARY,
        cost_estimate=pl.CostEstimate(flops=2 * 10**9, bytes_accessed=2 * 10**7, transcendentals=0),
    )(place, local_rt, local_dt, rt, dt, factors)

    value = keep + arrived.astype(F32)
    parts = [exchange(value[:, d].astype(BF16), d * n_slab, devices) for d in farthest_first(n_band)]
    value = sum([p.astype(F32) for p in parts], value[:, 0])
    parts = [exchange(value[e].astype(BF16), 2 * e, devices) for e in range(1, tiles // 2)]
    value = sum([p.astype(F32) for p in parts], value[0])
    value = value.reshape(groups, share, s.bands, GROUP).transpose(1, 2, 0, 3)
    return value.reshape(share, s.bands, groups * GROUP)


def solution(mesh):
    return jax.shard_map(
        body,
        mesh=mesh,
        in_specs=(P(None, None, None, AXES, None),),
        out_specs=P("band", None, "slab"),
        check_vma=False,
    )
```

```python
import jax
import jax.numpy as jnp
from jax import lax
from jax.experimental import pallas as pl
from jax.experimental.pallas import tpu as pltpu
from jax.sharding import PartitionSpec as P

AXES = ("band", "slab")
LANES = 128
GROUP = 16
SUBLANES = 8
F32 = jnp.float32
BF16 = jnp.bfloat16
VMEM = pl.BlockSpec(memory_space=pltpu.VMEM)
SMEM = pl.BlockSpec(memory_space=pltpu.SMEM)
HBM = pl.BlockSpec(memory_space=pltpu.HBM)
EDGE = pltpu.CompilerParams(vmem_limit_bytes=50 * 2**20)
LOCAL = pltpu.CompilerParams(vmem_limit_bytes=38 * 2**20)
BOUNDARY = pltpu.CompilerParams(vmem_limit_bytes=32 * 2**20)


class Sizes:
    def __init__(self, shape):
        self.bands, self.comps, self.planes, self.rows, cells = shape
        self.inner = self.planes - 2
        self.tiles = cells // LANES
        self.pitch = self.tiles + 1


TOTALS = (1, 4, 3, 5)


def row(ref, s, q, c, x, y):
    if s.rows == 1:
        return ref[q, c, x]
    return ref[q, c, x, pl.ds(y, s.tiles, stride=s.rows), :]


def z_difference(value):
    tiles = value.shape[0]
    lane = lax.broadcasted_iota(jnp.int32, value.shape, 1)
    left = pltpu.roll(value, LANES - 1, 1)
    right = pltpu.roll(value, 1, 1)
    after = jnp.where(lane == LANES - 1, pltpu.roll(left, tiles - 1, 0), left)
    before = jnp.where(lane == 0, pltpu.roll(right, 1, 0), right)
    return after - before


def edge_kernel(s, x_hbm, up_ref, rest_ref, down_ref, coefs, x_ref, sums, sems):
    last = s.rows - 1
    n = s.inner
    whole, inside = (pl.ds(4, 2), pl.ds(0, 4))
    copies = []
    for q in range(s.bands):
        copies.append(pltpu.make_async_copy(x_hbm.at[q, whole], x_ref.at[q, whole], sems.at[q, 0]))
        part = (q, inside, pl.ds(1, n))
        copies.append(pltpu.make_async_copy(x_hbm.at[part], x_ref.at[part], sems.at[q, 1]))
    for copy in copies:
        copy.start()

    def pack(first, count):
        target, start = (up_ref, 0) if first < s.bands // 2 else (rest_ref, s.bands // 2)

        def band(q, carry):
            for c in range(s.comps):
                for p in range(n // 2):
                    pair = [row(x_ref, s, q, c, 1 + 2 * p + k, last) for k in range(2)]
                    target[((q - start) * s.comps + c) * (n // 2) + p] = jnp.concatenate(pair, 0).astype(BF16)
            return carry

        lax.fori_loop(first, first + count, band, 0)

    def total_of(first, count, c, x):
        for y in range(s.rows):
            total = row(x_ref, s, first, c, x, y)
            for q in range(first + 1, first + count):
                total = total + row(x_ref, s, q, c, x, y)
            if first:
                total = total + sums[c, x, y]
            sums[c, x, y] = total

    def add(first, count):
        def one(j, carry):
            c, x = (j // n, j % n + 1)
            total_of(first, count, c, x)
            return carry

        lax.fori_loop(0, s.comps * n, one, 0)
        for c in (4, 5):
            for x in (0, s.planes - 1):
                total_of(first, count, c, x)

    share = s.bands // 4
    for first in range(0, s.bands, share):
        for copy in copies[2 * first : 2 * (first + share)]:
            copy.wait()
        pack(first, share)
        add(first, share)
    extras = [[], [], []] + [[sums[c, x + 1, last] for x in range(n)] for c in TOTALS]
    for x in range(n):
        down_ref[x] = sums[3, x + 1, 0]
        down_ref[n + x] = sums[5, x + 1, 0]
        for y in range(s.rows):
            v = [sums[c, x + 1, y] for c in range(3)]
            b = [sums[c, x + 1, y] for c in range(3, 6)]

            def dy(c):
                high = sums[c, x + 1, y + 1] if y + 1 < s.rows else 0.0
                low = sums[c, x + 1, y - 1] if y else 0.0
                return high - low

            def dx(c):
                return sums[c, x + 2, y] - sums[c, x, y]

            j = [dy(5) - z_difference(b[1]), z_difference(b[0]) - dx(5), dx(4) - dy(3)]
            j = [value * 0.5 for value in j]
            for d in range(3):
                coefs[x, y, d] = (v[d] - b[d]) * -0.25
                coefs[x, y, 3 + d] = (v[d] + b[d]) * -0.25
                coefs[x, y, 6 + d] = j[d]
                if y == last:
                    extras[d].append(j[d])
    base = s.bands // 2 * s.comps * (n // 2)
    for c, values in enumerate(extras):
        for p in range(n // 2):
            up_ref[base + c * (n // 2) + p] = jnp.concatenate(values[2 * p : 2 * p + 2], 0).astype(BF16)


def transposed(s, source, zt):
    depth = source.shape[0] // s.pitch
    return source[pl.ds(zt, depth, stride=s.pitch), :].astype(BF16).T


def put(s, target, zt, slot, block):
    target[zt, :, slot] = block.reshape(LANES // GROUP, GROUP, block.shape[-1])


def diagonal_products(s, left, right):
    wide = s.bands * GROUP
    full = lax.dot_general(left, right, (((1,), (1,)), ((), ())), preferred_element_type=F32)
    lane = lax.broadcasted_iota(jnp.int32, (SUBLANES, wide), 1)
    sublane = lax.broadcasted_iota(jnp.int32, (SUBLANES, wide), 0)
    upper = lane % GROUP >= SUBLANES
    skew = (sublane - lane) % SUBLANES
    blocks = []
    for first in range(0, s.bands, SUBLANES):
        mixed = None
        for k in range(SUBLANES):
            top = (first + k) * GROUP
            part = jnp.where(upper, full[top + SUBLANES : top + GROUP], full[top : top + SUBLANES])
            part = pltpu.roll(part, k, 0) if k else part
            mixed = part if mixed is None else jnp.where(skew == k, part, mixed)
        for bit in (1, 2, 4):
            mixed = jnp.where((lane & bit) != 0, pltpu.roll(mixed, SUBLANES - bit, 0), mixed)
        blocks.append(mixed)
    return jnp.concatenate(blocks, 0)


def cross(a, b):
    return [a[1] * b[2] - a[2] * b[1], a[2] * b[0] - a[0] * b[2], a[0] * b[1] - a[1] * b[0]]


LAST_PAIRS = ((0, 1), (1, 0), (1, 2), (2, 1))


def local_depth(s):
    return (s.rows - 1) * s.inner * 9 + 4 * s.inner if s.rows > 1 else 0


def set_row(s, ref, entry, value):
    ref[pl.ds(entry * s.pitch, s.tiles), :] = value


def shift_matrix():
    source = lax.broadcasted_iota(jnp.int32, (2 * LANES, 2 * LANES), 0) % LANES
    target = lax.broadcasted_iota(jnp.int32, (2 * LANES, 2 * LANES), 1)
    inside = jnp.where(source == target + 1, 1.0, jnp.where(source == target - 1, -1.0, 0.0))
    carry_up = (target == 2 * LANES - 1) & (source == 0)
    carry_down = (target == LANES) & (source == LANES - 1)
    across = jnp.where(carry_up, 1.0, jnp.where(carry_down, -1.0, 0.0))
    return jnp.where(target < LANES, inside, across).astype(BF16)


def z_differences(s, values, matrix):
    rows = jnp.concatenate(values, 0)
    high = rows.astype(BF16)
    low = (rows - high.astype(F32)).astype(BF16)
    both = jnp.dot(jnp.concatenate([high, low], 1), matrix, preferred_element_type=F32)
    lane = lax.broadcasted_iota(jnp.int32, (s.tiles, LANES), 1)
    out = []
    for i in range(len(values)):
        part = both[i * s.tiles : (i + 1) * s.tiles]
        across = part[:, LANES:]
        across = jnp.where(lane < LANES // 2, pltpu.roll(across, 1, 0), pltpu.roll(across, s.tiles - 1, 0))
        out.append(part[:, :LANES] + across)
    return out


def local_band(s, q, z_ref, x_ref, coefs, drive_ref, field_ref, sr, sd, before, begin, between):
    n, last = (s.inner, s.rows - 1)
    entry = 0
    for y in range(s.rows):
        before(y)
        behind, here = ([row(x_ref, s, q, c, x, y) for c in range(6)] for x in range(2))
        for x in range(n):
            held = begin(y * n + x)
            ahead = [row(x_ref, s, q, c, x + 2, y) for c in range(6)]
            f = here
            dx = [p - m for p, m in zip(ahead, behind)]
            dy, dz = ([], [z_ref[y, x, c] for c in range(6)])
            for c in range(6):
                high = row(x_ref, s, q, c, x + 1, y + 1) if y < last else None
                low = row(x_ref, s, q, c, x + 1, y - 1) if y else None
                if high is None:
                    dy.append(jnp.zeros_like(f[0]) if low is None else -low)
                else:
                    dy.append(high if low is None else high - low)
            deltas = (dx, dy, dz)
            da, dc = ([], [])
            for c in range(3):
                plus = minus = None
                for d in range(3):
                    p = coefs[x, y, d] * (deltas[d][c] + deltas[d][c + 3])
                    m = coefs[x, y, 3 + d] * (deltas[d][c] - deltas[d][c + 3])
                    plus = p if plus is None else plus + p
                    minus = m if minus is None else minus + m
                da.append(plus + minus)
                dc.append(plus - minus)
            j = [(dy[5] - dz[4]) * 0.5, (dz[3] - dx[5]) * 0.5, (dx[4] - dy[3]) * 0.5]
            drives = da + dc
            if y == 0:
                for c in range(6):
                    drive_ref[q, x, c] = drives[c]
                    field_ref[q, x, c] = f[c]
                for c in range(3):
                    drive_ref[q, x, 6 + c] = j[c]
            else:
                turn = [coefs[x, y, 6 + d] * -0.5 for d in range(3)]
                left, right = (f + j, drives + cross(turn, f[3:6]))
                if y == last:
                    left += [j[c] for c, _ in LAST_PAIRS]
                    right += [f[3 + c] for _, c in LAST_PAIRS]
                for a, b in zip(left, right):
                    set_row(s, sr, entry, a)
                    set_row(s, sd, entry, b)
                    entry += 1
            behind, here = (here, ahead)
            between(y * n + x, held)


def local_kernel(s, x_hbm, coefs, rt, dt, drive_ref, field_ref, x_ref, sems, matrix, *rest):
    n = s.inner
    z_refs, pads = (rest[:2], rest[2:])

    def fetch(q):
        return pltpu.make_async_copy(x_hbm.at[q], x_ref.at[q], sems.at[q])

    for q in range(s.bands):
        fetch(q).start()
    matrix[...] = shift_matrix()
    used = local_depth(s)
    for ref in pads:
        tail = ref.shape[0] - used * s.pitch
        ref[pl.ds(used * s.pitch, tail), :] = jnp.zeros((tail, LANES), F32)

    def shifted(z_ref, q, y):
        values = [row(x_ref, s, q, c, x + 1, y) for x in range(n) for c in range(6)]
        for i, value in enumerate(z_differences(s, values, matrix[...])):
            z_ref[y, i // 6, i % 6] = value

    def turn(sr, sd, q, tiles):
        for zt in tiles:
            put(s, rt, zt, q, transposed(s, sr, zt))
            put(s, dt, zt, q, transposed(s, sd, zt))

    def pair(p, carry):
        for k in range(2):
            q = 2 * p + k
            other = pads[2 - 2 * k : 4 - 2 * k]
            behind = lax.rem(q + s.bands - 1, s.bands)
            ahead = lax.rem(q + 1, s.bands)

            @pl.when(q + 1 < s.bands)
            def _():
                fetch(ahead).wait()

            def before(y):
                shifted(z_refs[1 - k], ahead, y)

            def begin(step):
                steps = s.rows * n
                items = range(step * 2 * s.tiles // steps, (step + 1) * 2 * s.tiles // steps if used else 0)
                return [(item, transposed(s, other[item % 2], item // 2)) for item in items]

            def between(step, held):
                for item, block in held:
                    if item % 2:
                        put(s, dt, item // 2, behind, block)
                    else:
                        put(s, rt, item // 2, behind, block)

            local_band(s, q, z_refs[k], x_ref, coefs, drive_ref, field_ref, *pads[2 * k : 2 * k + 2], before, begin, between)
        return carry

    fetch(0).wait()
    for y in range(s.rows):
        shifted(z_refs[0], 0, y)
    lax.fori_loop(0, s.bands // 2, pair, 0)
    if used:
        turn(*pads[2:4], s.bands - 1, range(s.tiles))
    else:
        rt[...] = jnp.zeros_like(rt)
        dt[...] = jnp.zeros_like(dt)


def factor_kernel(s, above_ref, factors, held):
    n = s.inner
    for entry in range(LANES):
        x, i = divmod(entry - (s.rows - 2) * n * 9, 13)
        value = jnp.ones((s.tiles, LANES), F32)
        if 0 <= x < n and i >= 9:
            value = above_ref[(i - 9) // 2 * n + x] * (-0.25, 0.25, 0.25, -0.25)[i - 9]
        set_row(s, held, entry, value)
    for zt in range(s.tiles):
        factors[zt] = transposed(s, held, zt).reshape(LANES // GROUP, GROUP, LANES)


def halo_pair(s, up_ref, index):
    rows = []
    for p in range(s.inner // 2):
        both = up_ref[index * (s.inner // 2) + p].astype(F32)
        rows += [both[: s.tiles], both[s.tiles :]]
    return rows


def first_kernel(s, drive_ref, field_ref, coefs, down_ref, up_ref, above_ref, rt, dt, tots, *pads):
    n = s.inner
    base = s.bands // 2 * s.comps
    behinds = [halo_pair(s, up_ref, base + c) for c in range(3)]
    totals = [halo_pair(s, up_ref, base + 3 + k) for k in range(len(TOTALS))]
    for x in range(n):
        vy, my, bx, bz = (total[x] for total in totals)
        tots[x, 0] = coefs[x, 0, 1]
        tots[x, 1] = coefs[x, 0, 4]
        tots[x, 2] = (vy - my) * -0.25
        tots[x, 3] = (vy + my) * -0.25
        j = [coefs[x, 0, 6] - bz * 0.5, coefs[x, 0, 7], coefs[x, 0, 8] + bx * 0.5]
        if s.rows == 1:
            j = [j[0] + above_ref[n + x] * 0.5, j[1], j[2] - above_ref[x] * 0.5]
        behind = [behinds[0][x] + down_ref[n + x] * 0.5, behinds[1][x], behinds[2][x] - down_ref[x] * 0.5]
        for c in range(3):
            tots[x, 4 + c] = j[c] * -0.5
            tots[x, 7 + c] = behind[c] * -0.5
    boundary_bands(s, 0, drive_ref, field_ref, up_ref, tots, rt, dt, pads)


def second_kernel(s, n_band, scale, place, local_rt, local_dt, drive_ref, field_ref, up_ref, tots, factors, rt_0, dt_0, send_ref, rt, dt, *pads):
    boundary_bands(s, s.bands // 2, drive_ref, field_ref, up_ref, tots, rt, dt, pads)
    products(s, n_band, scale, 1, place, local_rt, local_dt, factors, rt_0, dt_0, rt, dt, send_ref)


def boundary_bands(s, first, drive_ref, field_ref, up_ref, tots, rt, dt, pads):
    n = s.inner
    count = s.bands // 2
    half = LANES // 2
    used = n * 15
    for ref in pads:
        tail = (half - used) * s.pitch
        ref[pl.ds(used * s.pitch, tail), :] = jnp.zeros((tail, LANES), F32)

    def turned(source, t):
        both = [source[pl.ds(2 * t + k, half, stride=s.pitch), :] for k in range(2)]
        return jnp.concatenate(both, 0).astype(BF16).T

    def turn(sr, sd, q, pairs):
        for t in pairs:
            put(s, rt, t, q, turned(sr, t))
            put(s, dt, t, q, turned(sd, t))

    def band(q, sr, sd, begin, between):
        entry = 0
        h_all = [halo_pair(s, up_ref, q * s.comps + c) for c in range(6)]
        k = first + q
        for x in range(n):
            held = begin(x)
            f = [field_ref[k, x, c] for c in range(6)]
            h = [h_all[c][x] for c in range(6)]
            da, dc, ea, ec = ([], [], [], [])
            for c in range(3):
                p = tots[x, 0] * (h[c] + h[c + 3])
                m = tots[x, 1] * (h[c] - h[c + 3])
                da.append(drive_ref[k, x, c] - (p + m))
                dc.append(drive_ref[k, x, 3 + c] - (p - m))
                p = tots[x, 2] * (f[c] + f[c + 3])
                m = tots[x, 3] * (f[c] - f[c + 3])
                ea.append(p + m)
                ec.append(p - m)
            behind = cross([tots[x, 7 + c] for c in range(3)], h[3:6])
            dc[0] = dc[0] - behind[2] * 0.5
            dc[2] = dc[2] + behind[0] * 0.5
            j = [drive_ref[k, x, 6] - h[5] * 0.5, drive_ref[k, x, 7], drive_ref[k, x, 8] + h[3] * 0.5]
            left = f + j + h
            right = da + dc + cross([tots[x, 4 + c] for c in range(3)], f[3:6]) + ea + ec
            for a, b in zip(left, right):
                set_row(s, sr, entry, a)
                set_row(s, sd, entry, b)
                entry += 1
            between(held)

    def pair(p, carry):
        for k in range(2):
            q = 2 * p + k
            before = lax.rem(q + count - 1, count)
            other = pads[2 - 2 * k : 4 - 2 * k]

            def begin(x):
                return [(t, turned(other[0], t), turned(other[1], t)) for t in range(x * steps // n, (x + 1) * steps // n)]

            def between(held):
                for t, left, right in held:
                    put(s, rt, t, before, left)
                    put(s, dt, t, before, right)

            band(q, *pads[2 * k : 2 * k + 2], begin, between)
        return carry

    steps = s.tiles // 2
    lax.fori_loop(0, count // 2, pair, 0)
    turn(*pads[2:4], count - 1, range(steps))


def products(s, n_band, scale, core, place, local_rt, local_dt, factors, rt_0, dt_0, rt_1, dt_1, out_ref):
    wide = s.bands * GROUP
    half = LANES // 2
    share = s.bands // n_band
    lane = lax.broadcasted_iota(jnp.int32, (wide, LANES), 1)
    wanted = (lane >= half) == ((core ^ place[1]) % 2 == 1)

    def tile(r, carry):
        zt = (r * 2 + core) ^ place[1]
        parts = []
        for g in range(LANES // GROUP):
            left = jnp.concatenate([ref[zt // 2, g].reshape(wide // 2, LANES) for ref in (rt_0, rt_1)], 0)
            left = jnp.where(wanted, left, jnp.zeros_like(left))
            right = jnp.concatenate([ref[zt // 2, g].reshape(wide // 2, LANES) for ref in (dt_0, dt_1)], 0)
            if s.rows > 1:
                scaled = local_rt[zt, g] * factors[zt, g][None]
                left = jnp.concatenate([scaled.reshape(wide, -1), left], 1)
                right = jnp.concatenate([local_dt[zt, g].reshape(wide, -1), right], 1)
            parts.append(diagonal_products(s, left, right) * scale)
        for b in range(n_band):
            block = jnp.concatenate([p[b * share : (b + 1) * share] for p in parts], 0)
            out_ref[r, b ^ place[0]] = block.astype(out_ref.dtype)
        return carry

    lax.fori_loop(0, s.tiles // 2, tile, 0, unroll=4)


def farthest_first(size):
    return sorted(range(1, size), key=lambda d: (-d.bit_count(), d))


def exchange(value, distance, size):
    return lax.ppermute(value, AXES, [(i, i ^ distance) for i in range(size)])


def body(band_fields):
    s = Sizes(band_fields.shape)
    n_band, n_slab = (lax.axis_size("band"), lax.axis_size("slab"))
    devices = n_band * n_slab
    n, tiles, rows = (s.inner, s.tiles, s.rows)
    x = band_fields.reshape(s.bands, s.comps, s.planes, rows, tiles, LANES)
    x = x.transpose(0, 1, 2, 4, 3, 5).reshape(s.bands, s.comps, s.planes, tiles * rows, LANES)
    place = jnp.stack([lax.axis_index("band"), lax.axis_index("slab")]).astype(jnp.int32)

    def vector(*lead):
        return jax.ShapeDtypeStruct(lead + (tiles, LANES), F32)

    depth = -(-(max(local_depth(s), 1)) // LANES) * LANES
    groups = LANES // GROUP
    wide = s.bands * GROUP
    share = s.bands // n_band
    rows_up = s.bands // 2 * s.comps * (n // 2)
    rows_first = rows_up + (3 + len(TOTALS)) * (n // 2)

    up, rest, down, coefs = pl.pallas_call(
        lambda *refs: edge_kernel(s, *refs),
        out_shape=tuple(jax.ShapeDtypeStruct((count, 2 * tiles, LANES), BF16) for count in (rows_first, rows_up)) + (vector(2 * n), vector(n, rows, 9)),
        in_specs=[HBM],
        out_specs=(VMEM,) * 4,
        scratch_shapes=[pltpu.VMEM(x.shape, F32), pltpu.VMEM((s.comps, s.planes, rows, tiles, LANES), F32), pltpu.SemaphoreType.DMA((s.bands, 2))],
        compiler_params=EDGE,
    )(x)
    step = [(i, (i + 1) % devices) for i in range(devices)]
    from_below = lax.ppermute(up, AXES, step)
    rest_below = lax.ppermute(rest, AXES, step)
    from_above = lax.ppermute(down, AXES, [(j, i) for i, j in step])

    turned = jax.ShapeDtypeStruct((tiles, groups, s.bands, GROUP, depth), BF16)
    local_rt, local_dt, drive, field = pl.pallas_call(
        lambda *refs: local_kernel(s, *refs),
        out_shape=(turned, turned, vector(s.bands, n, 9), vector(s.bands, n, 6)),
        in_specs=[HBM, VMEM],
        out_specs=(VMEM,) * 4,
        scratch_shapes=[pltpu.VMEM(x.shape, F32), pltpu.SemaphoreType.DMA((s.bands,)), pltpu.VMEM((2 * LANES, 2 * LANES), BF16)]
        + [pltpu.VMEM((rows, n, 6, tiles, LANES), F32)] * 2
        + [pltpu.VMEM((depth * s.pitch, LANES), F32)] * 4,
        compiler_params=LOCAL,
        cost_estimate=pl.CostEstimate(flops=2 * 10**9, bytes_accessed=2 * 10**7, transcendentals=0),
    )(x, coefs)
    if rows == 1:
        two = lax.ppermute(down, AXES, [(i, (i + 2) % devices) for i in range(devices)])
        two = two.reshape(2, n // 2, 2 * tiles, LANES) * 0.5
        base = rows_up
        end = base + 3 * (n // 2)
        behind = from_below[base:end].astype(F32).reshape(3, n // 2, 2 * tiles, LANES)
        behind = jnp.stack([behind[0] - two[1], behind[1], behind[2] + two[0]])
        behind = behind.reshape(3 * (n // 2), 2 * tiles, LANES).astype(BF16)
        from_below = jnp.concatenate([from_below[:base], behind, from_below[end:]], 0)

    shape = (tiles // 2, n_band, groups * share, wide)
    scale = 1.0 / (n * rows * devices)
    blocks = jax.ShapeDtypeStruct((tiles // 2, groups, s.bands // 2, GROUP, LANES), BF16)
    staging = [pltpu.VMEM((LANES // 2 * s.pitch, LANES), F32)] * 4
    factors = pl.pallas_call(
        lambda *refs: factor_kernel(s, *refs),
        out_shape=jax.ShapeDtypeStruct((tiles, groups, GROUP, LANES), BF16),
        in_specs=[VMEM],
        out_specs=VMEM,
        scratch_shapes=[pltpu.VMEM((LANES * s.pitch, LANES), F32)],
        compiler_params=BOUNDARY,
    )(from_above)
    rt_0, dt_0, tots = pl.pallas_call(
        lambda *refs: first_kernel(s, *refs),
        out_shape=(blocks, blocks, vector(n, 10)),
        in_specs=[VMEM] * 6,
        out_specs=(VMEM,) * 3,
        scratch_shapes=staging,
        compiler_params=BOUNDARY,
    )(drive, field, coefs, down, from_below, from_above)
    send, rt_1, dt_1 = pl.pallas_call(
        lambda *refs: second_kernel(s, n_band, scale, *refs),
        out_shape=(jax.ShapeDtypeStruct(shape, BF16), blocks, blocks),
        in_specs=[SMEM] + [VMEM] * 9,
        out_specs=(VMEM,) * 3,
        scratch_shapes=staging,
        compiler_params=BOUNDARY,
    )(place, local_rt, local_dt, drive, field, rest_below, tots, factors, rt_0, dt_0)
    arrived = exchange(send, 1, devices)
    keep = pl.pallas_call(
        lambda place, *refs: products(s, n_band, scale, 0, place, *refs),
        out_shape=jax.ShapeDtypeStruct(shape, F32),
        in_specs=[SMEM] + [VMEM] * 7,
        out_specs=VMEM,
        compiler_params=BOUNDARY,
        cost_estimate=pl.CostEstimate(flops=2 * 10**9, bytes_accessed=2 * 10**7, transcendentals=0),
    )(place, local_rt, local_dt, factors, rt_0, dt_0, rt_1, dt_1)

    value = keep + arrived.astype(F32)
    parts = [exchange(value[:, d].astype(BF16), d * n_slab, devices) for d in farthest_first(n_band)]
    value = sum([p.astype(F32) for p in parts], value[:, 0])
    parts = [exchange(value[e].astype(BF16), 2 * e, devices) for e in range(1, tiles // 2)]
    value = sum([p.astype(F32) for p in parts], value[0])
    value = value.reshape(groups, share, s.bands, GROUP).transpose(1, 2, 0, 3)
    return value.reshape(share, s.bands, groups * GROUP)


def solution(mesh):
    return jax.shard_map(
        body,
        mesh=mesh,
        in_specs=(P(None, None, None, AXES, None),),
        out_specs=P("band", None, "slab"),
        check_vma=False,
    )
```

```python
import jax
import jax.numpy as jnp
from jax import lax
from jax.experimental import pallas as pl
from jax.experimental.pallas import tpu as pltpu
from jax.sharding import PartitionSpec as P

AXES = ("band", "slab")
LANES = 128
GROUP = 16
SUBLANES = 8
F32 = jnp.float32
BF16 = jnp.bfloat16
VMEM = pl.BlockSpec(memory_space=pltpu.VMEM)
SMEM = pl.BlockSpec(memory_space=pltpu.SMEM)
HBM = pl.BlockSpec(memory_space=pltpu.HBM)
EDGE = pltpu.CompilerParams(vmem_limit_bytes=50 * 2**20)
LOCAL = pltpu.CompilerParams(vmem_limit_bytes=38 * 2**20)
BOUNDARY = pltpu.CompilerParams(vmem_limit_bytes=32 * 2**20)


class Sizes:
    def __init__(self, shape):
        self.bands, self.comps, self.planes, self.rows, cells = shape
        self.inner = self.planes - 2
        self.tiles = cells // LANES
        self.first = self.bands // 2
        self.pitch = self.tiles + 1


TOTALS = (1, 4, 3, 5)


def row(ref, s, q, c, x, y):
    if s.rows == 1:
        return ref[q, c, x]
    return ref[q, c, x, pl.ds(y, s.tiles, stride=s.rows), :]


def z_difference(value):
    tiles = value.shape[0]
    lane = lax.broadcasted_iota(jnp.int32, value.shape, 1)
    left = pltpu.roll(value, LANES - 1, 1)
    right = pltpu.roll(value, 1, 1)
    after = jnp.where(lane == LANES - 1, pltpu.roll(left, tiles - 1, 0), left)
    before = jnp.where(lane == 0, pltpu.roll(right, 1, 0), right)
    return after - before


def edge_kernel(s, x_hbm, up_ref, rest_ref, down_ref, sent_ref, coefs, x_ref, sums, sems):
    last = s.rows - 1
    n = s.inner
    whole, inside = (pl.ds(4, 2), pl.ds(0, 4))
    copies = []
    for q in range(s.bands):
        copies.append(pltpu.make_async_copy(x_hbm.at[q, whole], x_ref.at[q, whole], sems.at[q, 0]))
        part = (q, inside, pl.ds(1, n))
        copies.append(pltpu.make_async_copy(x_hbm.at[part], x_ref.at[part], sems.at[q, 1]))
    for copy in copies:
        copy.start()

    def pack(first, count):
        target, start = (up_ref, 0) if first < s.first else (rest_ref, s.first)

        def band(q, carry):
            for c in range(s.comps):
                for p in range(n // 2):
                    pair = [row(x_ref, s, q, c, 1 + 2 * p + k, last) for k in range(2)]
                    target[((q - start) * s.comps + c) * (n // 2) + p] = jnp.concatenate(pair, 0).astype(BF16)
            return carry

        lax.fori_loop(first, first + count, band, 0)

    def total_of(first, count, c, x):
        for y in range(s.rows):
            total = row(x_ref, s, first, c, x, y)
            for q in range(first + 1, first + count):
                total = total + row(x_ref, s, q, c, x, y)
            if first:
                total = total + sums[c, x, y]
            sums[c, x, y] = total

    def add(first, count):
        def one(j, carry):
            c, x = (j // n, j % n + 1)
            total_of(first, count, c, x)
            return carry

        lax.fori_loop(0, s.comps * n, one, 0)
        for c in (4, 5):
            for x in (0, s.planes - 1):
                total_of(first, count, c, x)

    share = s.bands // 4
    for first in range(0, s.bands, share):
        for copy in copies[2 * first : 2 * (first + share)]:
            copy.wait()
        pack(first, share)
        add(first, share)
    for i in range(2 * n // 2):
        c, x = (3 + 2 * (2 * i // n), 2 * i % n + 1)
        sent_ref[i] = jnp.concatenate([sums[c, x, 0], sums[c, x + 1, 0]], 0).astype(BF16)
    extras = [[], [], []] + [[sums[c, x + 1, last] for x in range(n)] for c in TOTALS]
    for x in range(n):
        down_ref[x] = sums[3, x + 1, 0]
        down_ref[n + x] = sums[5, x + 1, 0]
        for y in range(s.rows):
            v = [sums[c, x + 1, y] for c in range(3)]
            b = [sums[c, x + 1, y] for c in range(3, 6)]

            def dy(c):
                high = sums[c, x + 1, y + 1] if y + 1 < s.rows else 0.0
                low = sums[c, x + 1, y - 1] if y else 0.0
                return high - low

            def dx(c):
                return sums[c, x + 2, y] - sums[c, x, y]

            j = [dy(5) - z_difference(b[1]), z_difference(b[0]) - dx(5), dx(4) - dy(3)]
            j = [value * 0.5 for value in j]
            for d in range(3):
                coefs[x, y, d] = (v[d] - b[d]) * -0.25
                coefs[x, y, 3 + d] = (v[d] + b[d]) * -0.25
                coefs[x, y, 6 + d] = j[d]
                if y == last:
                    extras[d].append(j[d])
    base = s.first * s.comps * (n // 2)
    for c, values in enumerate(extras):
        for p in range(n // 2):
            up_ref[base + c * (n // 2) + p] = jnp.concatenate(values[2 * p : 2 * p + 2], 0).astype(BF16)


def transposed(s, source, zt):
    depth = source.shape[0] // s.pitch
    return source[pl.ds(zt, depth, stride=s.pitch), :].astype(BF16).T


def put(s, target, zt, slot, block):
    target[zt, :, slot] = block.reshape(LANES // GROUP, GROUP, block.shape[-1])


def diagonal_products(s, left, right):
    wide = s.bands * GROUP
    full = lax.dot_general(left, right, (((1,), (1,)), ((), ())), preferred_element_type=F32)
    lane = lax.broadcasted_iota(jnp.int32, (SUBLANES, wide), 1)
    sublane = lax.broadcasted_iota(jnp.int32, (SUBLANES, wide), 0)
    upper = lane % GROUP >= SUBLANES
    skew = (sublane - lane) % SUBLANES
    blocks = []
    for first in range(0, s.bands, SUBLANES):
        mixed = None
        for k in range(SUBLANES):
            top = (first + k) * GROUP
            part = jnp.where(upper, full[top + SUBLANES : top + GROUP], full[top : top + SUBLANES])
            part = pltpu.roll(part, k, 0) if k else part
            mixed = part if mixed is None else jnp.where(skew == k, part, mixed)
        for bit in (1, 2, 4):
            mixed = jnp.where((lane & bit) != 0, pltpu.roll(mixed, SUBLANES - bit, 0), mixed)
        blocks.append(mixed)
    return jnp.concatenate(blocks, 0)


def cross(a, b):
    return [a[1] * b[2] - a[2] * b[1], a[2] * b[0] - a[0] * b[2], a[0] * b[1] - a[1] * b[0]]


LAST_PAIRS = ((0, 1), (1, 0), (1, 2), (2, 1))


def local_depth(s):
    return (s.rows - 1) * s.inner * 9 + 4 * s.inner if s.rows > 1 else 0


def set_row(s, ref, entry, value):
    ref[pl.ds(entry * s.pitch, s.tiles), :] = value


def shift_matrix():
    source = lax.broadcasted_iota(jnp.int32, (2 * LANES, 2 * LANES), 0) % LANES
    target = lax.broadcasted_iota(jnp.int32, (2 * LANES, 2 * LANES), 1)
    inside = jnp.where(source == target + 1, 1.0, jnp.where(source == target - 1, -1.0, 0.0))
    carry_up = (target == 2 * LANES - 1) & (source == 0)
    carry_down = (target == LANES) & (source == LANES - 1)
    across = jnp.where(carry_up, 1.0, jnp.where(carry_down, -1.0, 0.0))
    return jnp.where(target < LANES, inside, across).astype(BF16)


def z_differences(s, values, matrix):
    rows = jnp.concatenate(values, 0)
    high = rows.astype(BF16)
    low = (rows - high.astype(F32)).astype(BF16)
    both = jnp.dot(jnp.concatenate([high, low], 1), matrix, preferred_element_type=F32)
    lane = lax.broadcasted_iota(jnp.int32, (s.tiles, LANES), 1)
    out = []
    for i in range(len(values)):
        part = both[i * s.tiles : (i + 1) * s.tiles]
        across = part[:, LANES:]
        across = jnp.where(lane < LANES // 2, pltpu.roll(across, 1, 0), pltpu.roll(across, s.tiles - 1, 0))
        out.append(part[:, :LANES] + across)
    return out


def local_band(s, q, z_ref, x_ref, coefs, drive_ref, field_ref, sr, sd, before, begin, between):
    n, last = (s.inner, s.rows - 1)
    entry = 0
    for y in range(s.rows):
        before(y)
        behind, here = ([row(x_ref, s, q, c, x, y) for c in range(6)] for x in range(2))
        for x in range(n):
            held = begin(y * n + x)
            ahead = [row(x_ref, s, q, c, x + 2, y) for c in range(6)]
            f = here
            dx = [p - m for p, m in zip(ahead, behind)]
            dy, dz = ([], [z_ref[y, x, c] for c in range(6)])
            for c in range(6):
                high = row(x_ref, s, q, c, x + 1, y + 1) if y < last else None
                low = row(x_ref, s, q, c, x + 1, y - 1) if y else None
                if high is None:
                    dy.append(jnp.zeros_like(f[0]) if low is None else -low)
                else:
                    dy.append(high if low is None else high - low)
            deltas = (dx, dy, dz)
            da, dc = ([], [])
            for c in range(3):
                plus = minus = None
                for d in range(3):
                    p = coefs[x, y, d] * (deltas[d][c] + deltas[d][c + 3])
                    m = coefs[x, y, 3 + d] * (deltas[d][c] - deltas[d][c + 3])
                    plus = p if plus is None else plus + p
                    minus = m if minus is None else minus + m
                da.append(plus + minus)
                dc.append(plus - minus)
            j = [(dy[5] - dz[4]) * 0.5, (dz[3] - dx[5]) * 0.5, (dx[4] - dy[3]) * 0.5]
            drives = da + dc
            if y == 0:
                for c in range(6):
                    drive_ref[q, x, c] = drives[c]
                    field_ref[q, x, c] = f[c]
                for c in range(3):
                    drive_ref[q, x, 6 + c] = j[c]
            else:
                turn = [coefs[x, y, 6 + d] * -0.5 for d in range(3)]
                left, right = (f + j, drives + cross(turn, f[3:6]))
                if y == last:
                    left += [j[c] for c, _ in LAST_PAIRS]
                    right += [f[3 + c] for _, c in LAST_PAIRS]
                for a, b in zip(left, right):
                    set_row(s, sr, entry, a)
                    set_row(s, sd, entry, b)
                    entry += 1
            behind, here = (here, ahead)
            between(y * n + x, held)


def local_kernel(s, x_hbm, coefs, rt, dt, drive_ref, field_ref, x_ref, sems, matrix, *rest):
    n = s.inner
    z_refs, pads = (rest[:2], rest[2:])

    def fetch(q):
        return pltpu.make_async_copy(x_hbm.at[q], x_ref.at[q], sems.at[q])

    for q in range(s.bands):
        fetch(q).start()
    matrix[...] = shift_matrix()
    used = local_depth(s)
    for ref in pads:
        tail = ref.shape[0] - used * s.pitch
        ref[pl.ds(used * s.pitch, tail), :] = jnp.zeros((tail, LANES), F32)

    def shifted(z_ref, q, y):
        values = [row(x_ref, s, q, c, x + 1, y) for x in range(n) for c in range(6)]
        for i, value in enumerate(z_differences(s, values, matrix[...])):
            z_ref[y, i // 6, i % 6] = value

    def turn(sr, sd, q, tiles):
        for zt in tiles:
            put(s, rt, zt, q, transposed(s, sr, zt))
            put(s, dt, zt, q, transposed(s, sd, zt))

    def pair(p, carry):
        for k in range(2):
            q = 2 * p + k
            other = pads[2 - 2 * k : 4 - 2 * k]
            behind = lax.rem(q + s.bands - 1, s.bands)
            ahead = lax.rem(q + 1, s.bands)

            @pl.when(q + 1 < s.bands)
            def _():
                fetch(ahead).wait()

            def before(y):
                shifted(z_refs[1 - k], ahead, y)

            def begin(step):
                steps = s.rows * n
                items = range(step * 2 * s.tiles // steps, (step + 1) * 2 * s.tiles // steps if used else 0)
                return [(item, transposed(s, other[item % 2], item // 2)) for item in items]

            def between(step, held):
                for item, block in held:
                    if item % 2:
                        put(s, dt, item // 2, behind, block)
                    else:
                        put(s, rt, item // 2, behind, block)

            local_band(s, q, z_refs[k], x_ref, coefs, drive_ref, field_ref, *pads[2 * k : 2 * k + 2], before, begin, between)
        return carry

    fetch(0).wait()
    for y in range(s.rows):
        shifted(z_refs[0], 0, y)
    lax.fori_loop(0, s.bands // 2, pair, 0)
    if used:
        turn(*pads[2:4], s.bands - 1, range(s.tiles))
    else:
        rt[...] = jnp.zeros_like(rt)
        dt[...] = jnp.zeros_like(dt)


def factor_kernel(s, above_ref, factors, held):
    n = s.inner
    above = halo_pair(s, above_ref, 0) + halo_pair(s, above_ref, 1)
    for entry in range(LANES):
        x, i = divmod(entry - (s.rows - 2) * n * 9, 13)
        value = jnp.ones((s.tiles, LANES), F32)
        if 0 <= x < n and i >= 9:
            value = above[(i - 9) // 2 * n + x] * (-0.25, 0.25, 0.25, -0.25)[i - 9]
        set_row(s, held, entry, value)
    for zt in range(s.tiles):
        factors[zt] = transposed(s, held, zt).reshape(LANES // GROUP, GROUP, LANES)


def halo_pair(s, up_ref, index):
    rows = []
    for p in range(s.inner // 2):
        both = up_ref[index * (s.inner // 2) + p].astype(F32)
        rows += [both[: s.tiles], both[s.tiles :]]
    return rows


def first_kernel(s, drive_ref, field_ref, coefs, down_ref, up_ref, above_ref, rt, dt, tots, *pads):
    n = s.inner
    base = s.first * s.comps
    behinds = [halo_pair(s, up_ref, base + c) for c in range(3)]
    totals = [halo_pair(s, up_ref, base + 3 + k) for k in range(len(TOTALS))]
    for x in range(n):
        vy, my, bx, bz = (total[x] for total in totals)
        tots[x, 0] = coefs[x, 0, 1]
        tots[x, 1] = coefs[x, 0, 4]
        tots[x, 2] = (vy - my) * -0.25
        tots[x, 3] = (vy + my) * -0.25
        j = [coefs[x, 0, 6] - bz * 0.5, coefs[x, 0, 7], coefs[x, 0, 8] + bx * 0.5]
        if s.rows == 1:
            above_x, above_z = (halo_pair(s, above_ref, k)[x] for k in range(2))
            j = [j[0] + above_z * 0.5, j[1], j[2] - above_x * 0.5]
        behind = [behinds[0][x] + down_ref[n + x] * 0.5, behinds[1][x], behinds[2][x] - down_ref[x] * 0.5]
        for c in range(3):
            tots[x, 4 + c] = j[c] * -0.5
            tots[x, 7 + c] = behind[c] * -0.5
    boundary_bands(s, 0, s.first, drive_ref, field_ref, up_ref, tots, rt, dt, pads)


def second_kernel(s, n_band, scale, place, local_rt, local_dt, drive_ref, field_ref, up_ref, tots, factors, rt_0, dt_0, send_ref, rt, dt, *pads):
    boundary_bands(s, s.first, s.bands - s.first, drive_ref, field_ref, up_ref, tots, rt, dt, pads)
    products(s, n_band, scale, 1, place, local_rt, local_dt, factors, rt_0, dt_0, rt, dt, send_ref)


def boundary_bands(s, first, count, drive_ref, field_ref, up_ref, tots, rt, dt, pads):
    n = s.inner
    half = LANES // 2
    used = n * 15
    for ref in pads:
        tail = (half - used) * s.pitch
        ref[pl.ds(used * s.pitch, tail), :] = jnp.zeros((tail, LANES), F32)

    def turned(source, t):
        both = [source[pl.ds(2 * t + k, half, stride=s.pitch), :] for k in range(2)]
        return jnp.concatenate(both, 0).astype(BF16).T

    def turn(sr, sd, q, pairs):
        for t in pairs:
            put(s, rt, t, q, turned(sr, t))
            put(s, dt, t, q, turned(sd, t))

    def band(q, sr, sd, begin, between):
        entry = 0
        h_all = [halo_pair(s, up_ref, q * s.comps + c) for c in range(6)]
        k = first + q
        for x in range(n):
            held = begin(x)
            f = [field_ref[k, x, c] for c in range(6)]
            h = [h_all[c][x] for c in range(6)]
            da, dc, ea, ec = ([], [], [], [])
            for c in range(3):
                p = tots[x, 0] * (h[c] + h[c + 3])
                m = tots[x, 1] * (h[c] - h[c + 3])
                da.append(drive_ref[k, x, c] - (p + m))
                dc.append(drive_ref[k, x, 3 + c] - (p - m))
                p = tots[x, 2] * (f[c] + f[c + 3])
                m = tots[x, 3] * (f[c] - f[c + 3])
                ea.append(p + m)
                ec.append(p - m)
            behind = cross([tots[x, 7 + c] for c in range(3)], h[3:6])
            dc[0] = dc[0] - behind[2] * 0.5
            dc[2] = dc[2] + behind[0] * 0.5
            j = [drive_ref[k, x, 6] - h[5] * 0.5, drive_ref[k, x, 7], drive_ref[k, x, 8] + h[3] * 0.5]
            left = f + j + h
            right = da + dc + cross([tots[x, 4 + c] for c in range(3)], f[3:6]) + ea + ec
            for a, b in zip(left, right):
                set_row(s, sr, entry, a)
                set_row(s, sd, entry, b)
                entry += 1
            between(held)

    def pair(p, carry):
        for k in range(2):
            q = 2 * p + k
            before = lax.rem(q + count - 1, count)
            other = pads[2 - 2 * k : 4 - 2 * k]

            def begin(x):
                return [(t, turned(other[0], t), turned(other[1], t)) for t in range(x * steps // n, (x + 1) * steps // n)]

            def between(held):
                for t, left, right in held:
                    put(s, rt, t, before, left)
                    put(s, dt, t, before, right)

            band(q, *pads[2 * k : 2 * k + 2], begin, between)
        return carry

    steps = s.tiles // 2
    lax.fori_loop(0, count // 2, pair, 0, unroll=2)
    turn(*pads[2:4], count - 1, range(steps))


def products(s, n_band, scale, core, place, local_rt, local_dt, factors, rt_0, dt_0, rt_1, dt_1, out_ref):
    wide = s.bands * GROUP
    half = LANES // 2
    share = s.bands // n_band
    lane = lax.broadcasted_iota(jnp.int32, (wide, LANES), 1)
    wanted = (lane >= half) == ((core ^ place[1]) % 2 == 1)

    def tile(r, carry):
        zt = (r * 2 + core) ^ place[1]
        parts = []
        for g in range(LANES // GROUP):
            left = jnp.concatenate([ref[zt // 2, g].reshape(-1, LANES) for ref in (rt_0, rt_1)], 0)
            left = jnp.where(wanted, left, jnp.zeros_like(left))
            right = jnp.concatenate([ref[zt // 2, g].reshape(-1, LANES) for ref in (dt_0, dt_1)], 0)
            if s.rows > 1:
                scaled = local_rt[zt, g] * factors[zt, g][None]
                left = jnp.concatenate([scaled.reshape(wide, -1), left], 1)
                right = jnp.concatenate([local_dt[zt, g].reshape(wide, -1), right], 1)
            parts.append(diagonal_products(s, left, right) * scale)
        for b in range(n_band):
            block = jnp.concatenate([p[b * share : (b + 1) * share] for p in parts], 0)
            out_ref[r, b ^ place[0]] = block.astype(out_ref.dtype)
        return carry

    lax.fori_loop(0, s.tiles // 2, tile, 0, unroll=4)


def farthest_first(size):
    return sorted(range(1, size), key=lambda d: (-d.bit_count(), d))


def exchange(value, distance, size):
    return lax.ppermute(value, AXES, [(i, i ^ distance) for i in range(size)])


def body(band_fields):
    s = Sizes(band_fields.shape)
    n_band, n_slab = (lax.axis_size("band"), lax.axis_size("slab"))
    devices = n_band * n_slab
    n, tiles, rows = (s.inner, s.tiles, s.rows)
    x = band_fields.reshape(s.bands, s.comps, s.planes, rows, tiles, LANES)
    x = x.transpose(0, 1, 2, 4, 3, 5).reshape(s.bands, s.comps, s.planes, tiles * rows, LANES)
    place = jnp.stack([lax.axis_index("band"), lax.axis_index("slab")]).astype(jnp.int32)

    def vector(*lead):
        return jax.ShapeDtypeStruct(lead + (tiles, LANES), F32)

    depth = -(-(max(local_depth(s), 1)) // LANES) * LANES
    groups = LANES // GROUP
    wide = s.bands * GROUP
    share = s.bands // n_band
    per_band = s.comps * (n // 2)
    rows_first = s.first * per_band + (3 + len(TOTALS)) * (n // 2)
    rows_rest = (s.bands - s.first) * per_band

    up, rest, down, sent, coefs = pl.pallas_call(
        lambda *refs: edge_kernel(s, *refs),
        out_shape=tuple(jax.ShapeDtypeStruct((count, 2 * tiles, LANES), BF16) for count in (rows_first, rows_rest)) + (vector(2 * n), jax.ShapeDtypeStruct((n, 2 * tiles, LANES), BF16), vector(n, rows, 9)),
        in_specs=[HBM],
        out_specs=(VMEM,) * 5,
        scratch_shapes=[pltpu.VMEM(x.shape, F32), pltpu.VMEM((s.comps, s.planes, rows, tiles, LANES), F32), pltpu.SemaphoreType.DMA((s.bands, 2))],
        compiler_params=EDGE,
    )(x)
    step = [(i, (i + 1) % devices) for i in range(devices)]
    from_below = lax.ppermute(up, AXES, step)
    rest_below = lax.ppermute(rest, AXES, step)
    from_above = lax.ppermute(sent, AXES, [(j, i) for i, j in step])

    turned = jax.ShapeDtypeStruct((tiles, groups, s.bands, GROUP, depth), BF16)
    local_rt, local_dt, drive, field = pl.pallas_call(
        lambda *refs: local_kernel(s, *refs),
        out_shape=(turned, turned, vector(s.bands, n, 9), vector(s.bands, n, 6)),
        in_specs=[HBM, VMEM],
        out_specs=(VMEM,) * 4,
        scratch_shapes=[pltpu.VMEM(x.shape, F32), pltpu.SemaphoreType.DMA((s.bands,)), pltpu.VMEM((2 * LANES, 2 * LANES), BF16)]
        + [pltpu.VMEM((rows, n, 6, tiles, LANES), F32)] * 2
        + [pltpu.VMEM((depth * s.pitch, LANES), F32)] * 4,
        compiler_params=LOCAL,
        cost_estimate=pl.CostEstimate(flops=2 * 10**9, bytes_accessed=2 * 10**7, transcendentals=0),
    )(x, coefs)
    if rows == 1:
        two = lax.ppermute(down, AXES, [(i, (i + 2) % devices) for i in range(devices)])
        two = two.reshape(2, n // 2, 2 * tiles, LANES) * 0.5
        base = s.first * per_band
        end = base + 3 * (n // 2)
        behind = from_below[base:end].astype(F32).reshape(3, n // 2, 2 * tiles, LANES)
        behind = jnp.stack([behind[0] - two[1], behind[1], behind[2] + two[0]])
        behind = behind.reshape(3 * (n // 2), 2 * tiles, LANES).astype(BF16)
        from_below = jnp.concatenate([from_below[:base], behind, from_below[end:]], 0)

    shape = (tiles // 2, n_band, groups * share, wide)
    scale = 1.0 / (n * rows * devices)
    blocks = [jax.ShapeDtypeStruct((tiles // 2, groups, count, GROUP, LANES), BF16) for count in (s.first, s.bands - s.first)]
    staging = [pltpu.VMEM((LANES // 2 * s.pitch, LANES), F32)] * 4
    factors = pl.pallas_call(
        lambda *refs: factor_kernel(s, *refs),
        out_shape=jax.ShapeDtypeStruct((tiles, groups, GROUP, LANES), BF16),
        in_specs=[VMEM],
        out_specs=VMEM,
        scratch_shapes=[pltpu.VMEM((LANES * s.pitch, LANES), F32)],
        compiler_params=BOUNDARY,
    )(from_above)
    rt_0, dt_0, tots = pl.pallas_call(
        lambda *refs: first_kernel(s, *refs),
        out_shape=(blocks[0], blocks[0], vector(n, 10)),
        in_specs=[VMEM] * 6,
        out_specs=(VMEM,) * 3,
        scratch_shapes=staging,
        compiler_params=BOUNDARY,
    )(drive, field, coefs, down, from_below, from_above)
    send, rt_1, dt_1 = pl.pallas_call(
        lambda *refs: second_kernel(s, n_band, scale, *refs),
        out_shape=(jax.ShapeDtypeStruct(shape, BF16), blocks[1], blocks[1]),
        in_specs=[SMEM] + [VMEM] * 9,
        out_specs=(VMEM,) * 3,
        scratch_shapes=staging,
        compiler_params=BOUNDARY,
    )(place, local_rt, local_dt, drive, field, rest_below, tots, factors, rt_0, dt_0)
    arrived = exchange(send, 1, devices)
    keep = pl.pallas_call(
        lambda place, *refs: products(s, n_band, scale, 0, place, *refs),
        out_shape=jax.ShapeDtypeStruct(shape, F32),
        in_specs=[SMEM] + [VMEM] * 7,
        out_specs=VMEM,
        compiler_params=BOUNDARY,
        cost_estimate=pl.CostEstimate(flops=2 * 10**9, bytes_accessed=2 * 10**7, transcendentals=0),
    )(place, local_rt, local_dt, factors, rt_0, dt_0, rt_1, dt_1)

    value = keep + arrived.astype(F32)
    parts = [exchange(value[:, d].astype(BF16), d * n_slab, devices) for d in farthest_first(n_band)]
    value = sum([p.astype(F32) for p in parts], value[:, 0])
    parts = [exchange(value[e].astype(BF16), 2 * e, devices) for e in range(1, tiles // 2)]
    value = sum([p.astype(F32) for p in parts], value[0])
    value = value.reshape(groups, share, s.bands, GROUP).transpose(1, 2, 0, 3)
    return value.reshape(share, s.bands, groups * GROUP)


def solution(mesh):
    return jax.shard_map(
        body,
        mesh=mesh,
        in_specs=(P(None, None, None, AXES, None),),
        out_specs=P("band", None, "slab"),
        check_vma=False,
    )
```

```python
import jax
import jax.numpy as jnp
from jax import lax
from jax.experimental import pallas as pl
from jax.experimental.pallas import tpu as pltpu
from jax.sharding import PartitionSpec as P

AXES = ("band", "slab")
LANES = 128
GROUP = 16
SUBLANES = 8
F32 = jnp.float32
BF16 = jnp.bfloat16
VMEM = pl.BlockSpec(memory_space=pltpu.VMEM)
SMEM = pl.BlockSpec(memory_space=pltpu.SMEM)
HBM = pl.BlockSpec(memory_space=pltpu.HBM)
EDGE = pltpu.CompilerParams(vmem_limit_bytes=50 * 2**20)
LOCAL = pltpu.CompilerParams(vmem_limit_bytes=38 * 2**20)
BOUNDARY = pltpu.CompilerParams(vmem_limit_bytes=32 * 2**20)


class Sizes:
    def __init__(self, shape):
        self.bands, self.comps, self.planes, self.rows, cells = shape
        self.inner = self.planes - 2
        self.tiles = cells // LANES
        self.first = self.bands // 2
        self.pitch = self.tiles + 1


TOTALS = (1, 4, 3, 5)


def row(ref, s, q, c, x, y):
    if s.rows == 1:
        return ref[q, c, x]
    return ref[q, c, x, pl.ds(y, s.tiles, stride=s.rows), :]


def z_difference(value):
    tiles = value.shape[0]
    lane = lax.broadcasted_iota(jnp.int32, value.shape, 1)
    left = pltpu.roll(value, LANES - 1, 1)
    right = pltpu.roll(value, 1, 1)
    after = jnp.where(lane == LANES - 1, pltpu.roll(left, tiles - 1, 0), left)
    before = jnp.where(lane == 0, pltpu.roll(right, 1, 0), right)
    return after - before


def edge_kernel(s, x_hbm, up_ref, rest_ref, down_ref, sent_ref, coefs, x_ref, sums, sems):
    last = s.rows - 1
    n = s.inner
    whole, inside = (pl.ds(4, 2), pl.ds(0, 4))
    copies = []
    for q in range(s.bands):
        copies.append(pltpu.make_async_copy(x_hbm.at[q, whole], x_ref.at[q, whole], sems.at[q, 0]))
        part = (q, inside, pl.ds(1, n))
        copies.append(pltpu.make_async_copy(x_hbm.at[part], x_ref.at[part], sems.at[q, 1]))
    for copy in copies:
        copy.start()

    def pack(first, count):
        target, start = (up_ref, 0) if first < s.first else (rest_ref, s.first)

        def band(q, carry):
            for c in range(s.comps):
                for p in range(n // 2):
                    pair = [row(x_ref, s, q, c, 1 + 2 * p + k, last) for k in range(2)]
                    target[((q - start) * s.comps + c) * (n // 2) + p] = jnp.concatenate(pair, 0).astype(BF16)
            return carry

        lax.fori_loop(first, first + count, band, 0)

    def total_of(first, count, c, x):
        for y in range(s.rows):
            total = row(x_ref, s, first, c, x, y)
            for q in range(first + 1, first + count):
                total = total + row(x_ref, s, q, c, x, y)
            if first:
                total = total + sums[c, x, y]
            sums[c, x, y] = total

    def add(first, count):
        def one(j, carry):
            c, x = (j // n, j % n + 1)
            total_of(first, count, c, x)
            return carry

        lax.fori_loop(0, s.comps * n, one, 0)
        for c in (4, 5):
            for x in (0, s.planes - 1):
                total_of(first, count, c, x)

    share = s.bands // 4
    for first in range(0, s.bands, share):
        for copy in copies[2 * first : 2 * (first + share)]:
            copy.wait()
        pack(first, share)
        add(first, share)
    for i in range(2 * n // 2):
        c, x = (3 + 2 * (2 * i // n), 2 * i % n + 1)
        sent_ref[i] = jnp.concatenate([sums[c, x, 0], sums[c, x + 1, 0]], 0).astype(BF16)
    extras = [[], [], []] + [[sums[c, x + 1, last] for x in range(n)] for c in TOTALS]
    for x in range(n):
        down_ref[x] = sums[3, x + 1, 0]
        down_ref[n + x] = sums[5, x + 1, 0]
        for y in range(s.rows):
            v = [sums[c, x + 1, y] for c in range(3)]
            b = [sums[c, x + 1, y] for c in range(3, 6)]

            def dy(c):
                high = sums[c, x + 1, y + 1] if y + 1 < s.rows else 0.0
                low = sums[c, x + 1, y - 1] if y else 0.0
                return high - low

            def dx(c):
                return sums[c, x + 2, y] - sums[c, x, y]

            j = [dy(5) - z_difference(b[1]), z_difference(b[0]) - dx(5), dx(4) - dy(3)]
            j = [value * 0.5 for value in j]
            for d in range(3):
                coefs[x, y, d] = (v[d] - b[d]) * -0.25
                coefs[x, y, 3 + d] = (v[d] + b[d]) * -0.25
                coefs[x, y, 6 + d] = j[d]
                if y == last:
                    extras[d].append(j[d])
    base = s.first * s.comps * (n // 2)
    for c, values in enumerate(extras):
        for p in range(n // 2):
            up_ref[base + c * (n // 2) + p] = jnp.concatenate(values[2 * p : 2 * p + 2], 0).astype(BF16)


def transposed(s, source, zt):
    depth = source.shape[0] // s.pitch
    return source[pl.ds(zt, depth, stride=s.pitch), :].astype(BF16).T


def put(s, target, zt, slot, block):
    target[zt, :, slot] = block.reshape(LANES // GROUP, GROUP, block.shape[-1])


def diagonal_products(s, left, right):
    wide = s.bands * GROUP
    full = lax.dot_general(left, right, (((1,), (1,)), ((), ())), preferred_element_type=F32)
    lane = lax.broadcasted_iota(jnp.int32, (SUBLANES, wide), 1)
    sublane = lax.broadcasted_iota(jnp.int32, (SUBLANES, wide), 0)
    upper = lane % GROUP >= SUBLANES
    skew = (sublane - lane) % SUBLANES
    blocks = []
    for first in range(0, s.bands, SUBLANES):
        mixed = None
        for k in range(SUBLANES):
            top = (first + k) * GROUP
            part = jnp.where(upper, full[top + SUBLANES : top + GROUP], full[top : top + SUBLANES])
            part = pltpu.roll(part, k, 0) if k else part
            mixed = part if mixed is None else jnp.where(skew == k, part, mixed)
        for bit in (1, 2, 4):
            mixed = jnp.where((lane & bit) != 0, pltpu.roll(mixed, SUBLANES - bit, 0), mixed)
        blocks.append(mixed)
    return jnp.concatenate(blocks, 0)


def cross(a, b):
    return [a[1] * b[2] - a[2] * b[1], a[2] * b[0] - a[0] * b[2], a[0] * b[1] - a[1] * b[0]]


LAST_PAIRS = ((0, 1), (1, 0), (1, 2), (2, 1))


def local_depth(s):
    return (s.rows - 1) * s.inner * 9 + 4 * s.inner if s.rows > 1 else 0


def set_row(s, ref, entry, value):
    ref[pl.ds(entry * s.pitch, s.tiles), :] = value


def shift_matrix():
    source = lax.broadcasted_iota(jnp.int32, (2 * LANES, 2 * LANES), 0) % LANES
    target = lax.broadcasted_iota(jnp.int32, (2 * LANES, 2 * LANES), 1)
    inside = jnp.where(source == target + 1, 1.0, jnp.where(source == target - 1, -1.0, 0.0))
    carry_up = (target == 2 * LANES - 1) & (source == 0)
    carry_down = (target == LANES) & (source == LANES - 1)
    across = jnp.where(carry_up, 1.0, jnp.where(carry_down, -1.0, 0.0))
    return jnp.where(target < LANES, inside, across).astype(BF16)


def z_differences(s, values, matrix):
    rows = jnp.concatenate(values, 0)
    high = rows.astype(BF16)
    low = (rows - high.astype(F32)).astype(BF16)
    both = jnp.dot(jnp.concatenate([high, low], 1), matrix, preferred_element_type=F32)
    lane = lax.broadcasted_iota(jnp.int32, (s.tiles, LANES), 1)
    out = []
    for i in range(len(values)):
        part = both[i * s.tiles : (i + 1) * s.tiles]
        across = part[:, LANES:]
        across = jnp.where(lane < LANES // 2, pltpu.roll(across, 1, 0), pltpu.roll(across, s.tiles - 1, 0))
        out.append(part[:, :LANES] + across)
    return out


def local_band(s, q, z_ref, x_ref, coefs, drive_ref, field_ref, sr, sd, before, begin, between):
    n, last = (s.inner, s.rows - 1)
    entry = 0
    for y in range(s.rows):
        before(y)
        behind, here = ([row(x_ref, s, q, c, x, y) for c in range(6)] for x in range(2))
        for x in range(n):
            held = begin(y * n + x)
            ahead = [row(x_ref, s, q, c, x + 2, y) for c in range(6)]
            f = here
            dx = [p - m for p, m in zip(ahead, behind)]
            dy, dz = ([], [z_ref[y, x, c] for c in range(6)])
            for c in range(6):
                high = row(x_ref, s, q, c, x + 1, y + 1) if y < last else None
                low = row(x_ref, s, q, c, x + 1, y - 1) if y else None
                if high is None:
                    dy.append(jnp.zeros_like(f[0]) if low is None else -low)
                else:
                    dy.append(high if low is None else high - low)
            deltas = (dx, dy, dz)
            da, dc = ([], [])
            for c in range(3):
                plus = minus = None
                for d in range(3):
                    p = coefs[x, y, d] * (deltas[d][c] + deltas[d][c + 3])
                    m = coefs[x, y, 3 + d] * (deltas[d][c] - deltas[d][c + 3])
                    plus = p if plus is None else plus + p
                    minus = m if minus is None else minus + m
                da.append(plus + minus)
                dc.append(plus - minus)
            j = [(dy[5] - dz[4]) * 0.5, (dz[3] - dx[5]) * 0.5, (dx[4] - dy[3]) * 0.5]
            drives = da + dc
            if y == 0:
                for c in range(6):
                    drive_ref[q, x, c] = drives[c]
                    field_ref[q, x, c] = f[c]
                for c in range(3):
                    drive_ref[q, x, 6 + c] = j[c]
            else:
                turn = [coefs[x, y, 6 + d] * -0.5 for d in range(3)]
                left, right = (f + j, drives + cross(turn, f[3:6]))
                if y == last:
                    left += [j[c] for c, _ in LAST_PAIRS]
                    right += [f[3 + c] for _, c in LAST_PAIRS]
                for a, b in zip(left, right):
                    set_row(s, sr, entry, a)
                    set_row(s, sd, entry, b)
                    entry += 1
            behind, here = (here, ahead)
            between(y * n + x, held)


def local_kernel(s, x_hbm, coefs, rt, dt, drive_ref, field_ref, x_ref, sems, matrix, *rest):
    n = s.inner
    z_refs, pads = (rest[:2], rest[2:])

    def fetch(q):
        return pltpu.make_async_copy(x_hbm.at[q], x_ref.at[q], sems.at[q])

    for q in range(s.bands):
        fetch(q).start()
    matrix[...] = shift_matrix()
    used = local_depth(s)
    for ref in pads:
        tail = ref.shape[0] - used * s.pitch
        ref[pl.ds(used * s.pitch, tail), :] = jnp.zeros((tail, LANES), F32)

    def shifted(z_ref, q, y):
        values = [row(x_ref, s, q, c, x + 1, y) for x in range(n) for c in range(6)]
        for i, value in enumerate(z_differences(s, values, matrix[...])):
            z_ref[y, i // 6, i % 6] = value

    def turn(sr, sd, q, tiles):
        for zt in tiles:
            put(s, rt, zt, q, transposed(s, sr, zt))
            put(s, dt, zt, q, transposed(s, sd, zt))

    def pair(p, carry):
        for k in range(2):
            q = 2 * p + k
            other = pads[2 - 2 * k : 4 - 2 * k]
            behind = lax.rem(q + s.bands - 1, s.bands)
            ahead = lax.rem(q + 1, s.bands)

            @pl.when(q + 1 < s.bands)
            def _():
                fetch(ahead).wait()

            def before(y):
                shifted(z_refs[1 - k], ahead, y)

            def begin(step):
                steps = s.rows * n
                items = range(step * 2 * s.tiles // steps, (step + 1) * 2 * s.tiles // steps if used else 0)
                return [(item, transposed(s, other[item % 2], item // 2)) for item in items]

            def between(step, held):
                for item, block in held:
                    if item % 2:
                        put(s, dt, item // 2, behind, block)
                    else:
                        put(s, rt, item // 2, behind, block)

            local_band(s, q, z_refs[k], x_ref, coefs, drive_ref, field_ref, *pads[2 * k : 2 * k + 2], before, begin, between)
        return carry

    fetch(0).wait()
    for y in range(s.rows):
        shifted(z_refs[0], 0, y)
    lax.fori_loop(0, s.bands // 2, pair, 0, unroll=2)
    if used:
        turn(*pads[2:4], s.bands - 1, range(s.tiles))
    else:
        rt[...] = jnp.zeros_like(rt)
        dt[...] = jnp.zeros_like(dt)


def factor_kernel(s, above_ref, factors, held):
    n = s.inner
    above = halo_pair(s, above_ref, 0) + halo_pair(s, above_ref, 1)
    for entry in range(LANES):
        x, i = divmod(entry - (s.rows - 2) * n * 9, 13)
        value = jnp.ones((s.tiles, LANES), F32)
        if 0 <= x < n and i >= 9:
            value = above[(i - 9) // 2 * n + x] * (-0.25, 0.25, 0.25, -0.25)[i - 9]
        set_row(s, held, entry, value)
    for zt in range(s.tiles):
        factors[zt] = transposed(s, held, zt).reshape(LANES // GROUP, GROUP, LANES)


def halo_pair(s, up_ref, index):
    rows = []
    for p in range(s.inner // 2):
        both = up_ref[index * (s.inner // 2) + p].astype(F32)
        rows += [both[: s.tiles], both[s.tiles :]]
    return rows


def first_kernel(s, drive_ref, field_ref, coefs, down_ref, up_ref, above_ref, rt, dt, tots, *pads):
    n = s.inner
    base = s.first * s.comps
    behinds = [halo_pair(s, up_ref, base + c) for c in range(3)]
    totals = [halo_pair(s, up_ref, base + 3 + k) for k in range(len(TOTALS))]
    for x in range(n):
        vy, my, bx, bz = (total[x] for total in totals)
        tots[x, 0] = coefs[x, 0, 1]
        tots[x, 1] = coefs[x, 0, 4]
        tots[x, 2] = (vy - my) * -0.25
        tots[x, 3] = (vy + my) * -0.25
        j = [coefs[x, 0, 6] - bz * 0.5, coefs[x, 0, 7], coefs[x, 0, 8] + bx * 0.5]
        if s.rows == 1:
            above_x, above_z = (halo_pair(s, above_ref, k)[x] for k in range(2))
            j = [j[0] + above_z * 0.5, j[1], j[2] - above_x * 0.5]
        behind = [behinds[0][x] + down_ref[n + x] * 0.5, behinds[1][x], behinds[2][x] - down_ref[x] * 0.5]
        for c in range(3):
            tots[x, 4 + c] = j[c] * -0.5
            tots[x, 7 + c] = behind[c] * -0.5
    boundary_bands(s, 0, s.first, drive_ref, field_ref, up_ref, tots, rt, dt, pads)


def second_kernel(s, n_band, scale, place, local_rt, local_dt, drive_ref, field_ref, up_ref, tots, factors, rt_0, dt_0, send_ref, rt, dt, *pads):
    boundary_bands(s, s.first, s.bands - s.first, drive_ref, field_ref, up_ref, tots, rt, dt, pads)
    products(s, n_band, scale, 1, place, local_rt, local_dt, factors, rt_0, dt_0, rt, dt, send_ref)


def boundary_bands(s, first, count, drive_ref, field_ref, up_ref, tots, rt, dt, pads):
    n = s.inner
    half = LANES // 2
    used = n * 15
    for ref in pads:
        tail = (half - used) * s.pitch
        ref[pl.ds(used * s.pitch, tail), :] = jnp.zeros((tail, LANES), F32)

    def turned(source, t):
        both = [source[pl.ds(2 * t + k, half, stride=s.pitch), :] for k in range(2)]
        return jnp.concatenate(both, 0).astype(BF16).T

    def turn(sr, sd, q, pairs):
        for t in pairs:
            put(s, rt, t, q, turned(sr, t))
            put(s, dt, t, q, turned(sd, t))

    def band(q, sr, sd, begin, between):
        entry = 0
        h_all = [halo_pair(s, up_ref, q * s.comps + c) for c in range(6)]
        k = first + q
        for x in range(n):
            held = begin(x)
            f = [field_ref[k, x, c] for c in range(6)]
            h = [h_all[c][x] for c in range(6)]
            da, dc, ea, ec = ([], [], [], [])
            for c in range(3):
                p = tots[x, 0] * (h[c] + h[c + 3])
                m = tots[x, 1] * (h[c] - h[c + 3])
                da.append(drive_ref[k, x, c] - (p + m))
                dc.append(drive_ref[k, x, 3 + c] - (p - m))
                p = tots[x, 2] * (f[c] + f[c + 3])
                m = tots[x, 3] * (f[c] - f[c + 3])
                ea.append(p + m)
                ec.append(p - m)
            behind = cross([tots[x, 7 + c] for c in range(3)], h[3:6])
            dc[0] = dc[0] - behind[2] * 0.5
            dc[2] = dc[2] + behind[0] * 0.5
            j = [drive_ref[k, x, 6] - h[5] * 0.5, drive_ref[k, x, 7], drive_ref[k, x, 8] + h[3] * 0.5]
            left = f + j + h
            right = da + dc + cross([tots[x, 4 + c] for c in range(3)], f[3:6]) + ea + ec
            for a, b in zip(left, right):
                set_row(s, sr, entry, a)
                set_row(s, sd, entry, b)
                entry += 1
            between(held)

    def pair(p, carry):
        for k in range(2):
            q = 2 * p + k
            before = lax.rem(q + count - 1, count)
            other = pads[2 - 2 * k : 4 - 2 * k]

            def begin(x):
                return [(t, turned(other[0], t), turned(other[1], t)) for t in range(x * steps // n, (x + 1) * steps // n)]

            def between(held):
                for t, left, right in held:
                    put(s, rt, t, before, left)
                    put(s, dt, t, before, right)

            band(q, *pads[2 * k : 2 * k + 2], begin, between)
        return carry

    steps = s.tiles // 2
    lax.fori_loop(0, count // 2, pair, 0, unroll=2)
    turn(*pads[2:4], count - 1, range(steps))


def products(s, n_band, scale, core, place, local_rt, local_dt, factors, rt_0, dt_0, rt_1, dt_1, out_ref):
    wide = s.bands * GROUP
    half = LANES // 2
    share = s.bands // n_band
    lane = lax.broadcasted_iota(jnp.int32, (wide, LANES), 1)
    wanted = (lane >= half) == ((core ^ place[1]) % 2 == 1)

    def tile(r, carry):
        zt = (r * 2 + core) ^ place[1]
        parts = []
        for g in range(LANES // GROUP):
            left = jnp.concatenate([ref[zt // 2, g].reshape(-1, LANES) for ref in (rt_0, rt_1)], 0)
            left = jnp.where(wanted, left, jnp.zeros_like(left))
            right = jnp.concatenate([ref[zt // 2, g].reshape(-1, LANES) for ref in (dt_0, dt_1)], 0)
            if s.rows > 1:
                scaled = local_rt[zt, g] * factors[zt, g][None]
                left = jnp.concatenate([scaled.reshape(wide, -1), left], 1)
                right = jnp.concatenate([local_dt[zt, g].reshape(wide, -1), right], 1)
            parts.append(diagonal_products(s, left, right) * scale)
        for b in range(n_band):
            block = jnp.concatenate([p[b * share : (b + 1) * share] for p in parts], 0)
            out_ref[r, b ^ place[0]] = block.astype(out_ref.dtype)
        return carry

    lax.fori_loop(0, s.tiles // 2, tile, 0, unroll=4)


def farthest_first(size):
    return sorted(range(1, size), key=lambda d: (-d.bit_count(), d))


def exchange(value, distance, size):
    return lax.ppermute(value, AXES, [(i, i ^ distance) for i in range(size)])


def body(band_fields):
    s = Sizes(band_fields.shape)
    n_band, n_slab = (lax.axis_size("band"), lax.axis_size("slab"))
    devices = n_band * n_slab
    n, tiles, rows = (s.inner, s.tiles, s.rows)
    x = band_fields.reshape(s.bands, s.comps, s.planes, rows, tiles, LANES)
    x = x.transpose(0, 1, 2, 4, 3, 5).reshape(s.bands, s.comps, s.planes, tiles * rows, LANES)
    place = jnp.stack([lax.axis_index("band"), lax.axis_index("slab")]).astype(jnp.int32)

    def vector(*lead):
        return jax.ShapeDtypeStruct(lead + (tiles, LANES), F32)

    depth = -(-(max(local_depth(s), 1)) // LANES) * LANES
    groups = LANES // GROUP
    wide = s.bands * GROUP
    share = s.bands // n_band
    per_band = s.comps * (n // 2)
    rows_first = s.first * per_band + (3 + len(TOTALS)) * (n // 2)
    rows_rest = (s.bands - s.first) * per_band

    up, rest, down, sent, coefs = pl.pallas_call(
        lambda *refs: edge_kernel(s, *refs),
        out_shape=tuple(jax.ShapeDtypeStruct((count, 2 * tiles, LANES), BF16) for count in (rows_first, rows_rest)) + (vector(2 * n), jax.ShapeDtypeStruct((n, 2 * tiles, LANES), BF16), vector(n, rows, 9)),
        in_specs=[HBM],
        out_specs=(VMEM,) * 5,
        scratch_shapes=[pltpu.VMEM(x.shape, F32), pltpu.VMEM((s.comps, s.planes, rows, tiles, LANES), F32), pltpu.SemaphoreType.DMA((s.bands, 2))],
        compiler_params=EDGE,
    )(x)
    step = [(i, (i + 1) % devices) for i in range(devices)]
    from_below = lax.ppermute(up, AXES, step)
    rest_below = lax.ppermute(rest, AXES, step)
    from_above = lax.ppermute(sent, AXES, [(j, i) for i, j in step])

    turned = jax.ShapeDtypeStruct((tiles, groups, s.bands, GROUP, depth), BF16)
    local_rt, local_dt, drive, field = pl.pallas_call(
        lambda *refs: local_kernel(s, *refs),
        out_shape=(turned, turned, vector(s.bands, n, 9), vector(s.bands, n, 6)),
        in_specs=[HBM, VMEM],
        out_specs=(VMEM,) * 4,
        scratch_shapes=[pltpu.VMEM(x.shape, F32), pltpu.SemaphoreType.DMA((s.bands,)), pltpu.VMEM((2 * LANES, 2 * LANES), BF16)]
        + [pltpu.VMEM((rows, n, 6, tiles, LANES), F32)] * 2
        + [pltpu.VMEM((depth * s.pitch, LANES), F32)] * 4,
        compiler_params=LOCAL,
        cost_estimate=pl.CostEstimate(flops=2 * 10**9, bytes_accessed=2 * 10**7, transcendentals=0),
    )(x, coefs)
    if rows == 1:
        two = lax.ppermute(down, AXES, [(i, (i + 2) % devices) for i in range(devices)])
        two = two.reshape(2, n // 2, 2 * tiles, LANES) * 0.5
        base = s.first * per_band
        end = base + 3 * (n // 2)
        behind = from_below[base:end].astype(F32).reshape(3, n // 2, 2 * tiles, LANES)
        behind = jnp.stack([behind[0] - two[1], behind[1], behind[2] + two[0]])
        behind = behind.reshape(3 * (n // 2), 2 * tiles, LANES).astype(BF16)
        from_below = jnp.concatenate([from_below[:base], behind, from_below[end:]], 0)

    shape = (tiles // 2, n_band, groups * share, wide)
    scale = 1.0 / (n * rows * devices)
    blocks = [jax.ShapeDtypeStruct((tiles // 2, groups, count, GROUP, LANES), BF16) for count in (s.first, s.bands - s.first)]
    staging = [pltpu.VMEM((LANES // 2 * s.pitch, LANES), F32)] * 4
    factors = pl.pallas_call(
        lambda *refs: factor_kernel(s, *refs),
        out_shape=jax.ShapeDtypeStruct((tiles, groups, GROUP, LANES), BF16),
        in_specs=[VMEM],
        out_specs=VMEM,
        scratch_shapes=[pltpu.VMEM((LANES * s.pitch, LANES), F32)],
        compiler_params=BOUNDARY,
    )(from_above)
    rt_0, dt_0, tots = pl.pallas_call(
        lambda *refs: first_kernel(s, *refs),
        out_shape=(blocks[0], blocks[0], vector(n, 10)),
        in_specs=[VMEM] * 6,
        out_specs=(VMEM,) * 3,
        scratch_shapes=staging,
        compiler_params=BOUNDARY,
    )(drive, field, coefs, down, from_below, from_above)
    send, rt_1, dt_1 = pl.pallas_call(
        lambda *refs: second_kernel(s, n_band, scale, *refs),
        out_shape=(jax.ShapeDtypeStruct(shape, BF16), blocks[1], blocks[1]),
        in_specs=[SMEM] + [VMEM] * 9,
        out_specs=(VMEM,) * 3,
        scratch_shapes=staging,
        compiler_params=BOUNDARY,
    )(place, local_rt, local_dt, drive, field, rest_below, tots, factors, rt_0, dt_0)
    arrived = exchange(send, 1, devices)
    keep = pl.pallas_call(
        lambda place, *refs: products(s, n_band, scale, 0, place, *refs),
        out_shape=jax.ShapeDtypeStruct(shape, F32),
        in_specs=[SMEM] + [VMEM] * 7,
        out_specs=VMEM,
        compiler_params=BOUNDARY,
        cost_estimate=pl.CostEstimate(flops=2 * 10**9, bytes_accessed=2 * 10**7, transcendentals=0),
    )(place, local_rt, local_dt, factors, rt_0, dt_0, rt_1, dt_1)

    value = keep + arrived.astype(F32)
    parts = [exchange(value[:, d].astype(BF16), d * n_slab, devices) for d in farthest_first(n_band)]
    value = sum([p.astype(F32) for p in parts], value[:, 0])
    order = sorted(range(1, tiles // 2), key=lambda e: (e.bit_count(), -e))
    parts = {e: exchange(value[e].astype(BF16), 2 * e, devices) for e in order}
    parts = [parts[e] for e in sorted(parts)]
    value = sum([p.astype(F32) for p in parts], value[0])
    value = value.reshape(groups, share, s.bands, GROUP).transpose(1, 2, 0, 3)
    return value.reshape(share, s.bands, groups * GROUP)


def solution(mesh):
    return jax.shard_map(
        body,
        mesh=mesh,
        in_specs=(P(None, None, None, AXES, None),),
        out_specs=P("band", None, "slab"),
        check_vma=False,
    )
```
